32 devices in a mesh: groups: 2 (over y), replica: 4 (over z), tensor: 4 (over x, core).
Axes of the slice: x: 2, y: 2, z: 4, core: 2. Of those that a mesh axis runs over, the one named last changes fastest.
Arguments:
- queries: bfloat16 [8192, 8192], P(('groups', 'replica'), 'tensor'), parts along dimension 0, may hold values from -160 to 160
- suffix_cache: bfloat16 [8192, 2048], P(('groups', 'replica'), 'tensor'), parts along dimension 0, may hold values from -6 to 6
- cache_pool: bfloat16 [12288, 2048], P(('groups', 'replica'), 'tensor'), parts along dimension 0, may hold values from -6 to 6
- block_table: int32 [8, 4], P(('groups', 'replica')), parts along dimension 0, may hold values from 0 to 5, as said below
- prefix_blocks: int32 [8], P(('groups', 'replica')), parts along dimension 0, may hold values from 1 to 4, as said below
- segment_owner: int32 [128, 1], P(('groups', 'replica')), parts along dimension 0, may hold values from 0 to 3; in each aligned block of 16 rows (0 to 15, 16 to 31, ...) at most 8 rows name the same one
Outputs:
- placed_rows: bfloat16 [16384, 8192], P(('groups', 'replica'), 'tensor'), parts along dimension 0
The draws below stay inside these ranges and needn't reach their ends.
There are 2 independent parts, one for each index of `groups`. The reference program is written for one: setup_inputs(seed, part) draws one part's arguments, and reference() takes and returns one part's arrays. A program takes and returns all parts, laid end to end along the dimension named above; each array names one. Nothing has to cross between parts.
Inputs may be any that keep to these rules, and one draw needn't show every extreme that they name: `block_table`: the 4 entries of a row are distinct. `prefix_blocks`: some request has exactly 4 blocks. `segment_owner`: among the segments of one request at most 8 share an owner, and some owner gets exactly 8.
All inputs are finite; a program needn't handle non-finite values.
Results may differ from the reference program's by a relative error of at most 0.0046.
Values may be sent and summed in bfloat16 or wider, within the bound.
No kernel may reach another device: no remote copies, remote signals or barrier semaphores. Data moves between devices by JAX's collectives and lax.ppermute only.
A program may use at most 192 MiB of HBM per device.

```python
import math
import jax
import jax.numpy as jnp
import numpy as np
from jax import lax

HEADS = 64
KV_HEADS = 8
HEAD_DIM = 128
BLK = 256
MAXB = 4
POOL = 6
SEGS = 16
SEG = 64
REQS = 4
SUF = 1024
CAP = 8
ROWS = 4096
PROWS = 6144
SEGTOTAL = 64


def suffix_noise(key):
    return jnp.clip(jax.random.normal(key, (ROWS, KV_HEADS * 2 * HEAD_DIM), jnp.float32), -6.0, 6.0)


def draw_suffix_cache(key, part):
    shared = suffix_noise(key)
    return shared.astype(jnp.bfloat16)


def draw_queries(key, part):
    key = jax.random.fold_in(key, 23)
    drawn = jnp.clip(jax.random.normal(key, (ROWS, HEADS * HEAD_DIM), jnp.float32), -6.0, 6.0)
    return drawn.astype(jnp.bfloat16)


def draw_block_table(key, part):
    key = jax.random.fold_in(key, 31)
    row_keys = jax.random.split(key, REQS)
    return jax.vmap(lambda single_key: jax.random.permutation(single_key, POOL)[:MAXB])(row_keys).astype(jnp.int32)


def draw_prefix_blocks(key, part):
    key = jax.random.fold_in(key, 43)
    count_key, pick_key = jax.random.split(key)
    counts = jax.random.randint(count_key, (REQS,), 1, MAXB + 1)
    chosen = jax.random.randint(pick_key, (), 0, REQS)
    return jnp.where(jnp.arange(REQS) == chosen, MAXB, counts).astype(jnp.int32)


def block_levels(rng, dims, cuts, least, high):
    gain = 1.0
    for dim, shards_of in cuts:
        steps = jax.random.uniform(jax.random.fold_in(jax.random.fold_in(rng, 6), dim), (shards_of,), jnp.float32, least / len(cuts), high / len(cuts))
        gain = gain * jnp.repeat(jnp.exp(steps), dims[dim] // shards_of).reshape((-1,) + (1,) * (len(dims) - 1 - dim))
    return gain


def routed_block(own_key, own, number, rows, amount, top, most, lean):
    order = jax.random.permutation(own_key, amount)
    heavy_load, common = portions_of(amount, rows * top, most, lean, True), portions_of(amount, rows * top, most, lean, False)
    places = jnp.arange(amount)

    def named(lengths, offset_by):
        used = int((lengths > 0).sum())
        fixed = max(1, used // 4)
        shifted = fixed + (places - fixed + offset_by * (used - fixed)) % max(1, amount - fixed)
        return jnp.zeros((amount,), jnp.int32).at[order[jnp.where(places < fixed, places, shifted)]].set(jnp.asarray(lengths, jnp.int32))

    lengths = jnp.where(number % 4 == 0, named(heavy_load, number // 4), named(common, number - number // 4 - 1))
    mixed = jax.random.permutation(jax.random.fold_in(own, 3), amount)
    donor, sink = mixed[0:amount // 2 * 2:2], mixed[1:amount // 2 * 2:2]
    margin = jnp.minimum(lengths[donor] - 1, most - lengths[sink]) // 2
    margin = jnp.where((donor == order[0]) | (sink == order[0]) | (lengths[sink] == 0), 0, jnp.maximum(margin, 0))
    shifted = jax.random.randint(jax.random.fold_in(own, 4), (amount // 2,), 0, 1 << 20) % (margin + 1)
    lengths = lengths.at[donor].add(-shifted).at[sink].add(shifted)
    labels = jnp.searchsorted(jnp.cumsum(lengths), jnp.arange(rows * top), side="right").astype(jnp.int32)
    listing = labels.reshape(top, rows).T
    listing = listing[jax.random.permutation(jax.random.fold_in(own, 1), rows)]
    offset_by = jax.random.randint(jax.random.fold_in(own, 2), (rows, 1), 0, top)
    return jnp.take_along_axis(listing, (jnp.arange(top)[None, :] + offset_by) % top, axis=1)


def portions_of(amount, total, reach, skew, full):
    portions = [(1 << 20) // math.isqrt(standing ** skew) + 1 for standing in range(1, amount + 1)]
    largest = reach if full else min(reach, max(-(-total // amount), total * portions[0] // sum(portions)))
    least = 1 if total - largest >= amount - 1 else 0
    given, surplus = [largest] + [least] * (amount - 1), total - largest - least * (amount - 1)
    while surplus > 0:
        movable = [i for i in range(1, amount) if given[i] < largest] or [i for i in range(1, amount) if given[i] < reach]
        whole, remaining = sum([portions[i] for i in movable]), surplus
        for i in movable:
            extra = min(reach - given[i], max(1, remaining * portions[i] // whole), surplus)
            given[i] = given[i] + extra
            surplus = surplus - extra
    return np.array(given)


def centred(stream_key, extent, scale, reach, shards=(), kind=jnp.bfloat16):
    entries = jax.random.normal(stream_key, extent, jnp.float32) * scale
    if len(shards) > 0:
        entries = block_levels(stream_key, extent, shards, -0.22, 0.18) * entries
    return jnp.clip(entries, min=-reach, max=reach).astype(kind)


def setup_inputs(seed: int = 0, part: int = 0) -> dict:
    keys = jax.random.split(jax.random.key(seed), 7)
    part_splits = jax.random.split(jax.random.fold_in(keys[6], part), 7)
    queries = draw_queries(jax.random.fold_in(jax.random.fold_in(keys[6], part), 71), part)
    suffix_cache = draw_suffix_cache(jax.random.fold_in(jax.random.fold_in(keys[6], part), 71), part)
    cache_pool = centred(part_splits[2], (PROWS, KV_HEADS * 2 * HEAD_DIM), 1.0, 6.0, ((0, 4), (1, 4)))
    block_table = draw_block_table(jax.random.fold_in(jax.random.fold_in(keys[6], part), 71), part)
    prefix_blocks = draw_prefix_blocks(jax.random.fold_in(jax.random.fold_in(keys[6], part), 71), part)
    segment_owner_keys = jax.random.split(jax.random.fold_in(part_splits[5], 1), SEGTOTAL // SEGS)
    segment_owner_turns = jax.random.permutation(jax.random.fold_in(part_splits[5], 3), SEGTOTAL // SEGS)
    segment_owner = jax.vmap(lambda own, number: routed_block(jax.random.fold_in(part_splits[5], 2), own, number, SEGS, REQS, 1, CAP, 1))(segment_owner_keys, segment_owner_turns).reshape((SEGTOTAL, 1))
    return dict(queries=queries, suffix_cache=suffix_cache, cache_pool=cache_pool, block_table=block_table, prefix_blocks=prefix_blocks, segment_owner=segment_owner)


def selection(owner_list, replicas, capacity):
    seg_order = jnp.arange(owner_list.shape[0], dtype=jnp.int32)
    same_owner = owner_list[None, :] == owner_list[:, None]
    earlier = seg_order[None, :] < seg_order[:, None]
    slot_index = jnp.sum((same_owner & earlier).astype(jnp.int32), axis=1)
    target = owner_list * capacity + slot_index
    return jnp.arange(replicas * capacity, dtype=jnp.int32)[:, None] == target[None, :]


def attend(queries, cache_rows, key_flags, query_pos, prefix_rows):
    query_count = queries.shape[0]
    key_count = cache_rows.shape[0]
    kv_heads = cache_rows.shape[1] // (2 * HEAD_DIM)
    group_size = queries.shape[1] // (HEAD_DIM * kv_heads)
    grouped = queries.astype(jnp.float32).reshape(query_count, kv_heads, group_size, HEAD_DIM)
    paired = cache_rows.astype(jnp.float32).reshape(key_count, kv_heads, 2, HEAD_DIM)
    scores = jnp.einsum("qkgd,nkd->kgqn", grouped, paired[:, :, 0, :]) * (HEAD_DIM ** -0.5)
    key_pos = jnp.arange(key_count, dtype=jnp.int32)
    allowed = jnp.where(key_pos[None, :] < prefix_rows, key_flags[None, :] > 0.5,
                        (key_pos[None, :] - prefix_rows) <= query_pos[:, None])
    highest = jnp.max(jnp.where(allowed, scores, -jnp.inf), axis=-1, keepdims=True)
    weights = jnp.exp(jnp.where(allowed, scores - highest, -jnp.inf))
    totals = jnp.sum(weights, axis=-1, keepdims=True)
    rounded = lax.optimization_barrier(weights.astype(jnp.bfloat16)).astype(jnp.float32)
    mixed = jnp.einsum("kgqn,nkd->kgqd", rounded, paired[:, :, 1, :]) / totals
    return jnp.transpose(mixed, (2, 0, 1, 3)).reshape(query_count, kv_heads * group_size * HEAD_DIM)


def reference(queries, suffix_cache, cache_pool, block_table, prefix_blocks, segment_owner):
    width = queries.shape[1]
    columns = suffix_cache.shape[1]
    prefix_rows = MAXB * BLK

    def one_request(items):
        home_queries, home_suffix, home_pool, home_table, home_blocks, home_owner = items
        prefix = jnp.take(home_pool.reshape(POOL, BLK, columns), home_table, axis=0).reshape(prefix_rows, columns)
        cache_rows = jnp.concatenate([prefix, home_suffix], axis=0)
        key_flags = jnp.concatenate([(jnp.arange(prefix_rows, dtype=jnp.int32) < home_blocks * BLK).astype(jnp.float32),
                                     jnp.ones((SUF,), jnp.float32)])
        result = attend(home_queries, cache_rows, key_flags, jnp.arange(SUF, dtype=jnp.int32), prefix_rows).astype(jnp.bfloat16)
        chooser = selection(home_owner, REQS, CAP).astype(jnp.bfloat16)
        placed = jnp.dot(chooser, result.reshape(SEGS, SEG * width), preferred_element_type=jnp.float32)
        return placed.astype(jnp.bfloat16)

    stacked = lax.map(one_request, (queries.reshape(REQS, SUF, width),
                                    suffix_cache.reshape(REQS, SUF, columns),
                                    cache_pool.reshape(REQS, POOL * BLK, columns),
                                    block_table, prefix_blocks,
                                    segment_owner.reshape(REQS, SEGS)))
    stacked = stacked.reshape(REQS, REQS, CAP * SEG, width)
    return jnp.transpose(stacked, (1, 0, 2, 3)).reshape(REQS * REQS * CAP * SEG, width)
```

```python
import functools
import math

import jax
import jax.numpy as jnp
from jax import lax
from jax.experimental import pallas as pl
from jax.experimental.pallas import tpu as pltpu
from jax.sharding import PartitionSpec as P

HEAD_DIM = 128
BLK = 256
MAXB = 4
SEGS = 16
SEG = 64
EXPO = HEAD_DIM ** (-0.5) * math.log2(math.e)
LOWEST = -1e38


def attend_kernel(
    segs, table, blocks, q_ref, suffix_hbm, pool_hbm, o_ref, cache, scores, peak, acc, total, sems
):
    step = pl.program_id(0)
    seg = segs[step]
    suffix_rows = suffix_hbm.shape[0]
    kv_heads = suffix_hbm.shape[1] // (2 * HEAD_DIM)
    group = q_ref.shape[1] // (HEAD_DIM * kv_heads)
    rows = group * SEG

    @pl.when(step == 0)
    def _():
        copies = [
            pltpu.make_async_copy(suffix_hbm, cache.at[pl.ds(0, suffix_rows)], sems.at[MAXB])
        ]
        for b in range(MAXB):
            start = pl.multiple_of(table[b] * BLK, BLK)
            copies.append(
                pltpu.make_async_copy(
                    pool_hbm.at[pl.ds(start, BLK)],
                    cache.at[pl.ds(suffix_rows + b * BLK, BLK)],
                    sems.at[b],
                )
            )
        for copy in copies:
            copy.start()
        for copy in copies:
            copy.wait()

    @pl.when(seg < 0)
    def _():
        o_ref[...] = jnp.zeros_like(o_ref)

    @pl.when(seg >= 0)
    def _():
        whole = seg * SEG // BLK
        chunks = whole + blocks[0]

        def queries_of(g):
            first = g * group
            return jnp.concatenate(
                [q_ref[:, (first + h) * HEAD_DIM : (first + h + 1) * HEAD_DIM] for h in range(group)],
                axis=0,
            )

        def keys_of(start, g):
            return cache[pl.ds(start, BLK), 2 * g * HEAD_DIM : (2 * g + 1) * HEAD_DIM]

        def values_of(start, g):
            return cache[pl.ds(start, BLK), (2 * g + 1) * HEAD_DIM : (2 * g + 2) * HEAD_DIM]

        def start_of(t):
            start = jnp.where(t < whole, t * BLK, suffix_rows + (t - whole) * BLK)
            return pl.multiple_of(start, BLK)

        def dot_keys(start, g):
            return lax.dot_general(
                queries_of(g),
                keys_of(start, g),
                (((1,), (1,)), ((), ())),
                preferred_element_type=jnp.float32,
            )

        def halves_max(s):
            top = s[:, :HEAD_DIM]
            for c in range(1, BLK // HEAD_DIM):
                top = jnp.maximum(top, s[:, c * HEAD_DIM : (c + 1) * HEAD_DIM])
            return top

        last = pl.multiple_of(whole * BLK, BLK)
        token = lax.broadcasted_iota(jnp.int32, (rows, BLK), 0) % SEG + (seg * SEG - whole * BLK)
        seen = lax.broadcasted_iota(jnp.int32, (rows, BLK), 1) <= token
        for g in range(kv_heads):
            s = jnp.where(seen, dot_keys(last, g), LOWEST)
            scores[g, 0] = s
            peak[g] = halves_max(s)

        @pl.loop(0, chunks)
        def _(t):
            start = start_of(t)
            for g in range(kv_heads):
                s = dot_keys(start, g)
                scores[g, t + 1] = s
                peak[g] = jnp.maximum(peak[g], halves_max(s))

        for g in range(kv_heads):
            top = jnp.max(peak[g], axis=-1, keepdims=True)
            peak[g] = jnp.broadcast_to(top, (rows, HEAD_DIM))

        def weigh(start, t, g):
            top = peak[g]
            parts = [
                jnp.exp2((scores[g, t, :, c * HEAD_DIM : (c + 1) * HEAD_DIM] - top) * EXPO)
                for c in range(BLK // HEAD_DIM)
            ]
            mixed = jnp.dot(
                jnp.concatenate(parts, axis=1).astype(jnp.bfloat16),
                values_of(start, g),
                preferred_element_type=jnp.float32,
            )
            return mixed, sum(parts[1:], parts[0])

        for g in range(kv_heads):
            acc[g], total[g] = weigh(last, 0, g)

        @pl.loop(0, chunks)
        def _(t):
            start = start_of(t)
            for g in range(kv_heads):
                mixed, part = weigh(start, t + 1, g)
                acc[g] += mixed
                total[g] += part

        for g in range(kv_heads):
            out = (acc[g] / jnp.sum(total[g], axis=-1, keepdims=True)).astype(o_ref.dtype)
            for h in range(group):
                column = (g * group + h) * HEAD_DIM
                o_ref[:, column : column + HEAD_DIM] = out[h * SEG : (h + 1) * SEG]


def attend(segs, table, blocks, queries, suffix, pool):
    count = segs.shape[0]
    width = queries.shape[1]
    suffix_rows, columns = suffix.shape
    kv_heads = columns // (2 * HEAD_DIM)
    rows = width // (HEAD_DIM * kv_heads) * SEG
    keys = suffix_rows // 2 + MAXB * BLK
    chunks = suffix_rows // BLK + MAXB
    return pl.pallas_call(
        attend_kernel,
        out_shape=jax.ShapeDtypeStruct((count * SEG, width), queries.dtype),
        grid_spec=pltpu.PrefetchScalarGridSpec(
            num_scalar_prefetch=3,
            grid=(count,),
            in_specs=[
                pl.BlockSpec((SEG, width), lambda i, segs, *_: (jnp.maximum(segs[i], 0), 0)),
                pl.BlockSpec(memory_space=pl.ANY),
                pl.BlockSpec(memory_space=pl.ANY),
            ],
            out_specs=pl.BlockSpec((SEG, width), lambda i, *_: (i, 0)),
            scratch_shapes=[
                pltpu.VMEM((suffix_rows + MAXB * BLK, columns), suffix.dtype),
                pltpu.VMEM((kv_heads, chunks, rows, BLK), jnp.float32),
                pltpu.VMEM((kv_heads, rows, HEAD_DIM), jnp.float32),
                pltpu.VMEM((kv_heads, rows, HEAD_DIM), jnp.float32),
                pltpu.VMEM((kv_heads, rows, HEAD_DIM), jnp.float32),
                pltpu.SemaphoreType.DMA((MAXB + 1,)),
            ],
        ),
        compiler_params=pltpu.CompilerParams(vmem_limit_bytes=40 * 2**20),
        cost_estimate=pl.CostEstimate(
            flops=8 * count * SEG * width * keys,
            bytes_accessed=2 * (2 * count * SEG * width + 2 * suffix_rows * columns),
            transcendentals=count * SEG * keys * width // HEAD_DIM,
        ),
    )(segs, table, blocks, queries, suffix, pool)


def place_kernel(spans, starts, *refs):
    pieces, out, sems = refs[: len(spans)], refs[len(spans)], refs[len(spans) + 1]
    copies = []
    for i, rows in enumerate(spans):
        start = pl.multiple_of(starts[i], SEG)
        copies.append(pltpu.make_async_copy(pieces[i], out.at[pl.ds(start, rows)], sems.at[i]))
    for copy in copies:
        copy.start()
    for copy in copies:
        copy.wait()


def place(pieces, starts, rows):
    spans = [piece.shape[0] for piece in pieces]
    assert sum(spans) == rows
    return pl.pallas_call(
        functools.partial(place_kernel, spans),
        out_shape=jax.ShapeDtypeStruct((rows, pieces[0].shape[1]), pieces[0].dtype),
        grid_spec=pltpu.PrefetchScalarGridSpec(
            num_scalar_prefetch=1,
            grid=(),
            in_specs=[pl.BlockSpec(memory_space=pl.ANY)] * len(pieces),
            out_specs=pl.BlockSpec(memory_space=pl.ANY),
            scratch_shapes=[pltpu.SemaphoreType.DMA((len(pieces),))],
        ),
        cost_estimate=pl.CostEstimate(
            flops=0, bytes_accessed=4 * rows * pieces[0].shape[1], transcendentals=0
        ),
    )(starts, *pieces)


def swap(rows, distance):
    size = lax.axis_size("replica")
    return lax.ppermute(rows, "replica", [(i, i ^ distance) for i in range(size)])


def swap_some(rows, distance, segments):
    def branch(count):
        def run(rows):
            if count == 0:
                return jnp.zeros_like(rows)
            got = swap(rows[: count * SEG], distance)
            return jnp.pad(got, ((0, rows.shape[0] - got.shape[0]), (0, 0)))

        return run

    return lax.switch(segments, [branch(c) for c in range(rows.shape[0] // SEG + 1)], rows)


def body(queries, suffix_cache, cache_pool, block_table, prefix_blocks, segment_owner):
    replicas = lax.axis_size("replica")
    me = lax.axis_index("replica")
    capacity = max(2, 2 * SEGS // replicas)
    base = SEGS // replicas
    order = jnp.arange(SEGS, dtype=jnp.int32)
    owner = segment_owner[:, 0]
    same = owner[None, :] == owner[:, None]
    slot = jnp.sum((same & (order[None, :] < order[:, None])).astype(jnp.int32), axis=1)
    distance = owner ^ me
    chooser = (distance[None, None, :] == jnp.arange(replicas, dtype=jnp.int32)[:, None, None]) & (
        slot[None, None, :] == jnp.arange(capacity, dtype=jnp.int32)[None, :, None]
    )
    segs = jnp.sum(jnp.where(chooser, order + 1, 0), axis=2) - 1
    counts = jnp.sum((segs >= 0).astype(jnp.int32), axis=1)
    every = lax.all_gather(counts, "replica")
    others = jnp.arange(replicas, dtype=jnp.int32)
    incoming = jnp.sum(
        jnp.where(others[:, None] ^ me == others[None, :], every, 0), axis=0
    )
    extra = jnp.clip(jnp.maximum(counts, incoming) - base, 0, capacity - base)

    run = lambda ids: attend(
        ids, block_table[0], prefix_blocks, queries, suffix_cache, cache_pool
    )
    far = list(range(replicas - 1, 0, -1))
    if replicas == 4:
        stages = [[(3, 0, 2)], [(2, 0, 2)], [(3, 2, 4)], [(2, 2, 4)], [(1, 0, 4)]]
    else:
        stages = [[(k, 0, base) for k in far]]
    pieces, starts = [], []

    def put(rows, k, first):
        pieces.append(rows)
        starts.append(((me ^ k) * capacity + first) * SEG)

    for stage in stages:
        rows = run(jnp.concatenate([segs[k, a:b] for k, a, b in stage]))
        at = 0
        for k, a, b in stage:
            put(swap(rows[at : at + (b - a) * SEG], k), k, a)
            at += (b - a) * SEG
    rest = run(jnp.concatenate([segs[k, base:] for k in far] + [segs[0]]))
    span = (capacity - base) * SEG
    for i, k in enumerate(far):
        put(swap_some(rest[i * span : (i + 1) * span], k, extra[k]), k, base)
    put(rest[len(far) * span :], 0, 0)
    return place(pieces, jnp.stack(starts).astype(jnp.int32), replicas * capacity * SEG)


def solution(mesh):
    in_specs = (
        P(("groups", "replica"), "tensor"),
        P(("groups", "replica"), "tensor"),
        P(("groups", "replica"), "tensor"),
        P(("groups", "replica"), None),
        P(("groups", "replica")),
        P(("groups", "replica"), None),
    )
    out_specs = P(("groups", "replica"), "tensor")
    return jax.shard_map(body, mesh=mesh, in_specs=in_specs, out_specs=out_specs, check_vma=False)
```

```python
import functools
import math

import jax
import jax.numpy as jnp
from jax import lax
from jax.experimental import pallas as pl
from jax.experimental.pallas import tpu as pltpu
from jax.sharding import PartitionSpec as P

HEAD_DIM = 128
BLK = 256
MAXB = 4
SEGS = 16
SEG = 64
EXPO = HEAD_DIM ** (-0.5) * math.log2(math.e)
LOWEST = -1e38


def segment_at(plan, step, me, owner):
    distance, slot = jnp.int32(plan[0][0]), jnp.int32(plan[0][1])
    for i, (k, j) in enumerate(plan[1:], 1):
        distance, slot = jnp.where(step == i, k, distance), jnp.where(step == i, j, slot)
    target = me[0] ^ distance
    seen, seg = jnp.int32(0), jnp.int32(-1)
    for s in range(SEGS):
        match = owner[s] == target
        seg = jnp.where(match & (seen == slot), s, seg)
        seen = seen + match.astype(jnp.int32)
    return seg


def attend_kernel(
    plan, me, owner, table, blocks, q_ref, suffix_hbm, pool_hbm, o_ref, cache, scores, peak, acc, total, sems
):
    step = pl.program_id(0)
    seg = segment_at(plan, step, me, owner)
    suffix_rows = suffix_hbm.shape[0]
    kv_heads = suffix_hbm.shape[1] // (2 * HEAD_DIM)
    group = q_ref.shape[1] // (HEAD_DIM * kv_heads)
    rows = group * SEG

    @pl.when(step == 0)
    def _():
        copies = [
            pltpu.make_async_copy(suffix_hbm, cache.at[pl.ds(0, suffix_rows)], sems.at[MAXB])
        ]
        for b in range(MAXB):
            start = pl.multiple_of(table[b] * BLK, BLK)
            copies.append(
                pltpu.make_async_copy(
                    pool_hbm.at[pl.ds(start, BLK)],
                    cache.at[pl.ds(suffix_rows + b * BLK, BLK)],
                    sems.at[b],
                )
            )
        for copy in copies:
            copy.start()
        for copy in copies:
            copy.wait()

    @pl.when(seg < 0)
    def _():
        o_ref[...] = jnp.zeros_like(o_ref)

    @pl.when(seg >= 0)
    def _():
        whole = seg * SEG // BLK
        chunks = whole + blocks[0]

        def queries_of(g):
            first = g * group
            return jnp.concatenate(
                [q_ref[:, (first + h) * HEAD_DIM : (first + h + 1) * HEAD_DIM] for h in range(group)],
                axis=0,
            )

        def keys_of(start, g):
            return cache[pl.ds(start, BLK), 2 * g * HEAD_DIM : (2 * g + 1) * HEAD_DIM]

        def values_of(start, g):
            return cache[pl.ds(start, BLK), (2 * g + 1) * HEAD_DIM : (2 * g + 2) * HEAD_DIM]

        def start_of(t):
            start = jnp.where(t < whole, t * BLK, suffix_rows + (t - whole) * BLK)
            return pl.multiple_of(start, BLK)

        def dot_keys(start, g):
            return lax.dot_general(
                queries_of(g),
                keys_of(start, g),
                (((1,), (1,)), ((), ())),
                preferred_element_type=jnp.float32,
            )

        def halves_max(s):
            top = s[:, :HEAD_DIM]
            for c in range(1, BLK // HEAD_DIM):
                top = jnp.maximum(top, s[:, c * HEAD_DIM : (c + 1) * HEAD_DIM])
            return top

        last = pl.multiple_of(whole * BLK, BLK)
        token = lax.broadcasted_iota(jnp.int32, (rows, BLK), 0) % SEG + (seg * SEG - whole * BLK)
        seen = lax.broadcasted_iota(jnp.int32, (rows, BLK), 1) <= token
        for g in range(kv_heads):
            s = jnp.where(seen, dot_keys(last, g), LOWEST)
            scores[g, 0] = s
            peak[g] = halves_max(s)

        @pl.loop(0, chunks)
        def _(t):
            start = start_of(t)
            for g in range(kv_heads):
                s = dot_keys(start, g)
                scores[g, t + 1] = s
                peak[g] = jnp.maximum(peak[g], halves_max(s))

        for g in range(kv_heads):
            top = jnp.max(peak[g], axis=-1, keepdims=True)
            peak[g] = jnp.broadcast_to(top, (rows, HEAD_DIM))

        def weigh(start, t, g):
            top = peak[g]
            parts = [
                jnp.exp2((scores[g, t, :, c * HEAD_DIM : (c + 1) * HEAD_DIM] - top) * EXPO)
                for c in range(BLK // HEAD_DIM)
            ]
            mixed = jnp.dot(
                jnp.concatenate(parts, axis=1).astype(jnp.bfloat16),
                values_of(start, g),
                preferred_element_type=jnp.float32,
            )
            return mixed, sum(parts[1:], parts[0])

        for g in range(kv_heads):
            acc[g], total[g] = weigh(last, 0, g)

        @pl.loop(0, chunks)
        def _(t):
            start = start_of(t)
            for g in range(kv_heads):
                mixed, part = weigh(start, t + 1, g)
                acc[g] += mixed
                total[g] += part

        for g in range(kv_heads):
            out = (acc[g] / jnp.sum(total[g], axis=-1, keepdims=True)).astype(o_ref.dtype)
            for h in range(group):
                column = (g * group + h) * HEAD_DIM
                o_ref[:, column : column + HEAD_DIM] = out[h * SEG : (h + 1) * SEG]


def attend(plan, me, owner, table, blocks, queries, suffix, pool):
    count = len(plan)
    width = queries.shape[1]
    suffix_rows, columns = suffix.shape
    kv_heads = columns // (2 * HEAD_DIM)
    rows = width // (HEAD_DIM * kv_heads) * SEG
    chunks = suffix_rows // BLK + MAXB
    return pl.pallas_call(
        functools.partial(attend_kernel, plan),
        out_shape=jax.ShapeDtypeStruct((count * SEG, width), queries.dtype),
        grid_spec=pltpu.PrefetchScalarGridSpec(
            num_scalar_prefetch=4,
            grid=(count,),
            in_specs=[
                pl.BlockSpec(
                    (SEG, width),
                    lambda i, me, owner, *_: (
                        jnp.maximum(segment_at(plan, i, me, owner), 0),
                        0,
                    ),
                ),
                pl.BlockSpec(memory_space=pl.ANY),
                pl.BlockSpec(memory_space=pl.ANY),
            ],
            out_specs=pl.BlockSpec((SEG, width), lambda i, *_: (i, 0)),
            scratch_shapes=[
                pltpu.VMEM((suffix_rows + MAXB * BLK, columns), suffix.dtype),
                pltpu.VMEM((kv_heads, chunks, rows, BLK), jnp.float32),
                pltpu.VMEM((kv_heads, rows, HEAD_DIM), jnp.float32),
                pltpu.VMEM((kv_heads, rows, HEAD_DIM), jnp.float32),
                pltpu.VMEM((kv_heads, rows, HEAD_DIM), jnp.float32),
                pltpu.SemaphoreType.DMA((MAXB + 1,)),
            ],
        ),
        compiler_params=pltpu.CompilerParams(vmem_limit_bytes=56 * 2**20),
        cost_estimate=pl.CostEstimate(flops=0, bytes_accessed=SEG * width, transcendentals=0),
    )(me, owner, table, blocks, queries, suffix, pool)


def swap(rows, distance):
    size = lax.axis_size("replica")
    return lax.ppermute(rows, "replica", [(i, i ^ distance) for i in range(size)])


def put(out, rows, start):
    return lax.dynamic_update_slice(out, rows, (start, 0))


def swap_some(out, rows, distance, start, segments):
    def branch(count):
        def run(out, rows):
            if count == 0:
                return out
            return put(out, swap(rows[: count * SEG], distance), start)

        return run

    return lax.switch(segments, [branch(c) for c in range(rows.shape[0] // SEG + 1)], out, rows)


def body(queries, suffix_cache, cache_pool, block_table, prefix_blocks, segment_owner):
    replicas = lax.axis_size("replica")
    me = lax.axis_index("replica").astype(jnp.int32)
    capacity = max(2, 2 * SEGS // replicas)
    base = SEGS // replicas
    owner = segment_owner[:, 0]
    far = list(range(replicas - 1, 0, -1))
    if replicas == 4:
        stages = [[(3, 0, 2)], [(2, 0, 4)], [(3, 2, 3)], [(1, 0, 4)]]
        final = [(3, 3, 4)]
    else:
        stages = [[(k, 0, base) for k in far]]
        final = []

    def plan_of(stage):
        return [(k, j) for k, a, b in stage for j in range(a, b)]

    def run(plan):
        return attend(
            plan, me[None], owner, block_table[0], prefix_blocks, queries, suffix_cache, cache_pool
        )

    def row_of(k, slot):
        return ((me ^ k) * capacity + slot) * SEG

    extra = [jnp.int32(0)]
    for k in range(1, replicas):
        mine = jnp.sum((owner == (me ^ k)).astype(jnp.int32))
        most = jnp.maximum(mine, swap(mine[None], k)[0])
        extra.append(jnp.clip(most - base, 0, capacity - base))
    sent = []

    def send(rows, stage):
        at = 0
        for k, a, b in stage:
            sent.append((swap(rows[at : at + (b - a) * SEG], k), row_of(k, a)))
            at += (b - a) * SEG
        return rows[at:]

    for stage in stages:
        rows = run(plan_of(stage))
        owner, rows, extra = lax.optimization_barrier((owner, rows, extra))
        send(rows, stage)
    owner, sent[0] = lax.optimization_barrier((owner, sent[0]))
    early = len(sent)
    rest = run(plan_of(final + [(k, base, capacity) for k in far] + [(0, 0, capacity)]))
    rest = send(rest, final)
    span = (capacity - base) * SEG
    out = jnp.zeros((replicas * capacity * SEG, queries.shape[1]), queries.dtype)
    out = put(out, rest[len(far) * span :], row_of(0, 0))
    for rows, start in sent[:early]:
        out = put(out, rows, start)
    for i, k in enumerate(reversed(far)):
        at = (len(far) - 1 - i) * span
        out = swap_some(out, rest[at : at + span], k, row_of(k, base), extra[k])
    for rows, start in sent[early:]:
        out = put(out, rows, start)
    return out


def solution(mesh):
    in_specs = (
        P(("groups", "replica"), "tensor"),
        P(("groups", "replica"), "tensor"),
        P(("groups", "replica"), "tensor"),
        P(("groups", "replica"), None),
        P(("groups", "replica")),
        P(("groups", "replica"), None),
    )
    out_specs = P(("groups", "replica"), "tensor")
    return jax.shard_map(body, mesh=mesh, in_specs=in_specs, out_specs=out_specs, check_vma=False)
```

```python
import functools
import math

import jax
import jax.numpy as jnp
from jax import lax
from jax.experimental import pallas as pl
from jax.experimental.pallas import tpu as pltpu
from jax.sharding import PartitionSpec as P

HEAD_DIM = 128
BLK = 256
MAXB = 4
SEGS = 16
SEG = 64
EXPO = HEAD_DIM ** (-0.5) * math.log2(math.e)
LOWEST = -1e38
HEADROOM = 64.0


def pick(slots, step):
    distance, slot = jnp.int32(slots[0][0]), jnp.int32(slots[0][1])
    for i, (k, j) in enumerate(slots[1:], 1):
        distance, slot = jnp.where(step >= i, k, distance), jnp.where(step >= i, j, slot)
    return distance, slot


def segment_at(plan, step, me, owner):
    distance, slot = pick(plan, step)
    target = me[0] ^ distance
    seen, seg = jnp.int32(0), jnp.int32(-1)
    for s in range(SEGS):
        match = owner[s] == target
        seg = jnp.where(match & (seen == slot), s, seg)
        seen = seen + match.astype(jnp.int32)
    return seg


def attend_kernel(
    plan, firsts, me, owner, table, blocks, q_ref, suffix_hbm, pool_hbm, *refs
):
    outs, (cache, shift, acc, total, sems) = refs[:-5], refs[-5:]
    step = pl.program_id(0)
    seg = segment_at(plan, step, me, owner)
    suffix_rows = suffix_hbm.shape[0]
    kv_heads = suffix_hbm.shape[1] // (2 * HEAD_DIM)
    group = q_ref.shape[1] // (HEAD_DIM * kv_heads)
    rows = group * SEG
    halves = BLK // HEAD_DIM

    @pl.when(step == 0)
    def _():
        copies = [
            pltpu.make_async_copy(suffix_hbm, cache.at[pl.ds(0, suffix_rows)], sems.at[MAXB])
        ]
        for b in range(MAXB):
            start = pl.multiple_of(table[b] * BLK, BLK)
            copies.append(
                pltpu.make_async_copy(
                    pool_hbm.at[pl.ds(start, BLK)],
                    cache.at[pl.ds(suffix_rows + b * BLK, BLK)],
                    sems.at[b],
                )
            )
        for copy in copies:
            copy.start()
        for copy in copies:
            copy.wait()

    def each_out(write):
        for i, o_ref in enumerate(outs):
            end = firsts[i + 1] if i + 1 < len(outs) else len(plan)
            pl.when((step >= firsts[i]) & (step < end))(functools.partial(write, o_ref))

    @pl.when(seg < 0)
    def _():
        def clear(o_ref):
            o_ref[...] = jnp.zeros_like(o_ref)

        each_out(clear)

    @pl.when(seg >= 0)
    def _():
        whole = seg * SEG // BLK
        chunks = whole + blocks[0]
        last = pl.multiple_of(whole * BLK, BLK)

        def queries_of(g):
            at = g * group
            return jnp.concatenate(
                [q_ref[:, (at + h) * HEAD_DIM : (at + h + 1) * HEAD_DIM] for h in range(group)],
                axis=0,
            )

        def start_of(t):
            start = jnp.where(t < whole, t * BLK, suffix_rows + (t - whole) * BLK)
            return pl.multiple_of(start, BLK)

        def dot_keys(start, g):
            return lax.dot_general(
                queries_of(g),
                cache[pl.ds(start, BLK), 2 * g * HEAD_DIM : (2 * g + 1) * HEAD_DIM],
                (((1,), (1,)), ((), ())),
                preferred_element_type=jnp.float32,
            )

        def dot_last(g):
            token = lax.broadcasted_iota(jnp.int32, (rows, BLK), 0) % SEG + (seg * SEG - last)
            seen = lax.broadcasted_iota(jnp.int32, (rows, BLK), 1) <= token
            return jnp.where(seen, dot_keys(last, g), LOWEST)

        def parts_of(s):
            return [s[:, c * HEAD_DIM : (c + 1) * HEAD_DIM] for c in range(halves)]

        def most_of(parts):
            return functools.reduce(jnp.maximum, parts)

        def weigh(s, start, g):
            shifted = [(part - shift[g]) * EXPO for part in parts_of(s)]
            weights = [jnp.exp2(part) for part in shifted]
            mixed = jnp.dot(
                jnp.concatenate(weights, axis=1).astype(jnp.bfloat16),
                cache[pl.ds(start, BLK), (2 * g + 1) * HEAD_DIM : (2 * g + 2) * HEAD_DIM],
                preferred_element_type=jnp.float32,
            )
            over = jnp.max(most_of(shifted).reshape(rows // 8, 8, HEAD_DIM), axis=0)
            return mixed, functools.reduce(jnp.add, weights), over

        def visit(starts, over):
            for g in range(kv_heads):
                found = [weigh(dot_keys(start, g), start, g) for start in starts]
                acc[g] += functools.reduce(jnp.add, [f[0] for f in found])
                total[g] += functools.reduce(jnp.add, [f[1] for f in found])
                over = most_of([over] + [f[2] for f in found])
            return over

        def visit_all():
            over = jnp.zeros((8, HEAD_DIM), jnp.float32)
            over = lax.fori_loop(
                0,
                chunks // 2,
                lambda t, over: visit([start_of(2 * t), start_of(2 * t + 1)], over),
                over,
            )
            return lax.fori_loop(
                chunks // 2 * 2, chunks, lambda t, over: visit([start_of(t)], over), over
            )

        def begin(g, s):
            acc[g], total[g], _ = weigh(s, last, g)

        def widest(top):
            return jnp.broadcast_to(jnp.max(top, axis=-1, keepdims=True), (rows, HEAD_DIM))

        for g in range(kv_heads):
            s = dot_last(g)
            shift[g] = widest(most_of(parts_of(s)))
            begin(g, s)
        over = visit_all()

        @pl.when(jnp.max(over) > HEADROOM)
        def _():
            for g in range(kv_heads):
                shift[g] = most_of(parts_of(dot_last(g)))

            @pl.loop(0, chunks)
            def _(t):
                for g in range(kv_heads):
                    shift[g] = most_of([shift[g]] + parts_of(dot_keys(start_of(t), g)))

            for g in range(kv_heads):
                shift[g] = widest(shift[g])
                begin(g, dot_last(g))
            visit_all()

        def finish(o_ref):
            for g in range(kv_heads):
                out = (acc[g] / jnp.sum(total[g], axis=-1, keepdims=True)).astype(o_ref.dtype)
                for h in range(group):
                    column = (g * group + h) * HEAD_DIM
                    o_ref[:, column : column + HEAD_DIM] = out[h * SEG : (h + 1) * SEG]

        each_out(finish)


def attend(groups, placed, me, owner, table, blocks, queries, suffix, pool):
    width = queries.shape[1]
    suffix_rows, columns = suffix.shape
    kv_heads = columns // (2 * HEAD_DIM)
    rows = width // (HEAD_DIM * kv_heads) * SEG
    steps, firsts, shapes, specs = [], [], [], []

    def block_of(first, count, i, *_):
        return (jnp.clip(i - first, 0, count - 1), 0)

    for group in groups:
        firsts.append(len(steps))
        shapes.append(jax.ShapeDtypeStruct((len(group) * SEG, width), queries.dtype))
        specs.append(
            pl.BlockSpec((SEG, width), functools.partial(block_of, len(steps), len(group)))
        )
        steps += group
    if placed:
        slots, total_rows, capacity = placed
        own = len(steps)
        firsts.append(own)

        def place_of(i, me, *_):
            k, slot = pick(slots, i - own)
            return ((me[0] ^ k) * capacity + slot, 0)

        shapes.append(jax.ShapeDtypeStruct((total_rows, width), queries.dtype))
        specs.append(pl.BlockSpec((SEG, width), place_of))
        steps += [(k, slot if k == 0 else SEGS) for k, slot in slots]
    return pl.pallas_call(
        functools.partial(attend_kernel, steps, firsts),
        out_shape=shapes,
        grid_spec=pltpu.PrefetchScalarGridSpec(
            num_scalar_prefetch=4,
            grid=(len(steps),),
            in_specs=[
                pl.BlockSpec(
                    (SEG, width),
                    lambda i, me, owner, *_: (
                        jnp.maximum(segment_at(steps, i, me, owner), 0),
                        0,
                    ),
                ),
                pl.BlockSpec(memory_space=pl.ANY),
                pl.BlockSpec(memory_space=pl.ANY),
            ],
            out_specs=specs,
            scratch_shapes=[
                pltpu.VMEM((suffix_rows + MAXB * BLK, columns), suffix.dtype),
                pltpu.VMEM((kv_heads, rows, HEAD_DIM), jnp.float32),
                pltpu.VMEM((kv_heads, rows, HEAD_DIM), jnp.float32),
                pltpu.VMEM((kv_heads, rows, HEAD_DIM), jnp.float32),
                pltpu.SemaphoreType.DMA((MAXB + 1,)),
            ],
        ),
        compiler_params=pltpu.CompilerParams(vmem_limit_bytes=56 * 2**20),
        cost_estimate=pl.CostEstimate(flops=0, bytes_accessed=SEG * width, transcendentals=0),
    )(me, owner, table, blocks, queries, suffix, pool)


def put_kernel(start, rows_ref, old, o_ref):
    o_ref[...] = rows_ref[...]


def put(out, rows, start):
    width = out.shape[1]
    return pl.pallas_call(
        put_kernel,
        out_shape=jax.ShapeDtypeStruct(out.shape, out.dtype),
        grid_spec=pltpu.PrefetchScalarGridSpec(
            num_scalar_prefetch=1,
            grid=(rows.shape[0] // SEG,),
            in_specs=[
                pl.BlockSpec((SEG, width), lambda i, start: (i, 0)),
                pl.BlockSpec(memory_space=pl.ANY),
            ],
            out_specs=pl.BlockSpec((SEG, width), lambda i, start: (start[0] + i, 0)),
        ),
        input_output_aliases={2: 0},
        compiler_params=pltpu.CompilerParams(vmem_limit_bytes=4 * 2**20),
        cost_estimate=pl.CostEstimate(flops=0, bytes_accessed=SEG * width, transcendentals=0),
    )(start[None], rows, out)


def swap(rows, distance):
    size = lax.axis_size("replica")
    return lax.ppermute(rows, "replica", [(i, i ^ distance) for i in range(size)])


def swap_some(out, rows, distance, start, segments):
    def branch(count):
        def run(out, rows):
            if count == 0:
                return out
            return put(out, swap(rows[: count * SEG], distance), start)

        return run

    return lax.switch(segments, [branch(c) for c in range(rows.shape[0] // SEG + 1)], out, rows)


def body(queries, suffix_cache, cache_pool, block_table, prefix_blocks, segment_owner):
    replicas = lax.axis_size("replica")
    me = lax.axis_index("replica").astype(jnp.int32)
    capacity = max(2, 2 * SEGS // replicas)
    base = SEGS // replicas
    owner = segment_owner[:, 0]
    far = list(range(replicas - 1, 0, -1))
    before = far[:1] if replicas == 4 else far

    def slots_of(k, a, b):
        return [(k, j) for j in range(a, b)]

    def run(groups, placed=None):
        return attend(
            groups,
            placed,
            me[None],
            owner,
            block_table[0],
            prefix_blocks,
            queries,
            suffix_cache,
            cache_pool,
        )

    def row_of(k, slot):
        return (me ^ k) * capacity + slot

    theirs = [swap(segment_owner, k) for k in range(1, replicas)]
    sent = {}
    for k, rows in zip(before, run([slots_of(k, 0, base) for k in before])):
        owner, rows, theirs = lax.optimization_barrier((owner, rows, theirs))
        sent[k] = swap(rows, k)
    after = [k for k in far if k not in before]
    *rest, out = run(
        [slots_of(k, 0, base) for k in after] + [slots_of(k, base, capacity) for k in far],
        (
            slots_of(0, 0, capacity) + [s for k in far for s in slots_of(k, base, capacity)],
            replicas * capacity * SEG,
            capacity,
        ),
    )
    for k, rows in zip(after, rest):
        sent[k] = swap(rows, k)
    distances = jnp.arange(1, replicas, dtype=jnp.int32)
    mine = jnp.sum((owner[None, :] == (me ^ distances)[:, None]).astype(jnp.int32), axis=1)
    given = jnp.sum((jnp.concatenate(theirs, axis=1) == me).astype(jnp.int32), axis=0)
    extra = jnp.clip(jnp.maximum(mine, given) - base, 0, capacity - base)
    for k in before:
        out = put(out, sent[k], row_of(k, 0))
    for k, rows in reversed(list(zip(far, rest[len(after) :]))):
        out = swap_some(out, rows, k, row_of(k, base), extra[k - 1])
    for k in reversed(after):
        out = put(out, sent[k], row_of(k, 0))
    return out


def solution(mesh):
    in_specs = (
        P(("groups", "replica"), "tensor"),
        P(("groups", "replica"), "tensor"),
        P(("groups", "replica"), "tensor"),
        P(("groups", "replica"), None),
        P(("groups", "replica")),
        P(("groups", "replica"), None),
    )
    out_specs = P(("groups", "replica"), "tensor")
    return jax.shard_map(body, mesh=mesh, in_specs=in_specs, out_specs=out_specs, check_vma=False)
```

```python
import functools
import math

import jax
import jax.numpy as jnp
from jax import lax
from jax.experimental import pallas as pl
from jax.experimental.pallas import tpu as pltpu
from jax.sharding import PartitionSpec as P

HEAD_DIM = 128
BLK = 256
MAXB = 4
SEGS = 16
SEG = 64
EXPO = HEAD_DIM ** (-0.5) * math.log2(math.e)
LOWEST = -1e38
HEADROOM = 64.0


def pick(slots, step):
    distance, slot = jnp.int32(slots[0][0]), jnp.int32(slots[0][1])
    for i, (k, j) in enumerate(slots[1:], 1):
        distance, slot = jnp.where(step >= i, k, distance), jnp.where(step >= i, j, slot)
    return distance, slot


def segment_at(plan, step, me, owner):
    distance, slot = pick(plan, step)
    target = me[0] ^ distance
    seen, seg = jnp.int32(0), jnp.int32(-1)
    for s in range(SEGS):
        match = owner[s] == target
        seg = jnp.where(match & (seen == slot), s, seg)
        seen = seen + match.astype(jnp.int32)
    return seg


def attend_kernel(
    plan, firsts, me, owner, table, blocks, q_ref, suffix_hbm, pool_hbm, *refs
):
    outs, (cache, shift, acc, total, sems) = refs[:-5], refs[-5:]
    step = pl.program_id(0)
    seg = segment_at(plan, step, me, owner)
    suffix_rows = suffix_hbm.shape[0]
    kv_heads = suffix_hbm.shape[1] // (2 * HEAD_DIM)
    group = q_ref.shape[1] // (HEAD_DIM * kv_heads)
    rows = group * SEG
    halves = BLK // HEAD_DIM

    @pl.when(step == 0)
    def _():
        copies = [
            pltpu.make_async_copy(suffix_hbm, cache.at[pl.ds(0, suffix_rows)], sems.at[MAXB])
        ]
        for b in range(MAXB):
            start = pl.multiple_of(table[b] * BLK, BLK)
            copies.append(
                pltpu.make_async_copy(
                    pool_hbm.at[pl.ds(start, BLK)],
                    cache.at[pl.ds(suffix_rows + b * BLK, BLK)],
                    sems.at[b],
                )
            )
        for copy in copies:
            copy.start()
        for copy in copies:
            copy.wait()

    def each_out(write):
        for i, o_ref in enumerate(outs):
            end = firsts[i + 1] if i + 1 < len(outs) else len(plan)
            pl.when((step >= firsts[i]) & (step < end))(functools.partial(write, o_ref))

    @pl.when(seg < 0)
    def _():
        def clear(o_ref):
            o_ref[...] = jnp.zeros_like(o_ref)

        each_out(clear)

    @pl.when(seg >= 0)
    def _():
        whole = seg * SEG // BLK
        chunks = whole + blocks[0]
        last = pl.multiple_of(whole * BLK, BLK)

        def queries_of(g):
            at = g * group
            return jnp.concatenate(
                [q_ref[:, (at + h) * HEAD_DIM : (at + h + 1) * HEAD_DIM] for h in range(group)],
                axis=0,
            )

        def start_of(t):
            start = jnp.where(t < whole, t * BLK, suffix_rows + (t - whole) * BLK)
            return pl.multiple_of(start, BLK)

        def dot_keys(start, g):
            return lax.dot_general(
                queries_of(g),
                cache[pl.ds(start, BLK), 2 * g * HEAD_DIM : (2 * g + 1) * HEAD_DIM],
                (((1,), (1,)), ((), ())),
                preferred_element_type=jnp.float32,
            )

        def dot_last(g):
            token = lax.broadcasted_iota(jnp.int32, (rows, BLK), 0) % SEG + (seg * SEG - last)
            seen = lax.broadcasted_iota(jnp.int32, (rows, BLK), 1) <= token
            return jnp.where(seen, dot_keys(last, g), LOWEST)

        def parts_of(s):
            return [s[:, c * HEAD_DIM : (c + 1) * HEAD_DIM] for c in range(halves)]

        def most_of(parts):
            return functools.reduce(jnp.maximum, parts)

        def weigh(s, start, g):
            shifted = [(part - shift[g]) * EXPO for part in parts_of(s)]
            weights = [jnp.exp2(part) for part in shifted]
            mixed = jnp.dot(
                jnp.concatenate(weights, axis=1).astype(jnp.bfloat16),
                cache[pl.ds(start, BLK), (2 * g + 1) * HEAD_DIM : (2 * g + 2) * HEAD_DIM],
                preferred_element_type=jnp.float32,
            )
            over = jnp.max(most_of(shifted).reshape(rows // 8, 8, HEAD_DIM), axis=0)
            return mixed, functools.reduce(jnp.add, weights), over

        def visit(starts, over):
            for g in range(kv_heads):
                found = [weigh(dot_keys(start, g), start, g) for start in starts]
                acc[g] += functools.reduce(jnp.add, [f[0] for f in found])
                total[g] += functools.reduce(jnp.add, [f[1] for f in found])
                over = most_of([over] + [f[2] for f in found])
            return over

        def visit_all():
            over = jnp.zeros((8, HEAD_DIM), jnp.float32)
            over = lax.fori_loop(
                0,
                chunks // 2,
                lambda t, over: visit([start_of(2 * t), start_of(2 * t + 1)], over),
                over,
            )
            return lax.fori_loop(
                chunks // 2 * 2, chunks, lambda t, over: visit([start_of(t)], over), over
            )

        def begin(g, s):
            acc[g], total[g], _ = weigh(s, last, g)

        def widest(top):
            return jnp.broadcast_to(jnp.max(top, axis=-1, keepdims=True), (rows, HEAD_DIM))

        for g in range(kv_heads):
            s = dot_last(g)
            shift[g] = widest(most_of(parts_of(s)))
            begin(g, s)
        over = visit_all()

        @pl.when(jnp.max(over) > HEADROOM)
        def _():
            for g in range(kv_heads):
                shift[g] = most_of(parts_of(dot_last(g)))

            @pl.loop(0, chunks)
            def _(t):
                for g in range(kv_heads):
                    shift[g] = most_of([shift[g]] + parts_of(dot_keys(start_of(t), g)))

            for g in range(kv_heads):
                shift[g] = widest(shift[g])
                begin(g, dot_last(g))
            visit_all()

        def finish(o_ref):
            for g in range(kv_heads):
                out = (acc[g] / jnp.sum(total[g], axis=-1, keepdims=True)).astype(o_ref.dtype)
                for h in range(group):
                    column = (g * group + h) * HEAD_DIM
                    o_ref[:, column : column + HEAD_DIM] = out[h * SEG : (h + 1) * SEG]

        each_out(finish)


def attend(groups, placed, me, owner, table, blocks, queries, suffix, pool):
    width = queries.shape[1]
    suffix_rows, columns = suffix.shape
    kv_heads = columns // (2 * HEAD_DIM)
    rows = width // (HEAD_DIM * kv_heads) * SEG
    steps, firsts, shapes, specs = [], [], [], []

    def block_of(first, count, i, *_):
        return (jnp.clip(i - first, 0, count - 1), 0)

    for group in groups:
        firsts.append(len(steps))
        shapes.append(jax.ShapeDtypeStruct((len(group) * SEG, width), queries.dtype))
        specs.append(
            pl.BlockSpec((SEG, width), functools.partial(block_of, len(steps), len(group)))
        )
        steps += group
    if placed:
        slots, total_rows, capacity = placed
        own = len(steps)
        firsts.append(own)

        def place_of(i, me, *_):
            k, slot = pick(slots, i - own)
            return ((me[0] ^ k) * capacity + slot, 0)

        shapes.append(jax.ShapeDtypeStruct((total_rows, width), queries.dtype))
        specs.append(pl.BlockSpec((SEG, width), place_of))
        steps += [(k, slot if k == 0 else SEGS) for k, slot in slots]
    return pl.pallas_call(
        functools.partial(attend_kernel, steps, firsts),
        out_shape=shapes,
        grid_spec=pltpu.PrefetchScalarGridSpec(
            num_scalar_prefetch=4,
            grid=(len(steps),),
            in_specs=[
                pl.BlockSpec(
                    (SEG, width),
                    lambda i, me, owner, *_: (
                        jnp.maximum(segment_at(steps, i, me, owner), 0),
                        0,
                    ),
                ),
                pl.BlockSpec(memory_space=pl.ANY),
                pl.BlockSpec(memory_space=pl.ANY),
            ],
            out_specs=specs,
            scratch_shapes=[
                pltpu.VMEM((suffix_rows + MAXB * BLK, columns), suffix.dtype),
                pltpu.VMEM((kv_heads, rows, HEAD_DIM), jnp.float32),
                pltpu.VMEM((kv_heads, rows, HEAD_DIM), jnp.float32),
                pltpu.VMEM((kv_heads, rows, HEAD_DIM), jnp.float32),
                pltpu.SemaphoreType.DMA((MAXB + 1,)),
            ],
        ),
        compiler_params=pltpu.CompilerParams(vmem_limit_bytes=56 * 2**20),
        cost_estimate=pl.CostEstimate(flops=0, bytes_accessed=SEG * width, transcendentals=0),
    )(me, owner, table, blocks, queries, suffix, pool)


def put_kernel(start, rows_ref, old, o_ref):
    o_ref[...] = rows_ref[...]


def put(out, rows, start):
    width = out.shape[1]
    return pl.pallas_call(
        put_kernel,
        out_shape=jax.ShapeDtypeStruct(out.shape, out.dtype),
        grid_spec=pltpu.PrefetchScalarGridSpec(
            num_scalar_prefetch=1,
            grid=(rows.shape[0] // SEG,),
            in_specs=[
                pl.BlockSpec((SEG, width), lambda i, start: (i, 0)),
                pl.BlockSpec(memory_space=pl.ANY),
            ],
            out_specs=pl.BlockSpec((SEG, width), lambda i, start: (start[0] + i, 0)),
        ),
        input_output_aliases={2: 0},
        compiler_params=pltpu.CompilerParams(vmem_limit_bytes=4 * 2**20),
        cost_estimate=pl.CostEstimate(flops=0, bytes_accessed=SEG * width, transcendentals=0),
    )(start[None], rows, out)


def swap(rows, distance):
    size = lax.axis_size("replica")
    return lax.ppermute(rows, "replica", [(i, i ^ distance) for i in range(size)])


def swap_some(out, rows, distance, start, segments):
    def branch(count):
        def run(out, rows):
            if count == 0:
                return out
            return put(out, swap(rows[: count * SEG], distance), start)

        return run

    return lax.switch(segments, [branch(c) for c in range(rows.shape[0] // SEG + 1)], out, rows)


def body(queries, suffix_cache, cache_pool, block_table, prefix_blocks, segment_owner):
    replicas = lax.axis_size("replica")
    me = lax.axis_index("replica").astype(jnp.int32)
    capacity = max(2, 2 * SEGS // replicas)
    base = SEGS // replicas
    owner = segment_owner[:, 0]
    far = list(range(replicas - 1, 0, -1))
    if replicas == 4:
        calls = [[(3, 0, 2)], [(2, 0, 4), (3, 2, 4)], [(1, 0, 4)]]
    else:
        calls = [[(k, 0, base) for k in far], []]

    def slots_of(k, a, b):
        return [(k, j) for j in range(a, b)]

    def run(groups, placed=None):
        return attend(
            groups,
            placed,
            me[None],
            owner,
            block_table[0],
            prefix_blocks,
            queries,
            suffix_cache,
            cache_pool,
        )

    def row_of(k, slot):
        return (me ^ k) * capacity + slot

    theirs = [swap(segment_owner, k) for k in range(1, replicas)]
    sent = []
    for call in calls[:-1]:
        made = run([slots_of(*part) for part in call])
        owner, made, theirs = lax.optimization_barrier((owner, made, theirs))
        sent.append([(swap(rows, k), row_of(k, a)) for (k, a, _), rows in zip(call, made)])
    owner, sent[0] = lax.optimization_barrier((owner, sent[0]))
    *rest, out = run(
        [slots_of(*part) for part in calls[-1]] + [slots_of(k, base, capacity) for k in far],
        (
            slots_of(0, 0, capacity) + [s for k in far for s in slots_of(k, base, capacity)],
            replicas * capacity * SEG,
            capacity,
        ),
    )
    last = [(swap(rows, k), row_of(k, a)) for (k, a, _), rows in zip(calls[-1], rest)]
    rest = rest[len(last) :]
    distances = jnp.arange(1, replicas, dtype=jnp.int32)
    mine = jnp.sum((owner[None, :] == (me ^ distances)[:, None]).astype(jnp.int32), axis=1)
    given = jnp.sum((jnp.concatenate(theirs, axis=1) == me).astype(jnp.int32), axis=0)
    extra = jnp.clip(jnp.maximum(mine, given) - base, 0, capacity - base)
    before = sent[0] + [s for part in sent[1:] for s in part[:1]]
    after = [s for part in sent[1:] for s in part[1:]] + last
    for rows, start in before:
        out = put(out, rows, start)
    for k, rows in reversed(list(zip(far, rest))):
        out = swap_some(out, rows, k, row_of(k, base), extra[k - 1])
    for rows, start in after:
        out = put(out, rows, start)
    return out


def solution(mesh):
    in_specs = (
        P(("groups", "replica"), "tensor"),
        P(("groups", "replica"), "tensor"),
        P(("groups", "replica"), "tensor"),
        P(("groups", "replica"), None),
        P(("groups", "replica")),
        P(("groups", "replica"), None),
    )
    out_specs = P(("groups", "replica"), "tensor")
    return jax.shard_map(body, mesh=mesh, in_specs=in_specs, out_specs=out_specs, check_vma=False)
```

```python
import functools
import math

import jax
import jax.numpy as jnp
from jax import lax
from jax.experimental import pallas as pl
from jax.experimental.pallas import tpu as pltpu
from jax.sharding import PartitionSpec as P

HEAD_DIM = 128
BLK = 256
MAXB = 4
SEGS = 16
SEG = 64
EXPO = HEAD_DIM ** (-0.5) * math.log2(math.e)
LOWEST = -1e38
HEADS_AT_ONCE = 4


def pick(slots, step):
    distance, slot = jnp.int32(slots[0][0]), jnp.int32(slots[0][1])
    for i, (k, j) in enumerate(slots[1:], 1):
        distance, slot = jnp.where(step >= i, k, distance), jnp.where(step >= i, j, slot)
    return distance, slot


def segment_at(plan, step, me, owner):
    distance, slot = pick(plan, step)
    target = me[0] ^ distance
    seen, seg = jnp.int32(0), jnp.int32(-1)
    for s in range(SEGS):
        match = owner[s] == target
        seg = jnp.where(match & (seen == slot), s, seg)
        seen = seen + match.astype(jnp.int32)
    return seg


def attend_kernel(plan, firsts, me, owner, table, blocks, q_ref, suffix_hbm, pool_hbm, *refs):
    outs, (cache, work, sems) = refs[:-3], refs[-3:]
    step = pl.program_id(0)
    seg = segment_at(plan, step, me, owner)
    suffix_rows = suffix_hbm.shape[0]
    heads = q_ref.shape[1] // HEAD_DIM
    group = heads // (suffix_hbm.shape[1] // (2 * HEAD_DIM))
    at_once = min(HEADS_AT_ONCE, group)
    rows = at_once * SEG
    prefix = MAXB * BLK

    @pl.when(step == 0)
    def _():
        copies = [
            pltpu.make_async_copy(suffix_hbm, cache.at[pl.ds(prefix, suffix_rows)], sems.at[MAXB])
        ]
        for b in range(MAXB):
            start = pl.multiple_of(table[b] * BLK, BLK)
            to = pl.multiple_of((b + MAXB - blocks[0]) % MAXB * BLK, BLK)
            copies.append(
                pltpu.make_async_copy(
                    pool_hbm.at[pl.ds(start, BLK)], cache.at[pl.ds(to, BLK)], sems.at[b]
                )
            )
        for copy in copies:
            copy.start()
        for copy in copies:
            copy.wait()

    def each_out(write):
        for i, o_ref in enumerate(outs):
            end = firsts[i + 1] if i + 1 < len(outs) else len(plan)
            pl.when((step >= firsts[i]) & (step < end))(functools.partial(write, o_ref))

    def attend_rows(o_ref, count, i):
        first = i * at_once
        low = pl.multiple_of((MAXB - blocks[0]) * BLK, BLK)
        pair = first // group * (2 * HEAD_DIM)

        def column(h):
            return pl.ds(pl.multiple_of((first + h) * HEAD_DIM, HEAD_DIM), HEAD_DIM)

        def cached(offset):
            lanes = pl.ds(pl.multiple_of(pair + offset, HEAD_DIM), HEAD_DIM)
            return cache[pl.ds(low, count * BLK), lanes]

        q = jnp.concatenate([q_ref[:, column(h)] for h in range(at_once)], axis=0)
        s = lax.dot_general(
            q, cached(0), (((1,), (1,)), ((), ())), preferred_element_type=jnp.float32
        )
        parts = [s[:, c : c + HEAD_DIM] for c in range(0, count * BLK, HEAD_DIM)]
        token = lax.broadcasted_iota(jnp.int32, (rows, HEAD_DIM), 0) % SEG + seg * SEG % BLK
        key = lax.broadcasted_iota(jnp.int32, (rows, HEAD_DIM), 1)
        masked = BLK // HEAD_DIM
        for c in range(masked):
            at = len(parts) - masked + c
            parts[at] = jnp.where(key + c * HEAD_DIM <= token, parts[at], LOWEST)
        top = jnp.max(functools.reduce(jnp.maximum, parts), axis=-1, keepdims=True)
        top = jnp.broadcast_to(top, (rows, HEAD_DIM))
        weights = [jnp.exp2((part - top) * EXPO) for part in parts]
        total = jnp.sum(functools.reduce(jnp.add, weights), axis=-1, keepdims=True)
        mixed = jnp.dot(
            jnp.concatenate([w.astype(jnp.bfloat16) for w in weights], axis=1),
            cached(HEAD_DIM),
            preferred_element_type=jnp.float32,
        )
        out = (mixed / total).astype(o_ref.dtype)
        for h in range(at_once):
            o_ref[:, column(h)] = out[h * SEG : (h + 1) * SEG]

    result = outs[0] if len(outs) == 1 else work

    @pl.when(seg < 0)
    def _():
        def clear(o_ref):
            o_ref[...] = jnp.zeros_like(o_ref)

        each_out(clear)

    @pl.when(seg >= 0)
    def _():
        blocks_seen = blocks[0] + seg * SEG // BLK + 1
        for count in range(2, MAXB + suffix_rows // BLK + 1):

            @pl.when(blocks_seen == count)
            def _():
                @pl.loop(0, heads // at_once)
                def _(i):
                    attend_rows(result, count, i)

        if len(outs) > 1:

            def hand(o_ref):
                o_ref[...] = work[...]

            each_out(hand)


def attend(groups, placed, me, owner, table, blocks, queries, suffix, pool):
    width = queries.shape[1]
    suffix_rows, columns = suffix.shape
    steps, firsts, shapes, specs = [], [], [], []

    def block_of(first, count, i, *_):
        return (jnp.clip(i - first, 0, count - 1), 0)

    for group in groups:
        firsts.append(len(steps))
        shapes.append(jax.ShapeDtypeStruct((len(group) * SEG, width), queries.dtype))
        specs.append(
            pl.BlockSpec((SEG, width), functools.partial(block_of, len(steps), len(group)))
        )
        steps += group
    if placed:
        slots, total_rows, capacity = placed
        own = len(steps)
        firsts.append(own)

        def place_of(i, me, *_):
            k, slot = pick(slots, i - own)
            return ((me[0] ^ k) * capacity + slot, 0)

        shapes.append(jax.ShapeDtypeStruct((total_rows, width), queries.dtype))
        specs.append(pl.BlockSpec((SEG, width), place_of))
        steps += [(k, slot if k == 0 else SEGS) for k, slot in slots]
    return pl.pallas_call(
        functools.partial(attend_kernel, steps, firsts),
        out_shape=shapes,
        grid_spec=pltpu.PrefetchScalarGridSpec(
            num_scalar_prefetch=4,
            grid=(len(steps),),
            in_specs=[
                pl.BlockSpec(
                    (SEG, width),
                    lambda i, me, owner, *_: (
                        jnp.maximum(segment_at(steps, i, me, owner), 0),
                        0,
                    ),
                ),
                pl.BlockSpec(memory_space=pl.ANY),
                pl.BlockSpec(memory_space=pl.ANY),
            ],
            out_specs=specs,
            scratch_shapes=[
                pltpu.VMEM((suffix_rows + MAXB * BLK, columns), suffix.dtype),
                pltpu.VMEM((SEG, width), queries.dtype),
                pltpu.SemaphoreType.DMA((MAXB + 1,)),
            ],
        ),
        compiler_params=pltpu.CompilerParams(vmem_limit_bytes=56 * 2**20),
        cost_estimate=pl.CostEstimate(flops=0, bytes_accessed=SEG * width, transcendentals=0),
    )(me, owner, table, blocks, queries, suffix, pool)


def put_kernel(start, rows_ref, old, o_ref):
    o_ref[...] = rows_ref[...]


def put(out, rows, start):
    width = out.shape[1]
    return pl.pallas_call(
        put_kernel,
        out_shape=jax.ShapeDtypeStruct(out.shape, out.dtype),
        grid_spec=pltpu.PrefetchScalarGridSpec(
            num_scalar_prefetch=1,
            grid=(rows.shape[0] // SEG,),
            in_specs=[
                pl.BlockSpec((SEG, width), lambda i, start: (i, 0)),
                pl.BlockSpec(memory_space=pl.ANY),
            ],
            out_specs=pl.BlockSpec((SEG, width), lambda i, start: (start[0] + i, 0)),
        ),
        input_output_aliases={2: 0},
        compiler_params=pltpu.CompilerParams(vmem_limit_bytes=4 * 2**20),
        cost_estimate=pl.CostEstimate(flops=0, bytes_accessed=SEG * width, transcendentals=0),
    )(start[None], rows, out)


def swap(rows, distance):
    size = lax.axis_size("replica")
    return lax.ppermute(rows, "replica", [(i, i ^ distance) for i in range(size)])


def swap_some(out, rows, distance, start, segments):
    def branch(count):
        def run(out, rows):
            if count == 0:
                return out
            return put(out, swap(rows[: count * SEG], distance), start)

        return run

    return lax.switch(segments, [branch(c) for c in range(rows.shape[0] // SEG + 1)], out, rows)


def body(queries, suffix_cache, cache_pool, block_table, prefix_blocks, segment_owner):
    replicas = lax.axis_size("replica")
    me = lax.axis_index("replica").astype(jnp.int32)
    capacity = max(2, 2 * SEGS // replicas)
    base = SEGS // replicas
    owner = segment_owner[:, 0]
    far = list(range(replicas - 1, 0, -1))
    if replicas == 4:
        calls = [[(3, 0, 2)], [(2, 0, 4), (3, 2, 4)], [(1, 0, 4)]]
    else:
        calls = [[(k, 0, base) for k in far], []]

    def slots_of(k, a, b):
        return [(k, j) for j in range(a, b)]

    def run(groups, placed=None):
        return attend(
            groups,
            placed,
            me[None],
            owner,
            block_table[0],
            prefix_blocks,
            queries,
            suffix_cache,
            cache_pool,
        )

    def row_of(k, slot):
        return (me ^ k) * capacity + slot

    theirs = [swap(segment_owner, k) for k in range(1, replicas)]
    sent = []
    for call in calls[:-1]:
        made = run([slots_of(*part) for part in call])
        owner, made, theirs = lax.optimization_barrier((owner, made, theirs))
        sent.append([(swap(rows, k), row_of(k, a)) for (k, a, _), rows in zip(call, made)])
    owner, sent[0] = lax.optimization_barrier((owner, sent[0]))
    *rest, out = run(
        [slots_of(*part) for part in calls[-1]] + [slots_of(k, base, capacity) for k in far],
        (
            slots_of(0, 0, capacity) + [s for k in far for s in slots_of(k, base, capacity)],
            replicas * capacity * SEG,
            capacity,
        ),
    )
    last = [(swap(rows, k), row_of(k, a)) for (k, a, _), rows in zip(calls[-1], rest)]
    rest = rest[len(last) :]
    distances = jnp.arange(1, replicas, dtype=jnp.int32)
    mine = jnp.sum((owner[None, :] == (me ^ distances)[:, None]).astype(jnp.int32), axis=1)
    given = jnp.sum((jnp.concatenate(theirs, axis=1) == me).astype(jnp.int32), axis=0)
    extra = jnp.clip(jnp.maximum(mine, given) - base, 0, capacity - base)
    before = sent[0] + [s for part in sent[1:] for s in part[:1]]
    after = [s for part in sent[1:] for s in part[1:]] + last
    for rows, start in before:
        out = put(out, rows, start)
    for k, rows in reversed(list(zip(far, rest))):
        out = swap_some(out, rows, k, row_of(k, base), extra[k - 1])
    for rows, start in after:
        out = put(out, rows, start)
    return out


def solution(mesh):
    in_specs = (
        P(("groups", "replica"), "tensor"),
        P(("groups", "replica"), "tensor"),
        P(("groups", "replica"), "tensor"),
        P(("groups", "replica"), None),
        P(("groups", "replica")),
        P(("groups", "replica"), None),
    )
    out_specs = P(("groups", "replica"), "tensor")
    return jax.shard_map(body, mesh=mesh, in_specs=in_specs, out_specs=out_specs, check_vma=False)
```

```python
import functools

import jax
import jax.numpy as jnp
from jax import lax
from jax.experimental import pallas as pl
from jax.experimental.pallas import tpu as pltpu
from jax.sharding import PartitionSpec as P

HEAD_DIM = 128
BLK = 256
MAXB = 4
SEGS = 16
SEG = 64
SCALE = HEAD_DIM ** (-0.5)
LOWEST = -1e38
HEADS_AT_ONCE = 4


def pick(slots, step):
    distance, slot = jnp.int32(slots[0][0]), jnp.int32(slots[0][1])
    for i, (k, j) in enumerate(slots[1:], 1):
        distance, slot = jnp.where(step >= i, k, distance), jnp.where(step >= i, j, slot)
    return distance, slot


def segment_at(plan, step, me, owner):
    distance, slot = pick(plan, step)
    target = me[0] ^ distance
    seen, seg = jnp.int32(0), jnp.int32(-1)
    for s in range(SEGS):
        match = owner[s] == target
        seg = jnp.where(match & (seen == slot), s, seg)
        seen = seen + match.astype(jnp.int32)
    return seg


def segment_table(me, owner, replicas, capacity):
    order = jnp.arange(SEGS, dtype=jnp.int32)
    same = owner[None, :] == owner[:, None]
    slot = jnp.sum((same & (order[None, :] < order[:, None])).astype(jnp.int32), axis=1)
    at = (owner ^ me) * capacity + slot
    chosen = jnp.arange(replicas * capacity, dtype=jnp.int32)[:, None] == at[None, :]
    segs = jnp.sum(jnp.where(chosen, order + 1, 0), axis=1) - 1
    return segs.reshape(replicas, capacity)


def attend_kernel(
    segment, steps, firsts, given, own, table, blocks, q_ref, suffix_hbm, pool_hbm, *refs
):
    outs, (cache, work, sems) = refs[:-3], refs[-3:]
    step = pl.program_id(0)
    seg = segment(step, given, own)
    suffix_rows = suffix_hbm.shape[0]
    heads = q_ref.shape[1] // HEAD_DIM
    group = heads // (suffix_hbm.shape[1] // (2 * HEAD_DIM))
    at_once = min(HEADS_AT_ONCE, group)
    rows = at_once * SEG
    prefix = MAXB * BLK

    @pl.when(step == 0)
    def _():
        copies = [
            pltpu.make_async_copy(suffix_hbm, cache.at[pl.ds(prefix, suffix_rows)], sems.at[MAXB])
        ]
        for b in range(MAXB):
            start = pl.multiple_of(table[b] * BLK, BLK)
            to = pl.multiple_of((b + MAXB - blocks[0]) % MAXB * BLK, BLK)
            copies.append(
                pltpu.make_async_copy(
                    pool_hbm.at[pl.ds(start, BLK)], cache.at[pl.ds(to, BLK)], sems.at[b]
                )
            )
        for copy in copies:
            copy.start()
        for copy in copies:
            copy.wait()

    def each_out(write):
        for i, o_ref in enumerate(outs):
            end = firsts[i + 1] if i + 1 < len(outs) else steps
            pl.when((step >= firsts[i]) & (step < end))(functools.partial(write, o_ref))

    def attend_rows(o_ref, count, i):
        first = i * at_once
        low = pl.multiple_of((MAXB - blocks[0]) * BLK, BLK)
        pair = first // group * (2 * HEAD_DIM)

        def column(h):
            return pl.ds(pl.multiple_of((first + h) * HEAD_DIM, HEAD_DIM), HEAD_DIM)

        def cached(offset):
            lanes = pl.ds(pl.multiple_of(pair + offset, HEAD_DIM), HEAD_DIM)
            return cache[pl.ds(low, count * BLK), lanes]

        q = jnp.concatenate([q_ref[:, column(h)] for h in range(at_once)], axis=0)
        s = lax.dot_general(
            q, cached(0), (((1,), (1,)), ((), ())), preferred_element_type=jnp.float32
        )
        parts = [s[:, c : c + HEAD_DIM] for c in range(0, count * BLK, HEAD_DIM)]
        token = lax.broadcasted_iota(jnp.int32, (rows, HEAD_DIM), 0) % SEG + seg * SEG % BLK
        key = lax.broadcasted_iota(jnp.int32, (rows, HEAD_DIM), 1)
        masked = BLK // HEAD_DIM
        for c in range(masked):
            at = len(parts) - masked + c
            parts[at] = jnp.where(key + c * HEAD_DIM <= token, parts[at], LOWEST)
        top = jnp.max(functools.reduce(jnp.maximum, parts), axis=-1, keepdims=True)
        top = jnp.broadcast_to(top, (rows, HEAD_DIM))
        weights = [jnp.exp((part - top) * SCALE) for part in parts]
        total = jnp.sum(functools.reduce(jnp.add, weights), axis=-1, keepdims=True)
        mixed = jnp.dot(
            jnp.concatenate([w.astype(jnp.bfloat16) for w in weights], axis=1),
            cached(HEAD_DIM),
            preferred_element_type=jnp.float32,
        )
        out = (mixed / total).astype(o_ref.dtype)
        for h in range(at_once):
            o_ref[:, column(h)] = out[h * SEG : (h + 1) * SEG]

    result = outs[0] if len(outs) == 1 else work

    @pl.when(seg < 0)
    def _():
        def clear(o_ref):
            o_ref[...] = jnp.zeros_like(o_ref)

        each_out(clear)

    @pl.when(seg >= 0)
    def _():
        blocks_seen = blocks[0] + seg * SEG // BLK + 1
        for count in range(2, MAXB + suffix_rows // BLK + 1):

            @pl.when(blocks_seen == count)
            def _():
                @pl.loop(0, heads // at_once)
                def _(i):
                    attend_rows(result, count, i)

        if len(outs) > 1:

            def hand(o_ref):
                o_ref[...] = work[...]

            each_out(hand)


def attend(groups, segs, placed, me, owner, table, blocks, queries, suffix, pool):
    width = queries.shape[1]
    suffix_rows, columns = suffix.shape
    steps, firsts, shapes, specs = [], [], [], []

    def block_of(first, count, i, *_):
        return (jnp.clip(i - first, 0, count - 1), 0)

    for group in groups:
        firsts.append(len(steps))
        shapes.append(jax.ShapeDtypeStruct((len(group) * SEG, width), queries.dtype))
        specs.append(
            pl.BlockSpec((SEG, width), functools.partial(block_of, len(steps), len(group)))
        )
        steps += group
    if segs is None:
        given, own = me[None], owner
        segment = functools.partial(segment_at, tuple(steps))
    else:
        given = jnp.concatenate([segs[g[0][0], g[0][1] : g[0][1] + len(g)] for g in groups])
        own = jnp.zeros((1,), jnp.int32)
        segment = lambda i, given, own: given[i]
    if placed:
        slots, capacity, total_rows = placed
        before = len(steps)
        firsts.append(before)
        shapes.append(jax.ShapeDtypeStruct((total_rows, width), queries.dtype))
        specs.append(
            pl.BlockSpec(
                (SEG, width), lambda i, given, own, *_: (own[jnp.maximum(i - before, 0)], 0)
            )
        )
        steps = steps + slots
        none = jnp.full((len(slots) - capacity,), -1, jnp.int32)
        given = jnp.concatenate([given, segs[0], none])
        own = (me ^ jnp.array([k for k, _ in slots], jnp.int32)) * capacity + jnp.array(
            [j for _, j in slots], jnp.int32
        )
    return pl.pallas_call(
        functools.partial(attend_kernel, segment, len(steps), firsts),
        out_shape=shapes,
        grid_spec=pltpu.PrefetchScalarGridSpec(
            num_scalar_prefetch=4,
            grid=(len(steps),),
            in_specs=[
                pl.BlockSpec(
                    (SEG, width),
                    lambda i, given, own, *_: (jnp.maximum(segment(i, given, own), 0), 0),
                ),
                pl.BlockSpec(memory_space=pl.ANY),
                pl.BlockSpec(memory_space=pl.ANY),
            ],
            out_specs=specs,
            scratch_shapes=[
                pltpu.VMEM((suffix_rows + MAXB * BLK, columns), suffix.dtype),
                pltpu.VMEM((SEG, width), queries.dtype),
                pltpu.SemaphoreType.DMA((MAXB + 1,)),
            ],
        ),
        compiler_params=pltpu.CompilerParams(vmem_limit_bytes=56 * 2**20),
        cost_estimate=pl.CostEstimate(flops=0, bytes_accessed=SEG * width, transcendentals=0),
    )(given, own, table, blocks, queries, suffix, pool)


def put_kernel(start, rows_ref, old, o_ref):
    o_ref[...] = rows_ref[...]


def put(out, rows, start):
    width = out.shape[1]
    return pl.pallas_call(
        put_kernel,
        out_shape=jax.ShapeDtypeStruct(out.shape, out.dtype),
        grid_spec=pltpu.PrefetchScalarGridSpec(
            num_scalar_prefetch=1,
            grid=(rows.shape[0] // SEG,),
            in_specs=[
                pl.BlockSpec((SEG, width), lambda i, start: (i, 0)),
                pl.BlockSpec(memory_space=pl.ANY),
            ],
            out_specs=pl.BlockSpec((SEG, width), lambda i, start: (start[0] + i, 0)),
        ),
        input_output_aliases={2: 0},
        compiler_params=pltpu.CompilerParams(vmem_limit_bytes=4 * 2**20),
        cost_estimate=pl.CostEstimate(flops=0, bytes_accessed=SEG * width, transcendentals=0),
    )(start[None], rows, out)


def swap(rows, distance):
    size = lax.axis_size("replica")
    return lax.ppermute(rows, "replica", [(i, i ^ distance) for i in range(size)])


def swap_some(out, rows, distance, start, segments):
    def branch(count):
        def run(out, rows):
            if count == 0:
                return out
            return put(out, swap(rows[: count * SEG], distance), start)

        return run

    return lax.switch(segments, [branch(c) for c in range(rows.shape[0] // SEG + 1)], out, rows)


def body(queries, suffix_cache, cache_pool, block_table, prefix_blocks, segment_owner):
    replicas = lax.axis_size("replica")
    me = lax.axis_index("replica").astype(jnp.int32)
    capacity = max(2, 2 * SEGS // replicas)
    base = SEGS // replicas
    owner = segment_owner[:, 0]
    far = list(range(replicas - 1, 0, -1))
    if replicas == 4:
        calls = [[(3, 0, 2)], [(2, 0, 4), (3, 2, 4)], [(1, 0, 4)]]
    else:
        calls = [[(k, 0, base) for k in far], []]

    def slots_of(k, a, b):
        return [(k, j) for j in range(a, b)]

    def run(groups, segs=None, placed=None):
        return attend(
            groups,
            segs,
            placed,
            me,
            owner,
            block_table[0],
            prefix_blocks,
            queries,
            suffix_cache,
            cache_pool,
        )

    def row_of(k, slot):
        return (me ^ k) * capacity + slot

    theirs = [swap(segment_owner, k) for k in range(1, replicas)]
    sent, segs = [], None
    for call in calls[:-1]:
        made = run([slots_of(*part) for part in call], segs)
        owner, made, theirs = lax.optimization_barrier((owner, made, theirs))
        if segs is None:
            segs = segment_table(me, owner, replicas, capacity)
        else:
            segs, made = lax.optimization_barrier((segs, made))
        sent.append([(swap(rows, k), row_of(k, a)) for (k, a, _), rows in zip(call, made)])
    segs, sent[0] = lax.optimization_barrier((segs, sent[0]))
    *rest, out = run(
        [slots_of(*part) for part in calls[-1]] + [slots_of(k, base, capacity) for k in far],
        segs,
        (
            slots_of(0, 0, capacity) + [s for k in far for s in slots_of(k, base, capacity)],
            capacity,
            replicas * capacity * SEG,
        ),
    )
    last = [(swap(rows, k), row_of(k, a)) for (k, a, _), rows in zip(calls[-1], rest)]
    rest = rest[len(last) :]
    distances = jnp.arange(1, replicas, dtype=jnp.int32)
    mine = jnp.sum((owner[None, :] == (me ^ distances)[:, None]).astype(jnp.int32), axis=1)
    given = jnp.sum((jnp.concatenate(theirs, axis=1) == me).astype(jnp.int32), axis=0)
    extra = jnp.clip(jnp.maximum(mine, given) - base, 0, capacity - base)
    before = sent[0] + [s for part in sent[1:] for s in part[:1]]
    after = [s for part in sent[1:] for s in part[1:]] + last
    for rows, start in before:
        out = put(out, rows, start)
    for k, rows in reversed(list(zip(far, rest))):
        out = swap_some(out, rows, k, row_of(k, base), extra[k - 1])
    for rows, start in after:
        out = put(out, rows, start)
    return out


def solution(mesh):
    in_specs = (
        P(("groups", "replica"), "tensor"),
        P(("groups", "replica"), "tensor"),
        P(("groups", "replica"), "tensor"),
        P(("groups", "replica"), None),
        P(("groups", "replica")),
        P(("groups", "replica"), None),
    )
    out_specs = P(("groups", "replica"), "tensor")
    return jax.shard_map(body, mesh=mesh, in_specs=in_specs, out_specs=out_specs, check_vma=False)
```

```python
import functools

import jax
import jax.numpy as jnp
from jax import lax
from jax.experimental import pallas as pl
from jax.experimental.pallas import tpu as pltpu
from jax.sharding import PartitionSpec as P

HEAD_DIM = 128
BLK = 256
MAXB = 4
SEGS = 16
SEG = 64
SCALE = HEAD_DIM ** (-0.5)
LOWEST = -1e38
HEADS_AT_ONCE = 4


def attend_kernel(
    groups, zeros, capacity, me, owner, table, blocks, queries, suffix, pool, *refs
):
    outs, (cache, q_all, o_all, blank, segs, used, todo, place, sems, out_sems, zero_sems) = (
        refs[:-11],
        refs[-11:],
    )
    suffix_rows = suffix.shape[0]
    heads = queries.shape[1] // HEAD_DIM
    group = heads // (suffix.shape[1] // (2 * HEAD_DIM))
    at_once = min(HEADS_AT_ONCE, group)
    rows = at_once * SEG
    prefix = MAXB * BLK

    copies = [pltpu.make_async_copy(suffix, cache.at[pl.ds(prefix, suffix_rows)], sems.at[SEGS])]
    for b in range(MAXB):
        start = pl.multiple_of(table[b] * BLK, BLK)
        to = pl.multiple_of((b + MAXB - blocks[0]) % MAXB * BLK, BLK)
        copies.append(
            pltpu.make_async_copy(
                pool.at[pl.ds(start, BLK)], cache.at[pl.ds(to, BLK)], sems.at[SEGS + 1 + b]
            )
        )
    for copy in copies:
        copy.start()

    @pl.loop(0, segs.shape[0])
    def _(i):
        segs[i] = jnp.int32(-1)

    @pl.loop(0, used.shape[0])
    def _(i):
        used[i] = jnp.int32(0)

    @pl.loop(0, SEGS)
    def _(i):
        distance = owner[i] ^ me[0]
        slot = used[distance]
        used[distance] = slot + 1
        segs[distance * capacity + slot] = i

    def rows_of(ref, seg):
        return ref.at[pl.ds(pl.multiple_of(seg * SEG, SEG), SEG)]

    def fetch(seg):
        return pltpu.make_async_copy(rows_of(queries, seg), rows_of(q_all, seg), sems.at[seg])

    def hand(out, at, seg):
        return pltpu.make_async_copy(rows_of(o_all, seg), rows_of(out, at), out_sems.at[seg])

    def clear(out, at, i):
        return pltpu.make_async_copy(blank, rows_of(out, at), zero_sems.at[i])

    def at_of(distance, slot):
        return (me[0] ^ distance) * capacity + slot

    blank[...] = jnp.zeros_like(blank)
    firsts, found, slots = [], jnp.int32(0), 0
    for out, (distance, first, count, before) in zip(outs, groups):
        firsts.append(slots)

        def look(j, found):
            seg = segs[distance * capacity + first + j]
            at = at_of(distance, first + j) if before is None else before + j

            @pl.when(seg >= 0)
            def _():
                fetch(seg).start()
                todo[found] = seg
                place[found] = slots + j

            @pl.when(seg < 0)
            def _():
                clear(out, at, slots + j).start()

            return jnp.where(seg >= 0, found + 1, found)

        found = lax.fori_loop(0, count, look, found)
        slots += count
    blanks = slots
    for distance, first, count in zeros:
        for j in range(count):
            clear(outs[-1], at_of(distance, first + j), blanks + j).start()
        blanks += count
    for copy in copies:
        copy.wait()

    def attend_rows(seg, count, i):
        first = i * at_once
        low = pl.multiple_of((MAXB - blocks[0]) * BLK, BLK)
        pair = first // group * (2 * HEAD_DIM)

        def column(h):
            return pl.ds(pl.multiple_of((first + h) * HEAD_DIM, HEAD_DIM), HEAD_DIM)

        def cached(offset):
            lanes = pl.ds(pl.multiple_of(pair + offset, HEAD_DIM), HEAD_DIM)
            return cache[pl.ds(low, count * BLK), lanes]

        here = pl.ds(pl.multiple_of(seg * SEG, SEG), SEG)
        q = jnp.concatenate([q_all[here, column(h)] for h in range(at_once)], axis=0)
        s = lax.dot_general(
            q, cached(0), (((1,), (1,)), ((), ())), preferred_element_type=jnp.float32
        )
        parts = [s[:, c : c + HEAD_DIM] for c in range(0, count * BLK, HEAD_DIM)]
        token = lax.broadcasted_iota(jnp.int32, (rows, HEAD_DIM), 0) % SEG + seg * SEG % BLK
        key = lax.broadcasted_iota(jnp.int32, (rows, HEAD_DIM), 1)
        masked = BLK // HEAD_DIM
        for c in range(masked):
            at = len(parts) - masked + c
            parts[at] = jnp.where(key + c * HEAD_DIM <= token, parts[at], LOWEST)
        top = jnp.max(functools.reduce(jnp.maximum, parts), axis=-1, keepdims=True)
        top = jnp.broadcast_to(top, (rows, HEAD_DIM))
        weights = [jnp.exp((part - top) * SCALE) for part in parts]
        total = jnp.sum(functools.reduce(jnp.add, weights), axis=-1, keepdims=True)
        mixed = jnp.dot(
            jnp.concatenate([w.astype(jnp.bfloat16) for w in weights], axis=1),
            cached(HEAD_DIM),
            preferred_element_type=jnp.float32,
        )
        out = (mixed / total).astype(o_all.dtype)
        for h in range(at_once):
            o_all[here, column(h)] = out[h * SEG : (h + 1) * SEG]

    @pl.loop(0, found)
    def _(t):
        seg = todo[t]
        fetch(seg).wait()
        blocks_seen = blocks[0] + seg * SEG // BLK + 1
        for count in range(2, MAXB + suffix_rows // BLK + 1):

            @pl.when(blocks_seen == count)
            def _():
                @pl.loop(0, heads // at_once)
                def _(i):
                    attend_rows(seg, count, i)

        to = place[t]
        for out, first, (distance, slot, count, before) in zip(outs, firsts, groups):
            j = to - first

            @pl.when((j >= 0) & (j < count))
            def _():
                at = at_of(distance, slot + j) if before is None else before + j
                hand(out, at, seg).start()

    @pl.loop(0, found)
    def _(t):
        hand(outs[0], 0, todo[t]).wait()

    first = 0
    for distance, slot, count, _ in groups:

        @pl.loop(0, count)
        def _(j):
            @pl.when(segs[distance * capacity + slot + j] < 0)
            def _():
                clear(outs[0], 0, first + j).wait()

        first += count
    for i in range(slots, blanks):
        clear(outs[0], 0, i).wait()


def attend(groups, whole, capacity, me, owner, table, blocks, queries, suffix, pool):
    replicas = lax.axis_size("replica")
    width = queries.shape[1]
    suffix_rows, columns = suffix.shape
    held = [(k, a, b - a, 0) for k, a, b in groups]
    sizes = [(b - a) * SEG for _, a, b in groups]
    zeros = []
    if whole:
        held.append((0, 0, capacity, None))
        sizes.append(replicas * capacity * SEG)
        zeros = [(k, a, b - a) for k, a, b in whole]
    slots = sum(g[2] for g in held) + sum(z[2] for z in zeros)
    return pl.pallas_call(
        functools.partial(attend_kernel, held, zeros, capacity),
        out_shape=[jax.ShapeDtypeStruct((size, width), queries.dtype) for size in sizes],
        grid_spec=pltpu.PrefetchScalarGridSpec(
            num_scalar_prefetch=4,
            grid=(),
            in_specs=[pl.BlockSpec(memory_space=pl.ANY)] * 3,
            out_specs=[pl.BlockSpec(memory_space=pl.ANY)] * len(sizes),
            scratch_shapes=[
                pltpu.VMEM((suffix_rows + MAXB * BLK, columns), suffix.dtype),
                pltpu.VMEM(queries.shape, queries.dtype),
                pltpu.VMEM(queries.shape, queries.dtype),
                pltpu.VMEM((SEG, width), queries.dtype),
                pltpu.SMEM((replicas * capacity,), jnp.int32),
                pltpu.SMEM((replicas,), jnp.int32),
                pltpu.SMEM((SEGS,), jnp.int32),
                pltpu.SMEM((SEGS,), jnp.int32),
                pltpu.SemaphoreType.DMA((SEGS + MAXB + 1,)),
                pltpu.SemaphoreType.DMA((SEGS,)),
                pltpu.SemaphoreType.DMA((slots,)),
            ],
        ),
        compiler_params=pltpu.CompilerParams(vmem_limit_bytes=56 * 2**20),
        cost_estimate=pl.CostEstimate(flops=0, bytes_accessed=SEG * width, transcendentals=0),
    )(me[None], owner, table, blocks, queries, suffix, pool)


def put_kernel(start, rows_ref, old, o_ref):
    o_ref[...] = rows_ref[...]


def put(out, rows, start):
    width = out.shape[1]
    return pl.pallas_call(
        put_kernel,
        out_shape=jax.ShapeDtypeStruct(out.shape, out.dtype),
        grid_spec=pltpu.PrefetchScalarGridSpec(
            num_scalar_prefetch=1,
            grid=(rows.shape[0] // SEG,),
            in_specs=[
                pl.BlockSpec((SEG, width), lambda i, start: (i, 0)),
                pl.BlockSpec(memory_space=pl.ANY),
            ],
            out_specs=pl.BlockSpec((SEG, width), lambda i, start: (start[0] + i, 0)),
        ),
        input_output_aliases={2: 0},
        compiler_params=pltpu.CompilerParams(vmem_limit_bytes=4 * 2**20),
        cost_estimate=pl.CostEstimate(flops=0, bytes_accessed=SEG * width, transcendentals=0),
    )(start[None], rows, out)


def swap(rows, distance):
    size = lax.axis_size("replica")
    return lax.ppermute(rows, "replica", [(i, i ^ distance) for i in range(size)])


def swap_some(out, rows, distance, start, segments):
    def branch(count):
        def run(out, rows):
            if count == 0:
                return out
            return put(out, swap(rows[: count * SEG], distance), start)

        return run

    return lax.switch(segments, [branch(c) for c in range(rows.shape[0] // SEG + 1)], out, rows)


def body(queries, suffix_cache, cache_pool, block_table, prefix_blocks, segment_owner):
    replicas = lax.axis_size("replica")
    me = lax.axis_index("replica").astype(jnp.int32)
    capacity = max(2, 2 * SEGS // replicas)
    base = SEGS // replicas
    owner = segment_owner[:, 0]
    far = list(range(replicas - 1, 0, -1))
    if replicas == 4:
        calls = [[(3, 0, 2)], [(2, 0, 4), (3, 2, 4)], [(1, 0, 4)]]
    else:
        calls = [[(k, 0, base) for k in far], []]

    def run(groups, whole=()):
        return attend(
            groups,
            whole,
            capacity,
            me,
            owner,
            block_table[0],
            prefix_blocks,
            queries,
            suffix_cache,
            cache_pool,
        )

    def row_of(k, slot):
        return (me ^ k) * capacity + slot

    theirs = [swap(segment_owner, k) for k in range(1, replicas)]
    sent = []
    for call in calls[:-1]:
        made = run(call)
        owner, made, theirs = lax.optimization_barrier((owner, made, theirs))
        sent.append([(swap(rows, k), row_of(k, a)) for (k, a, _), rows in zip(call, made)])
    owner, sent[0] = lax.optimization_barrier((owner, sent[0]))
    over = [(k, base, capacity) for k in far]
    *rest, out = run(calls[-1] + over, over)
    last = [(swap(rows, k), row_of(k, a)) for (k, a, _), rows in zip(calls[-1], rest)]
    rest = rest[len(last) :]
    distances = jnp.arange(1, replicas, dtype=jnp.int32)
    mine = jnp.sum((owner[None, :] == (me ^ distances)[:, None]).astype(jnp.int32), axis=1)
    given = jnp.sum((jnp.concatenate(theirs, axis=1) == me).astype(jnp.int32), axis=0)
    extra = jnp.clip(jnp.maximum(mine, given) - base, 0, capacity - base)
    before = sent[0] + [s for part in sent[1:] for s in part[:1]]
    after = [s for part in sent[1:] for s in part[1:]] + last
    for rows, start in before:
        out = put(out, rows, start)
    for k, rows in reversed(list(zip(far, rest))):
        out = swap_some(out, rows, k, row_of(k, base), extra[k - 1])
    for rows, start in after:
        out = put(out, rows, start)
    return out


def solution(mesh):
    in_specs = (
        P(("groups", "replica"), "tensor"),
        P(("groups", "replica"), "tensor"),
        P(("groups", "replica"), "tensor"),
        P(("groups", "replica"), None),
        P(("groups", "replica")),
        P(("groups", "replica"), None),
    )
    out_specs = P(("groups", "replica"), "tensor")
    return jax.shard_map(body, mesh=mesh, in_specs=in_specs, out_specs=out_specs, check_vma=False)
```

```python
import functools

import jax
import jax.numpy as jnp
from jax import lax
from jax.experimental import pallas as pl
from jax.experimental.pallas import tpu as pltpu
from jax.sharding import PartitionSpec as P

HEAD_DIM = 128
BLK = 256
MAXB = 4
SEGS = 16
SEG = 64
SCALE = HEAD_DIM ** (-0.5)
LOWEST = -1e38
HEADS_AT_ONCE = 8


def attend_kernel(
    groups, zeros, capacity, me, owner, table, blocks, queries, suffix, pool, *refs
):
    outs, (cache, q_all, o_all, blank, segs, used, todo, place, sems, out_sems, zero_sems) = (
        refs[:-11],
        refs[-11:],
    )
    suffix_rows = suffix.shape[0]
    heads = queries.shape[1] // HEAD_DIM
    group = heads // (suffix.shape[1] // (2 * HEAD_DIM))
    at_once = min(HEADS_AT_ONCE, group)
    rows = at_once * SEG
    prefix = MAXB * BLK

    copies = [pltpu.make_async_copy(suffix, cache.at[pl.ds(prefix, suffix_rows)], sems.at[SEGS])]
    for b in range(MAXB):
        start = pl.multiple_of(table[b] * BLK, BLK)
        to = pl.multiple_of((b + MAXB - blocks[0]) % MAXB * BLK, BLK)
        copies.append(
            pltpu.make_async_copy(
                pool.at[pl.ds(start, BLK)], cache.at[pl.ds(to, BLK)], sems.at[SEGS + 1 + b]
            )
        )
    for copy in copies:
        copy.start()

    @pl.loop(0, segs.shape[0])
    def _(i):
        segs[i] = jnp.int32(-1)

    @pl.loop(0, used.shape[0])
    def _(i):
        used[i] = jnp.int32(0)

    @pl.loop(0, SEGS)
    def _(i):
        distance = owner[i] ^ me[0]
        slot = used[distance]
        used[distance] = slot + 1
        segs[distance * capacity + slot] = i

    def rows_of(ref, seg):
        return ref.at[pl.ds(pl.multiple_of(seg * SEG, SEG), SEG)]

    def fetch(seg):
        return pltpu.make_async_copy(rows_of(queries, seg), rows_of(q_all, seg), sems.at[seg])

    def hand(out, at, seg):
        return pltpu.make_async_copy(rows_of(o_all, seg), rows_of(out, at), out_sems.at[seg])

    def clear(out, at, i):
        return pltpu.make_async_copy(blank, rows_of(out, at), zero_sems.at[i])

    def at_of(distance, slot):
        return (me[0] ^ distance) * capacity + slot

    blank[...] = jnp.zeros_like(blank)
    firsts, found, slots = [], jnp.int32(0), 0
    for out, (distance, first, count, before) in zip(outs, groups):
        firsts.append(slots)

        def look(j, found):
            seg = segs[distance * capacity + first + j]
            at = at_of(distance, first + j) if before is None else before + j

            @pl.when(seg >= 0)
            def _():
                fetch(seg).start()
                todo[found] = seg
                place[found] = slots + j

            @pl.when(seg < 0)
            def _():
                clear(out, at, slots + j).start()

            return jnp.where(seg >= 0, found + 1, found)

        found = lax.fori_loop(0, count, look, found)
        slots += count
    blanks = slots
    for distance, first, count in zeros:
        for j in range(count):
            clear(outs[-1], at_of(distance, first + j), blanks + j).start()
        blanks += count
    for copy in copies:
        copy.wait()

    def attend_rows(seg, count, i):
        first = i * at_once
        low = pl.multiple_of((MAXB - blocks[0]) * BLK, BLK)
        pair = first // group * (2 * HEAD_DIM)

        def column(h):
            return pl.ds(pl.multiple_of((first + h) * HEAD_DIM, HEAD_DIM), HEAD_DIM)

        def cached(offset):
            lanes = pl.ds(pl.multiple_of(pair + offset, HEAD_DIM), HEAD_DIM)
            return cache[pl.ds(low, count * BLK), lanes]

        here = pl.ds(pl.multiple_of(seg * SEG, SEG), SEG)
        q = jnp.concatenate([q_all[here, column(h)] for h in range(at_once)], axis=0)
        s = lax.dot_general(
            q, cached(0), (((1,), (1,)), ((), ())), preferred_element_type=jnp.float32
        )
        parts = [s[:, c : c + HEAD_DIM] for c in range(0, count * BLK, HEAD_DIM)]
        token = lax.broadcasted_iota(jnp.int32, (rows, HEAD_DIM), 0) % SEG + seg * SEG % BLK
        key = lax.broadcasted_iota(jnp.int32, (rows, HEAD_DIM), 1)
        masked = BLK // HEAD_DIM
        for c in range(masked):
            at = len(parts) - masked + c
            parts[at] = jnp.where(key + c * HEAD_DIM <= token, parts[at], LOWEST)
        top = jnp.max(functools.reduce(jnp.maximum, parts), axis=-1, keepdims=True)
        top = jnp.broadcast_to(top, (rows, HEAD_DIM))
        weights = [jnp.exp((part - top) * SCALE) for part in parts]
        total = jnp.sum(functools.reduce(jnp.add, weights), axis=-1, keepdims=True)
        mixed = jnp.dot(
            jnp.concatenate([w.astype(jnp.bfloat16) for w in weights], axis=1),
            cached(HEAD_DIM),
            preferred_element_type=jnp.float32,
        )
        out = (mixed / total).astype(o_all.dtype)
        for h in range(at_once):
            o_all[here, column(h)] = out[h * SEG : (h + 1) * SEG]

    @pl.loop(0, found)
    def _(t):
        seg = todo[t]
        fetch(seg).wait()
        blocks_seen = blocks[0] + seg * SEG // BLK + 1
        for count in range(2, MAXB + suffix_rows // BLK + 1):

            @pl.when(blocks_seen == count)
            def _():
                @pl.loop(0, heads // at_once)
                def _(i):
                    attend_rows(seg, count, i)

        to = place[t]
        for out, first, (distance, slot, count, before) in zip(outs, firsts, groups):
            j = to - first

            @pl.when((j >= 0) & (j < count))
            def _():
                at = at_of(distance, slot + j) if before is None else before + j
                hand(out, at, seg).start()

    @pl.loop(0, found)
    def _(t):
        hand(outs[0], 0, todo[t]).wait()

    first = 0
    for distance, slot, count, _ in groups:

        @pl.loop(0, count)
        def _(j):
            @pl.when(segs[distance * capacity + slot + j] < 0)
            def _():
                clear(outs[0], 0, first + j).wait()

        first += count
    for i in range(slots, blanks):
        clear(outs[0], 0, i).wait()


def attend(groups, whole, capacity, me, owner, table, blocks, queries, suffix, pool):
    replicas = lax.axis_size("replica")
    width = queries.shape[1]
    suffix_rows, columns = suffix.shape
    held = [(k, a, b - a, 0) for k, a, b in groups]
    sizes = [(b - a) * SEG for _, a, b in groups]
    zeros = []
    if whole:
        held.append((0, 0, capacity, None))
        sizes.append(replicas * capacity * SEG)
        zeros = [(k, a, b - a) for k, a, b in whole]
    slots = sum(g[2] for g in held) + sum(z[2] for z in zeros)
    return pl.pallas_call(
        functools.partial(attend_kernel, held, zeros, capacity),
        out_shape=[jax.ShapeDtypeStruct((size, width), queries.dtype) for size in sizes],
        grid_spec=pltpu.PrefetchScalarGridSpec(
            num_scalar_prefetch=4,
            grid=(),
            in_specs=[pl.BlockSpec(memory_space=pl.ANY)] * 3,
            out_specs=[pl.BlockSpec(memory_space=pl.ANY)] * len(sizes),
            scratch_shapes=[
                pltpu.VMEM((suffix_rows + MAXB * BLK, columns), suffix.dtype),
                pltpu.VMEM(queries.shape, queries.dtype),
                pltpu.VMEM(queries.shape, queries.dtype),
                pltpu.VMEM((SEG, width), queries.dtype),
                pltpu.SMEM((replicas * capacity,), jnp.int32),
                pltpu.SMEM((replicas,), jnp.int32),
                pltpu.SMEM((SEGS,), jnp.int32),
                pltpu.SMEM((SEGS,), jnp.int32),
                pltpu.SemaphoreType.DMA((SEGS + MAXB + 1,)),
                pltpu.SemaphoreType.DMA((SEGS,)),
                pltpu.SemaphoreType.DMA((slots,)),
            ],
        ),
        compiler_params=pltpu.CompilerParams(vmem_limit_bytes=56 * 2**20),
        cost_estimate=pl.CostEstimate(flops=0, bytes_accessed=SEG * width, transcendentals=0),
    )(me[None], owner, table, blocks, queries, suffix, pool)


def put_kernel(start, rows_ref, old, o_ref):
    o_ref[...] = rows_ref[...]


def put(out, rows, start):
    width = out.shape[1]
    return pl.pallas_call(
        put_kernel,
        out_shape=jax.ShapeDtypeStruct(out.shape, out.dtype),
        grid_spec=pltpu.PrefetchScalarGridSpec(
            num_scalar_prefetch=1,
            grid=(rows.shape[0] // SEG,),
            in_specs=[
                pl.BlockSpec((SEG, width), lambda i, start: (i, 0)),
                pl.BlockSpec(memory_space=pl.ANY),
            ],
            out_specs=pl.BlockSpec((SEG, width), lambda i, start: (start[0] + i, 0)),
        ),
        input_output_aliases={2: 0},
        compiler_params=pltpu.CompilerParams(vmem_limit_bytes=4 * 2**20),
        cost_estimate=pl.CostEstimate(flops=0, bytes_accessed=SEG * width, transcendentals=0),
    )(start[None], rows, out)


def swap(rows, distance):
    size = lax.axis_size("replica")
    return lax.ppermute(rows, "replica", [(i, i ^ distance) for i in range(size)])


def swap_some(out, rows, distance, start, segments):
    def branch(count):
        def run(out, rows):
            if count == 0:
                return out
            return put(out, swap(rows[: count * SEG], distance), start)

        return run

    return lax.switch(segments, [branch(c) for c in range(rows.shape[0] // SEG + 1)], out, rows)


def body(queries, suffix_cache, cache_pool, block_table, prefix_blocks, segment_owner):
    replicas = lax.axis_size("replica")
    me = lax.axis_index("replica").astype(jnp.int32)
    capacity = max(2, 2 * SEGS // replicas)
    base = SEGS // replicas
    owner = segment_owner[:, 0]
    far = list(range(replicas - 1, 0, -1))
    if replicas == 4:
        calls = [[(3, 0, 2)], [(2, 0, 4), (3, 2, 4)], [(1, 0, 4)]]
    else:
        calls = [[(k, 0, base) for k in far], []]

    def run(groups, whole=()):
        return attend(
            groups,
            whole,
            capacity,
            me,
            owner,
            block_table[0],
            prefix_blocks,
            queries,
            suffix_cache,
            cache_pool,
        )

    def row_of(k, slot):
        return (me ^ k) * capacity + slot

    spread = lax.optimization_barrier(jnp.pad(owner[None, :], ((0, 7), (0, 128 - SEGS))))
    owners = lax.optimization_barrier(lax.all_gather(spread, "replica"))
    sent = []
    for call in calls[:-1]:
        made = run(call)
        owner, made = lax.optimization_barrier((owner, made))
        sent.append([(swap(rows, k), row_of(k, a)) for (k, a, _), rows in zip(call, made)])
    owner, owners, sent[0] = lax.optimization_barrier((owner, owners, sent[0]))
    over = [(k, base, capacity) for k in far]
    *rest, out = run(calls[-1] + over, over)
    last = [(swap(rows, k), row_of(k, a)) for (k, a, _), rows in zip(calls[-1], rest)]
    rest = rest[len(last) :]
    every = jnp.arange(replicas, dtype=jnp.int32)
    far_off = jnp.arange(1, replicas, dtype=jnp.int32)
    mine = jnp.sum((owner[None, :] == (me ^ far_off)[:, None]).astype(jnp.int32), axis=1)
    here = jnp.sum((owners[:, 0, :SEGS] == me).astype(jnp.int32), axis=1)
    given = jnp.sum(jnp.where((me ^ far_off)[:, None] == every[None, :], here[None, :], 0), axis=1)
    extra = jnp.clip(jnp.maximum(mine, given) - base, 0, capacity - base)
    before = sent[0] + [s for part in sent[1:] for s in part[:1]]
    after = [s for part in sent[1:] for s in part[1:]] + last
    for rows, start in before:
        out = put(out, rows, start)
    for k, rows in reversed(list(zip(far, rest))):
        out = swap_some(out, rows, k, row_of(k, base), extra[k - 1])
    for rows, start in after:
        out = put(out, rows, start)
    return out


def solution(mesh):
    in_specs = (
        P(("groups", "replica"), "tensor"),
        P(("groups", "replica"), "tensor"),
        P(("groups", "replica"), "tensor"),
        P(("groups", "replica"), None),
        P(("groups", "replica")),
        P(("groups", "replica"), None),
    )
    out_specs = P(("groups", "replica"), "tensor")
    return jax.shard_map(body, mesh=mesh, in_specs=in_specs, out_specs=out_specs, check_vma=False)
```

```python
import functools

import jax
import jax.numpy as jnp
from jax import lax
from jax.experimental import pallas as pl
from jax.experimental.pallas import tpu as pltpu
from jax.sharding import PartitionSpec as P

HEAD_DIM = 128
BLK = 256
MAXB = 4
SEGS = 16
SEG = 64
SCALE = HEAD_DIM ** (-0.5)
LOWEST = -1e38
HEADS_AT_ONCE = 4


def attend_kernel(
    groups, zeros, capacity, me, owner, table, blocks, queries, suffix, pool, *refs
):
    outs, (cache, q_all, o_all, blank, segs, used, todo, place, sems, out_sems, zero_sems) = (
        refs[:-11],
        refs[-11:],
    )
    suffix_rows = suffix.shape[0]
    heads = queries.shape[1] // HEAD_DIM
    kv_heads = suffix.shape[1] // (2 * HEAD_DIM)
    group = heads // kv_heads
    at_once = min(HEADS_AT_ONCE, group)
    rows = at_once * SEG
    prefix = MAXB * BLK

    copies = []
    for g in range(kv_heads):
        both = pl.ds(2 * g * HEAD_DIM, 2 * HEAD_DIM)
        to_both = pl.ds(3 * g * HEAD_DIM, 2 * HEAD_DIM)
        at = g * (MAXB + 1)
        copies.append(
            pltpu.make_async_copy(
                suffix.at[:, both],
                cache.at[pl.ds(prefix, suffix_rows), to_both],
                sems.at[SEGS + at],
            )
        )
        for b in range(MAXB):
            start = pl.multiple_of(table[b] * BLK, BLK)
            to = pl.multiple_of((b + MAXB - blocks[0]) % MAXB * BLK, BLK)
            copies.append(
                pltpu.make_async_copy(
                    pool.at[pl.ds(start, BLK), both],
                    cache.at[pl.ds(to, BLK), to_both],
                    sems.at[SEGS + at + 1 + b],
                )
            )
    for copy in copies:
        copy.start()

    @pl.loop(0, segs.shape[0])
    def _(i):
        segs[i] = jnp.int32(-1)

    @pl.loop(0, used.shape[0])
    def _(i):
        used[i] = jnp.int32(0)

    @pl.loop(0, SEGS)
    def _(i):
        distance = owner[i] ^ me[0]
        slot = used[distance]
        used[distance] = slot + 1
        segs[distance * capacity + slot] = i

    def rows_of(ref, seg):
        return ref.at[pl.ds(pl.multiple_of(seg * SEG, SEG), SEG)]

    def fetch(seg):
        return pltpu.make_async_copy(rows_of(queries, seg), rows_of(q_all, seg), sems.at[seg])

    def hand(out, at, seg):
        return pltpu.make_async_copy(rows_of(o_all, seg), rows_of(out, at), out_sems.at[seg])

    def clear(out, at, i):
        return pltpu.make_async_copy(blank, rows_of(out, at), zero_sems.at[i])

    def at_of(distance, slot):
        return (me[0] ^ distance) * capacity + slot

    blank[...] = jnp.zeros_like(blank)
    for g in range(kv_heads):
        ones = pl.ds((3 * g + 2) * HEAD_DIM, HEAD_DIM)
        cache[:, ones] = jnp.ones((cache.shape[0], HEAD_DIM), cache.dtype)
    firsts, found, slots = [], jnp.int32(0), 0
    for out, (distance, first, count, before) in zip(outs, groups):
        firsts.append(slots)

        def look(j, found):
            seg = segs[distance * capacity + first + j]
            at = at_of(distance, first + j) if before is None else before + j

            @pl.when(seg >= 0)
            def _():
                fetch(seg).start()
                todo[found] = seg
                place[found] = slots + j

            @pl.when(seg < 0)
            def _():
                clear(out, at, slots + j).start()

            return jnp.where(seg >= 0, found + 1, found)

        found = lax.fori_loop(0, count, look, found)
        slots += count
    blanks = slots
    for distance, first, count in zeros:
        for j in range(count):
            clear(outs[-1], at_of(distance, first + j), blanks + j).start()
        blanks += count
    for copy in copies:
        copy.wait()

    def attend_rows(seg, count, i):
        first = i * at_once
        low = pl.multiple_of((MAXB - blocks[0]) * BLK, BLK)
        triple = first // group * (3 * HEAD_DIM)

        def column(h):
            return pl.ds(pl.multiple_of((first + h) * HEAD_DIM, HEAD_DIM), HEAD_DIM)

        def cached(offset, width):
            lanes = pl.ds(pl.multiple_of(triple + offset, HEAD_DIM), width)
            return cache[pl.ds(low, count * BLK), lanes]

        here = pl.ds(pl.multiple_of(seg * SEG, SEG), SEG)
        q = jnp.concatenate([q_all[here, column(h)] for h in range(at_once)], axis=0)
        s = lax.dot_general(
            q, cached(0, HEAD_DIM), (((1,), (1,)), ((), ())), preferred_element_type=jnp.float32
        )
        parts = [s[:, c : c + HEAD_DIM] for c in range(0, count * BLK, HEAD_DIM)]
        token = lax.broadcasted_iota(jnp.int32, (rows, HEAD_DIM), 0) % SEG + seg * SEG % BLK
        key = lax.broadcasted_iota(jnp.int32, (rows, HEAD_DIM), 1)
        masked = BLK // HEAD_DIM
        for c in range(masked):
            at = len(parts) - masked + c
            parts[at] = jnp.where(key + c * HEAD_DIM <= token, parts[at], LOWEST)
        top = jnp.max(functools.reduce(jnp.maximum, parts), axis=-1, keepdims=True)
        top = jnp.broadcast_to(top, (rows, HEAD_DIM))
        weights = [jnp.exp((part - top) * SCALE) for part in parts]
        mixed = jnp.dot(
            jnp.concatenate([w.astype(jnp.bfloat16) for w in weights], axis=1),
            cached(HEAD_DIM, 2 * HEAD_DIM),
            preferred_element_type=jnp.float32,
        )
        out = (mixed[:, :HEAD_DIM] / mixed[:, HEAD_DIM:]).astype(o_all.dtype)
        for h in range(at_once):
            o_all[here, column(h)] = out[h * SEG : (h + 1) * SEG]

    @pl.loop(0, found)
    def _(t):
        seg = todo[t]
        fetch(seg).wait()
        blocks_seen = blocks[0] + seg * SEG // BLK + 1
        for count in range(2, MAXB + suffix_rows // BLK + 1):

            @pl.when(blocks_seen == count)
            def _():
                @pl.loop(0, heads // at_once)
                def _(i):
                    attend_rows(seg, count, i)

        to = place[t]
        for out, first, (distance, slot, count, before) in zip(outs, firsts, groups):
            j = to - first

            @pl.when((j >= 0) & (j < count))
            def _():
                at = at_of(distance, slot + j) if before is None else before + j
                hand(out, at, seg).start()

    @pl.loop(0, found)
    def _(t):
        hand(outs[0], 0, todo[t]).wait()

    first = 0
    for distance, slot, count, _ in groups:

        @pl.loop(0, count)
        def _(j):
            @pl.when(segs[distance * capacity + slot + j] < 0)
            def _():
                clear(outs[0], 0, first + j).wait()

        first += count
    for i in range(slots, blanks):
        clear(outs[0], 0, i).wait()


def attend(groups, whole, capacity, me, owner, table, blocks, queries, suffix, pool):
    replicas = lax.axis_size("replica")
    width = queries.shape[1]
    suffix_rows, columns = suffix.shape
    held = [(k, a, b - a, 0) for k, a, b in groups]
    sizes = [(b - a) * SEG for _, a, b in groups]
    zeros = []
    if whole:
        held.append((0, 0, capacity, None))
        sizes.append(replicas * capacity * SEG)
        zeros = [(k, a, b - a) for k, a, b in whole]
    slots = sum(g[2] for g in held) + sum(z[2] for z in zeros)
    return pl.pallas_call(
        functools.partial(attend_kernel, held, zeros, capacity),
        out_shape=[jax.ShapeDtypeStruct((size, width), queries.dtype) for size in sizes],
        grid_spec=pltpu.PrefetchScalarGridSpec(
            num_scalar_prefetch=4,
            grid=(),
            in_specs=[pl.BlockSpec(memory_space=pl.ANY)] * 3,
            out_specs=[pl.BlockSpec(memory_space=pl.ANY)] * len(sizes),
            scratch_shapes=[
                pltpu.VMEM((suffix_rows + MAXB * BLK, columns // 2 * 3), suffix.dtype),
                pltpu.VMEM(queries.shape, queries.dtype),
                pltpu.VMEM(queries.shape, queries.dtype),
                pltpu.VMEM((SEG, width), queries.dtype),
                pltpu.SMEM((replicas * capacity,), jnp.int32),
                pltpu.SMEM((replicas,), jnp.int32),
                pltpu.SMEM((SEGS,), jnp.int32),
                pltpu.SMEM((SEGS,), jnp.int32),
                pltpu.SemaphoreType.DMA((SEGS + columns // (2 * HEAD_DIM) * (MAXB + 1),)),
                pltpu.SemaphoreType.DMA((SEGS,)),
                pltpu.SemaphoreType.DMA((slots,)),
            ],
        ),
        compiler_params=pltpu.CompilerParams(vmem_limit_bytes=56 * 2**20),
        cost_estimate=pl.CostEstimate(flops=2**36, bytes_accessed=SEG * width, transcendentals=0),
    )(me[None], owner, table, blocks, queries, suffix, pool)


def put_kernel(start, rows_ref, old, o_ref):
    o_ref[...] = rows_ref[...]


def put(out, rows, start):
    width = out.shape[1]
    return pl.pallas_call(
        put_kernel,
        out_shape=jax.ShapeDtypeStruct(out.shape, out.dtype),
        grid_spec=pltpu.PrefetchScalarGridSpec(
            num_scalar_prefetch=1,
            grid=(rows.shape[0] // SEG,),
            in_specs=[
                pl.BlockSpec((SEG, width), lambda i, start: (i, 0)),
                pl.BlockSpec(memory_space=pl.ANY),
            ],
            out_specs=pl.BlockSpec((SEG, width), lambda i, start: (start[0] + i, 0)),
        ),
        input_output_aliases={2: 0},
        compiler_params=pltpu.CompilerParams(vmem_limit_bytes=4 * 2**20),
        cost_estimate=pl.CostEstimate(flops=0, bytes_accessed=SEG * width, transcendentals=0),
    )(start[None], rows, out)


def swap(rows, distance):
    size = lax.axis_size("replica")
    return lax.ppermute(rows, "replica", [(i, i ^ distance) for i in range(size)])


def swap_some(out, rows, distance, start, segments):
    def branch(count):
        def run(out, rows):
            if count == 0:
                return out
            return put(out, swap(rows[: count * SEG], distance), start)

        return run

    return lax.switch(segments, [branch(c) for c in range(rows.shape[0] // SEG + 1)], out, rows)


def body(queries, suffix_cache, cache_pool, block_table, prefix_blocks, segment_owner):
    replicas = lax.axis_size("replica")
    me = lax.axis_index("replica").astype(jnp.int32)
    capacity = max(2, 2 * SEGS // replicas)
    base = SEGS // replicas
    owner = segment_owner[:, 0]
    far = list(range(replicas - 1, 0, -1))
    if replicas == 4:
        calls = [[(3, 0, 1)], [(2, 0, 2)], [(2, 2, 4), (3, 1, 3)], [(3, 3, 4), (1, 0, 2), (1, 2, 4)]]
    else:
        calls = [[(k, 0, base) for k in far], []]

    def run(groups, whole=()):
        return attend(
            groups,
            whole,
            capacity,
            me,
            owner,
            block_table[0],
            prefix_blocks,
            queries,
            suffix_cache,
            cache_pool,
        )

    def row_of(k, slot):
        return (me ^ k) * capacity + slot

    sent = []
    for i, call in enumerate(calls[:-1]):
        if i >= 2:
            owner, sent[i - 2] = lax.optimization_barrier((owner, sent[i - 2]))
        made = run(call)
        owner, made = lax.optimization_barrier((owner, made))
        sent.append([(swap(rows, k), row_of(k, a)) for (k, a, _), rows in zip(call, made)])
        if i == min(1, len(calls) - 2):
            theirs = [swap(owner[:, None], k) for k in range(1, replicas)]
    settled = sent[-2] if len(sent) > 1 else sent[-1]
    owner, theirs, settled[:] = lax.optimization_barrier((owner, theirs, list(settled)))
    over = [(k, base, capacity) for k in far]
    *rest, out = run(calls[-1] + over, over)
    last = [(swap(rows, k), row_of(k, a)) for (k, a, _), rows in zip(calls[-1], rest)]
    rest = rest[len(last) :]
    distances = jnp.arange(1, replicas, dtype=jnp.int32)
    mine = jnp.sum((owner[None, :] == (me ^ distances)[:, None]).astype(jnp.int32), axis=1)
    given = jnp.sum((jnp.concatenate(theirs, axis=1) == me).astype(jnp.int32), axis=0)
    extra = jnp.clip(jnp.maximum(mine, given) - base, 0, capacity - base)
    before = sent[-1]
    after = [s for part in sent[:-1] for s in part] + last
    for rows, start in before:
        out = put(out, rows, start)
    for k, rows in reversed(list(zip(far, rest))):
        out = swap_some(out, rows, k, row_of(k, base), extra[k - 1])
    for rows, start in after:
        out = put(out, rows, start)
    return out


def solution(mesh):
    in_specs = (
        P(("groups", "replica"), "tensor"),
        P(("groups", "replica"), "tensor"),
        P(("groups", "replica"), "tensor"),
        P(("groups", "replica"), None),
        P(("groups", "replica")),
        P(("groups", "replica"), None),
    )
    out_specs = P(("groups", "replica"), "tensor")
    return jax.shard_map(body, mesh=mesh, in_specs=in_specs, out_specs=out_specs, check_vma=False)
```

```python
import functools

import jax
import jax.numpy as jnp
from jax import lax
from jax.experimental import pallas as pl
from jax.experimental.pallas import tpu as pltpu
from jax.sharding import PartitionSpec as P

HEAD_DIM = 128
BLK = 256
MAXB = 4
SEGS = 16
SEG = 64
SCALE = HEAD_DIM ** (-0.5)
LOWEST = -1e38
HEADS_AT_ONCE = 4


def attend_kernel(
    groups, zeros, capacity, me, owner, table, blocks, queries, suffix, pool, *refs
):
    outs, (cache, q_all, o_all, blank, segs, used, todo, place, sems, out_sems, zero_sems) = (
        refs[:-11],
        refs[-11:],
    )
    suffix_rows = suffix.shape[0]
    heads = queries.shape[1] // HEAD_DIM
    group = heads // (suffix.shape[1] // (2 * HEAD_DIM))
    at_once = min(HEADS_AT_ONCE, group)
    rows = at_once * SEG
    prefix = MAXB * BLK

    copies = [pltpu.make_async_copy(suffix, cache.at[pl.ds(prefix, suffix_rows)], sems.at[SEGS])]
    for b in range(MAXB):
        start = pl.multiple_of(table[b] * BLK, BLK)
        to = pl.multiple_of((b + MAXB - blocks[0]) % MAXB * BLK, BLK)
        copies.append(
            pltpu.make_async_copy(
                pool.at[pl.ds(start, BLK)], cache.at[pl.ds(to, BLK)], sems.at[SEGS + 1 + b]
            )
        )
    for copy in copies:
        copy.start()

    @pl.loop(0, segs.shape[0])
    def _(i):
        segs[i] = jnp.int32(-1)

    @pl.loop(0, used.shape[0])
    def _(i):
        used[i] = jnp.int32(0)

    @pl.loop(0, SEGS)
    def _(i):
        distance = owner[i] ^ me[0]
        slot = used[distance]
        used[distance] = slot + 1
        segs[distance * capacity + slot] = i

    def rows_of(ref, seg):
        return ref.at[pl.ds(pl.multiple_of(seg * SEG, SEG), SEG)]

    def fetch(seg):
        return pltpu.make_async_copy(rows_of(queries, seg), rows_of(q_all, seg), sems.at[seg])

    def hand(out, at, seg):
        return pltpu.make_async_copy(rows_of(o_all, seg), rows_of(out, at), out_sems.at[seg])

    def clear(out, at, i):
        return pltpu.make_async_copy(blank, rows_of(out, at), zero_sems.at[i])

    def at_of(distance, slot):
        return (me[0] ^ distance) * capacity + slot

    blank[...] = jnp.zeros_like(blank)
    firsts, found, slots = [], jnp.int32(0), 0
    for out, (distance, first, count, before) in zip(outs, groups):
        firsts.append(slots)

        def look(j, found):
            seg = segs[distance * capacity + first + j]
            at = at_of(distance, first + j) if before is None else before + j

            @pl.when(seg >= 0)
            def _():
                fetch(seg).start()
                todo[found] = seg
                place[found] = slots + j

            @pl.when(seg < 0)
            def _():
                clear(out, at, slots + j).start()

            return jnp.where(seg >= 0, found + 1, found)

        found = lax.fori_loop(0, count, look, found)
        slots += count
    blanks = slots
    for distance, first, count in zeros:
        for j in range(count):
            clear(outs[-1], at_of(distance, first + j), blanks + j).start()
        blanks += count
    for copy in copies:
        copy.wait()

    def attend_rows(seg, count, i):
        first = i * at_once
        low = pl.multiple_of((MAXB - blocks[0]) * BLK, BLK)
        pair = first // group * (2 * HEAD_DIM)

        def column(h):
            return pl.ds(pl.multiple_of((first + h) * HEAD_DIM, HEAD_DIM), HEAD_DIM)

        def cached(offset):
            lanes = pl.ds(pl.multiple_of(pair + offset, HEAD_DIM), HEAD_DIM)
            return cache[pl.ds(low, count * BLK), lanes]

        here = pl.ds(pl.multiple_of(seg * SEG, SEG), SEG)
        q = jnp.concatenate([q_all[here, column(h)] for h in range(at_once)], axis=0)
        s = lax.dot_general(
            q, cached(0), (((1,), (1,)), ((), ())), preferred_element_type=jnp.float32
        )
        parts = [s[:, c : c + HEAD_DIM] for c in range(0, count * BLK, HEAD_DIM)]
        token = lax.broadcasted_iota(jnp.int32, (rows, HEAD_DIM), 0) % SEG + seg * SEG % BLK
        key = lax.broadcasted_iota(jnp.int32, (rows, HEAD_DIM), 1)
        masked = BLK // HEAD_DIM
        for c in range(masked):
            at = len(parts) - masked + c
            parts[at] = jnp.where(key + c * HEAD_DIM <= token, parts[at], LOWEST)
        top = jnp.max(functools.reduce(jnp.maximum, parts), axis=-1, keepdims=True)
        top = jnp.broadcast_to(top, (rows, HEAD_DIM))
        weights = [jnp.exp((part - top) * SCALE) for part in parts]
        total = jnp.sum(functools.reduce(jnp.add, weights), axis=-1, keepdims=True)
        mixed = jnp.dot(
            jnp.concatenate([w.astype(jnp.bfloat16) for w in weights], axis=1),
            cached(HEAD_DIM),
            preferred_element_type=jnp.float32,
        )
        out = (mixed / total).astype(o_all.dtype)
        for h in range(at_once):
            o_all[here, column(h)] = out[h * SEG : (h + 1) * SEG]

    @pl.loop(0, found)
    def _(t):
        seg = todo[t]
        fetch(seg).wait()
        blocks_seen = blocks[0] + seg * SEG // BLK + 1
        for count in range(2, MAXB + suffix_rows // BLK + 1):

            @pl.when(blocks_seen == count)
            def _():
                @pl.loop(0, heads // at_once)
                def _(i):
                    attend_rows(seg, count, i)

        to = place[t]
        for out, first, (distance, slot, count, before) in zip(outs, firsts, groups):
            j = to - first

            @pl.when((j >= 0) & (j < count))
            def _():
                at = at_of(distance, slot + j) if before is None else before + j
                hand(out, at, seg).start()

    @pl.loop(0, found)
    def _(t):
        hand(outs[0], 0, todo[t]).wait()

    first = 0
    for distance, slot, count, _ in groups:

        @pl.loop(0, count)
        def _(j):
            @pl.when(segs[distance * capacity + slot + j] < 0)
            def _():
                clear(outs[0], 0, first + j).wait()

        first += count
    for i in range(slots, blanks):
        clear(outs[0], 0, i).wait()


def attend(groups, whole, capacity, me, owner, table, blocks, queries, suffix, pool):
    replicas = lax.axis_size("replica")
    width = queries.shape[1]
    suffix_rows, columns = suffix.shape
    held = [(k, a, b - a, 0) for k, a, b in groups]
    sizes = [(b - a) * SEG for _, a, b in groups]
    zeros = []
    if whole:
        held.append((0, 0, capacity, None))
        sizes.append(replicas * capacity * SEG)
        zeros = [(k, a, b - a) for k, a, b in whole]
    slots = sum(g[2] for g in held) + sum(z[2] for z in zeros)
    return pl.pallas_call(
        functools.partial(attend_kernel, held, zeros, capacity),
        out_shape=[jax.ShapeDtypeStruct((size, width), queries.dtype) for size in sizes],
        grid_spec=pltpu.PrefetchScalarGridSpec(
            num_scalar_prefetch=4,
            grid=(),
            in_specs=[pl.BlockSpec(memory_space=pl.ANY)] * 3,
            out_specs=[pl.BlockSpec(memory_space=pl.ANY)] * len(sizes),
            scratch_shapes=[
                pltpu.VMEM((suffix_rows + MAXB * BLK, columns), suffix.dtype),
                pltpu.VMEM(queries.shape, queries.dtype),
                pltpu.VMEM(queries.shape, queries.dtype),
                pltpu.VMEM((SEG, width), queries.dtype),
                pltpu.SMEM((replicas * capacity,), jnp.int32),
                pltpu.SMEM((replicas,), jnp.int32),
                pltpu.SMEM((SEGS,), jnp.int32),
                pltpu.SMEM((SEGS,), jnp.int32),
                pltpu.SemaphoreType.DMA((SEGS + MAXB + 1,)),
                pltpu.SemaphoreType.DMA((SEGS,)),
                pltpu.SemaphoreType.DMA((slots,)),
            ],
        ),
        compiler_params=pltpu.CompilerParams(vmem_limit_bytes=56 * 2**20),
        cost_estimate=pl.CostEstimate(flops=2**36, bytes_accessed=SEG * width, transcendentals=0),
    )(me[None], owner, table, blocks, queries, suffix, pool)


def put_kernel(start, rows_ref, old, o_ref):
    o_ref[...] = rows_ref[...]


def put(out, rows, start):
    width = out.shape[1]
    return pl.pallas_call(
        put_kernel,
        out_shape=jax.ShapeDtypeStruct(out.shape, out.dtype),
        grid_spec=pltpu.PrefetchScalarGridSpec(
            num_scalar_prefetch=1,
            grid=(rows.shape[0] // SEG,),
            in_specs=[
                pl.BlockSpec((SEG, width), lambda i, start: (i, 0)),
                pl.BlockSpec(memory_space=pl.ANY),
            ],
            out_specs=pl.BlockSpec((SEG, width), lambda i, start: (start[0] + i, 0)),
        ),
        input_output_aliases={2: 0},
        compiler_params=pltpu.CompilerParams(vmem_limit_bytes=4 * 2**20),
        cost_estimate=pl.CostEstimate(flops=3 * 2**27, bytes_accessed=SEG * width, transcendentals=0),
    )(start[None], rows, out)


def swap(rows, distance):
    size = lax.axis_size("replica")
    return lax.ppermute(rows, "replica", [(i, i ^ distance) for i in range(size)])


def swap_some(out, rows, distance, start, segments):
    def branch(count):
        def run(out, rows):
            if count == 0:
                return out
            return put(out, swap(rows[: count * SEG], distance), start)

        return run

    return lax.switch(segments, [branch(c) for c in range(rows.shape[0] // SEG + 1)], out, rows)


def body(queries, suffix_cache, cache_pool, block_table, prefix_blocks, segment_owner):
    replicas = lax.axis_size("replica")
    me = lax.axis_index("replica").astype(jnp.int32)
    capacity = max(2, 2 * SEGS // replicas)
    base = SEGS // replicas
    owner = segment_owner[:, 0]
    far = list(range(replicas - 1, 0, -1))
    if replicas == 4:
        calls = [[(3, 0, 1)], [(2, 0, 2)], [(2, 2, 4), (3, 1, 3)], [(3, 3, 4), (1, 0, 2), (1, 2, 4)]]
    else:
        calls = [[(k, 0, base) for k in far], []]

    def run(groups, whole=()):
        return attend(
            groups,
            whole,
            capacity,
            me,
            owner,
            block_table[0],
            prefix_blocks,
            queries,
            suffix_cache,
            cache_pool,
        )

    def row_of(k, slot):
        return (me ^ k) * capacity + slot

    sent = []
    for i, call in enumerate(calls[:-1]):
        made = run(call)
        if sent:
            made, sent[-1] = lax.optimization_barrier((made, sent[-1]))
        owner, made = lax.optimization_barrier((owner, made))
        sent.append([(swap(rows, k), row_of(k, a)) for (k, a, _), rows in zip(call, made)])
        if i == min(1, len(calls) - 2):
            theirs = [swap(owner[:, None], k) for k in range(1, replicas)]
    owner, theirs = lax.optimization_barrier((owner, theirs))
    over = [(k, base, capacity) for k in far]
    *rest, out = run(calls[-1] + over, over)
    last = [(swap(rows, k), row_of(k, a)) for (k, a, _), rows in zip(calls[-1], rest)]
    rest = rest[len(last) :]
    distances = jnp.arange(1, replicas, dtype=jnp.int32)
    mine = jnp.sum((owner[None, :] == (me ^ distances)[:, None]).astype(jnp.int32), axis=1)
    given = jnp.sum((jnp.concatenate(theirs, axis=1) == me).astype(jnp.int32), axis=0)
    extra = jnp.clip(jnp.maximum(mine, given) - base, 0, capacity - base)
    before = sent[-1]
    after = [s for part in sent[:-1] for s in part] + last
    for rows, start in before:
        out = put(out, rows, start)
    for k, rows in reversed(list(zip(far, rest))):
        out = swap_some(out, rows, k, row_of(k, base), extra[k - 1])
    for rows, start in after:
        out = put(out, rows, start)
    return out


def solution(mesh):
    in_specs = (
        P(("groups", "replica"), "tensor"),
        P(("groups", "replica"), "tensor"),
        P(("groups", "replica"), "tensor"),
        P(("groups", "replica"), None),
        P(("groups", "replica")),
        P(("groups", "replica"), None),
    )
    out_specs = P(("groups", "replica"), "tensor")
    return jax.shard_map(body, mesh=mesh, in_specs=in_specs, out_specs=out_specs, check_vma=False)
```

```python
import functools

import jax
import jax.numpy as jnp
from jax import lax
from jax.experimental import pallas as pl
from jax.experimental.pallas import tpu as pltpu
from jax.sharding import PartitionSpec as P

HEAD_DIM = 128
BLK = 256
MAXB = 4
SEGS = 16
SEG = 64
SCALE = HEAD_DIM ** (-0.5)
LOWEST = -1e38
HEADS_AT_ONCE = 4


def attend_kernel(
    groups, zeros, capacity, me, owner, table, blocks, queries, suffix, pool, *refs
):
    outs, (cache, q_all, o_all, blank, segs, used, todo, place, sems, out_sems, zero_sems) = (
        refs[:-11],
        refs[-11:],
    )
    suffix_rows = suffix.shape[0]
    heads = queries.shape[1] // HEAD_DIM
    group = heads // (suffix.shape[1] // (2 * HEAD_DIM))
    at_once = min(HEADS_AT_ONCE, group)
    rows = at_once * SEG
    prefix = MAXB * BLK

    copies = [pltpu.make_async_copy(suffix, cache.at[pl.ds(prefix, suffix_rows)], sems.at[SEGS])]
    for b in range(MAXB):
        start = pl.multiple_of(table[b] * BLK, BLK)
        to = pl.multiple_of((b + MAXB - blocks[0]) % MAXB * BLK, BLK)
        copies.append(
            pltpu.make_async_copy(
                pool.at[pl.ds(start, BLK)], cache.at[pl.ds(to, BLK)], sems.at[SEGS + 1 + b]
            )
        )
    for copy in copies:
        copy.start()

    @pl.loop(0, segs.shape[0])
    def _(i):
        segs[i] = jnp.int32(-1)

    @pl.loop(0, used.shape[0])
    def _(i):
        used[i] = jnp.int32(0)

    @pl.loop(0, SEGS)
    def _(i):
        distance = owner[i] ^ me[0]
        slot = used[distance]
        used[distance] = slot + 1
        segs[distance * capacity + slot] = i

    def rows_of(ref, seg):
        return ref.at[pl.ds(pl.multiple_of(seg * SEG, SEG), SEG)]

    def fetch(seg):
        return pltpu.make_async_copy(rows_of(queries, seg), rows_of(q_all, seg), sems.at[seg])

    def hand(out, at, seg):
        return pltpu.make_async_copy(rows_of(o_all, seg), rows_of(out, at), out_sems.at[seg])

    def clear(out, at, i):
        return pltpu.make_async_copy(blank, rows_of(out, at), zero_sems.at[i])

    def at_of(distance, slot):
        return (me[0] ^ distance) * capacity + slot

    blank[...] = jnp.zeros_like(blank)
    firsts, found, slots = [], jnp.int32(0), 0
    for out, (distance, first, count, before) in zip(outs, groups):
        firsts.append(slots)

        def look(j, found):
            seg = segs[distance * capacity + first + j]
            at = at_of(distance, first + j) if before is None else before + j

            @pl.when(seg >= 0)
            def _():
                fetch(seg).start()
                todo[found] = seg
                place[found] = slots + j

            @pl.when(seg < 0)
            def _():
                clear(out, at, slots + j).start()

            return jnp.where(seg >= 0, found + 1, found)

        found = lax.fori_loop(0, count, look, found)
        slots += count
    blanks = slots
    for distance, first, count in zeros:
        for j in range(count):
            clear(outs[-1], at_of(distance, first + j), blanks + j).start()
        blanks += count
    for copy in copies:
        copy.wait()

    def attend_rows(seg, count, i):
        first = i * at_once
        low = pl.multiple_of((MAXB - blocks[0]) * BLK, BLK)
        pair = first // group * (2 * HEAD_DIM)

        def column(h):
            return pl.ds(pl.multiple_of((first + h) * HEAD_DIM, HEAD_DIM), HEAD_DIM)

        def cached(offset):
            lanes = pl.ds(pl.multiple_of(pair + offset, HEAD_DIM), HEAD_DIM)
            return cache[pl.ds(low, count * BLK), lanes]

        here = pl.ds(pl.multiple_of(seg * SEG, SEG), SEG)
        q = jnp.concatenate([q_all[here, column(h)] for h in range(at_once)], axis=0)
        s = lax.dot_general(
            q, cached(0), (((1,), (1,)), ((), ())), preferred_element_type=jnp.float32
        )
        parts = [s[:, c : c + HEAD_DIM] for c in range(0, count * BLK, HEAD_DIM)]
        token = lax.broadcasted_iota(jnp.int32, (rows, HEAD_DIM), 0) % SEG + seg * SEG % BLK
        key = lax.broadcasted_iota(jnp.int32, (rows, HEAD_DIM), 1)
        masked = BLK // HEAD_DIM
        for c in range(masked):
            at = len(parts) - masked + c
            parts[at] = jnp.where(key + c * HEAD_DIM <= token, parts[at], LOWEST)
        top = jnp.max(functools.reduce(jnp.maximum, parts), axis=-1, keepdims=True)
        top = jnp.broadcast_to(top, (rows, HEAD_DIM))
        weights = [jnp.exp((part - top) * SCALE) for part in parts]
        total = jnp.sum(functools.reduce(jnp.add, weights), axis=-1, keepdims=True)
        mixed = jnp.dot(
            jnp.concatenate([w.astype(jnp.bfloat16) for w in weights], axis=1),
            cached(HEAD_DIM),
            preferred_element_type=jnp.float32,
        )
        out = (mixed / total).astype(o_all.dtype)
        for h in range(at_once):
            o_all[here, column(h)] = out[h * SEG : (h + 1) * SEG]

    @pl.loop(0, found)
    def _(t):
        seg = todo[t]
        fetch(seg).wait()
        blocks_seen = blocks[0] + seg * SEG // BLK + 1
        for count in range(2, MAXB + suffix_rows // BLK + 1):

            @pl.when(blocks_seen == count)
            def _():
                @pl.loop(0, heads // at_once)
                def _(i):
                    attend_rows(seg, count, i)

        to = place[t]
        for out, first, (distance, slot, count, before) in zip(outs, firsts, groups):
            j = to - first

            @pl.when((j >= 0) & (j < count))
            def _():
                at = at_of(distance, slot + j) if before is None else before + j
                hand(out, at, seg).start()

    @pl.loop(0, found)
    def _(t):
        hand(outs[0], 0, todo[t]).wait()

    first = 0
    for distance, slot, count, _ in groups:

        @pl.loop(0, count)
        def _(j):
            @pl.when(segs[distance * capacity + slot + j] < 0)
            def _():
                clear(outs[0], 0, first + j).wait()

        first += count
    for i in range(slots, blanks):
        clear(outs[0], 0, i).wait()


def attend(groups, whole, capacity, me, owner, table, blocks, queries, suffix, pool):
    replicas = lax.axis_size("replica")
    width = queries.shape[1]
    suffix_rows, columns = suffix.shape
    held = [(k, a, b - a, 0) for k, a, b in groups]
    sizes = [(b - a) * SEG for _, a, b in groups]
    zeros = []
    if whole:
        held.append((0, 0, capacity, None))
        sizes.append(replicas * capacity * SEG)
        zeros = [(k, a, b - a) for k, a, b in whole]
    slots = sum(g[2] for g in held) + sum(z[2] for z in zeros)
    return pl.pallas_call(
        functools.partial(attend_kernel, held, zeros, capacity),
        out_shape=[jax.ShapeDtypeStruct((size, width), queries.dtype) for size in sizes],
        grid_spec=pltpu.PrefetchScalarGridSpec(
            num_scalar_prefetch=4,
            grid=(),
            in_specs=[pl.BlockSpec(memory_space=pl.ANY)] * 3,
            out_specs=[pl.BlockSpec(memory_space=pl.ANY)] * len(sizes),
            scratch_shapes=[
                pltpu.VMEM((suffix_rows + MAXB * BLK, columns), suffix.dtype),
                pltpu.VMEM(queries.shape, queries.dtype),
                pltpu.VMEM(queries.shape, queries.dtype),
                pltpu.VMEM((SEG, width), queries.dtype),
                pltpu.SMEM((replicas * capacity,), jnp.int32),
                pltpu.SMEM((replicas,), jnp.int32),
                pltpu.SMEM((SEGS,), jnp.int32),
                pltpu.SMEM((SEGS,), jnp.int32),
                pltpu.SemaphoreType.DMA((SEGS + MAXB + 1,)),
                pltpu.SemaphoreType.DMA((SEGS,)),
                pltpu.SemaphoreType.DMA((slots,)),
            ],
        ),
        compiler_params=pltpu.CompilerParams(vmem_limit_bytes=56 * 2**20),
        cost_estimate=pl.CostEstimate(flops=2**36, bytes_accessed=SEG * width, transcendentals=0),
    )(me[None], owner, table, blocks, queries, suffix, pool)


def put_kernel(spans, *refs):
    count = len(spans)
    starts, pieces, out, stages = refs[0], refs[1 : 1 + count], refs[2 + count], refs[3 + count :]
    stages, sems = stages[:-1], stages[-1]
    loads = [
        pltpu.make_async_copy(piece, stage, sems.at[0, i])
        for i, (piece, stage) in enumerate(zip(pieces, stages))
    ]
    stores = []
    for i, (span, stage) in enumerate(zip(spans, stages)):
        at = pl.multiple_of(starts[i] * SEG, SEG)
        stores.append(pltpu.make_async_copy(stage, out.at[pl.ds(at, span)], sems.at[1, i]))
    for load in loads:
        load.start()
    for load, store in zip(loads, stores):
        load.wait()
        store.start()
    for store in stores:
        store.wait()


def put(out, pieces):
    rows = [piece for piece, _ in pieces]
    starts = jnp.stack([start for _, start in pieces])
    count = len(rows)
    return pl.pallas_call(
        functools.partial(put_kernel, [r.shape[0] for r in rows]),
        out_shape=jax.ShapeDtypeStruct(out.shape, out.dtype),
        grid_spec=pltpu.PrefetchScalarGridSpec(
            num_scalar_prefetch=1,
            grid=(),
            in_specs=[pl.BlockSpec(memory_space=pl.ANY)] * (count + 1),
            out_specs=pl.BlockSpec(memory_space=pl.ANY),
            scratch_shapes=[pltpu.VMEM(r.shape, r.dtype) for r in rows]
            + [pltpu.SemaphoreType.DMA((2, count))],
        ),
        input_output_aliases={count + 1: 0},
        compiler_params=pltpu.CompilerParams(vmem_limit_bytes=8 * 2**20),
        cost_estimate=pl.CostEstimate(flops=3 * 2**27, bytes_accessed=SEG, transcendentals=0),
    )(starts, *rows, out)


def swap(rows, distance):
    size = lax.axis_size("replica")
    return lax.ppermute(rows, "replica", [(i, i ^ distance) for i in range(size)])


def swap_some(out, rows, distance, start, segments):
    def branch(count):
        def run(out, rows):
            if count == 0:
                return out
            return put(out, [(swap(rows[: count * SEG], distance), start)])

        return run

    return lax.switch(segments, [branch(c) for c in range(rows.shape[0] // SEG + 1)], out, rows)


def body(queries, suffix_cache, cache_pool, block_table, prefix_blocks, segment_owner):
    replicas = lax.axis_size("replica")
    me = lax.axis_index("replica").astype(jnp.int32)
    capacity = max(2, 2 * SEGS // replicas)
    base = SEGS // replicas
    owner = segment_owner[:, 0]
    far = list(range(replicas - 1, 0, -1))
    if replicas == 4:
        calls = [[(3, 0, 2)], [(2, 0, 3), (1, 0, 1)], [(2, 3, 4), (3, 2, 4), (1, 1, 4)]]
    else:
        calls = [[(k, 0, base) for k in far]]

    def run(groups, whole=()):
        return attend(
            groups,
            whole,
            capacity,
            me,
            owner,
            block_table[0],
            prefix_blocks,
            queries,
            suffix_cache,
            cache_pool,
        )

    def row_of(k, slot):
        return (me ^ k) * capacity + slot

    sent = []
    for i, call in enumerate(calls):
        if i >= 2:
            owner, sent[i - 2] = lax.optimization_barrier((owner, sent[i - 2]))
        made = run(call)
        owner, made = lax.optimization_barrier((owner, made))
        sent.append([(swap(rows, k), row_of(k, a)) for (k, a, _), rows in zip(call, made)])
    for i in range(max(0, len(calls) - 2), len(calls) - 1):
        owner, sent[i] = lax.optimization_barrier((owner, sent[i]))
    over = [(k, base, capacity) for k in far]
    *rest, out = run(over, over)
    owner, rest = lax.optimization_barrier((owner, rest))
    theirs = [swap(owner[:, None], k) for k in range(1, replicas)]
    distances = jnp.arange(1, replicas, dtype=jnp.int32)
    mine = jnp.sum((owner[None, :] == (me ^ distances)[:, None]).astype(jnp.int32), axis=1)
    given = jnp.sum((jnp.concatenate(theirs, axis=1) == me).astype(jnp.int32), axis=0)
    extra = jnp.clip(jnp.maximum(mine, given) - base, 0, capacity - base)
    early = [piece for part in sent[:-1] for piece in part]
    if early:
        out = put(out, early)
    out = put(out, sent[-1])
    for k, rows in reversed(list(zip(far, rest))):
        out = swap_some(out, rows, k, row_of(k, base), extra[k - 1])
    return out


def solution(mesh):
    in_specs = (
        P(("groups", "replica"), "tensor"),
        P(("groups", "replica"), "tensor"),
        P(("groups", "replica"), "tensor"),
        P(("groups", "replica"), None),
        P(("groups", "replica")),
        P(("groups", "replica"), None),
    )
    out_specs = P(("groups", "replica"), "tensor")
    return jax.shard_map(body, mesh=mesh, in_specs=in_specs, out_specs=out_specs, check_vma=False)
```

```python
import functools

import jax
import jax.numpy as jnp
from jax import lax
from jax.experimental import pallas as pl
from jax.experimental.pallas import tpu as pltpu
from jax.sharding import PartitionSpec as P

HEAD_DIM = 128
BLK = 256
MAXB = 4
SEGS = 16
SEG = 64
SCALE = HEAD_DIM ** (-0.5)
LOWEST = -1e38
HEADS_AT_ONCE = 4


def attend_kernel(
    groups, zeros, capacity, extra, me, owner, table, blocks, queries, suffix, pool, *refs
):
    outs, (cache, q_all, o_all, blank, segs, used, todo, place, sems, out_sems, zero_sems) = (
        refs[extra:-11],
        refs[-11:],
    )
    suffix_rows = suffix.shape[0]
    heads = queries.shape[1] // HEAD_DIM
    group = heads // (suffix.shape[1] // (2 * HEAD_DIM))
    at_once = min(HEADS_AT_ONCE, group)
    rows = at_once * SEG
    prefix = MAXB * BLK

    copies = [pltpu.make_async_copy(suffix, cache.at[pl.ds(prefix, suffix_rows)], sems.at[SEGS])]
    for b in range(MAXB):
        start = pl.multiple_of(table[b] * BLK, BLK)
        to = pl.multiple_of((b + MAXB - blocks[0]) % MAXB * BLK, BLK)
        copies.append(
            pltpu.make_async_copy(
                pool.at[pl.ds(start, BLK)], cache.at[pl.ds(to, BLK)], sems.at[SEGS + 1 + b]
            )
        )
    for copy in copies:
        copy.start()

    @pl.loop(0, segs.shape[0])
    def _(i):
        segs[i] = jnp.int32(-1)

    @pl.loop(0, used.shape[0])
    def _(i):
        used[i] = jnp.int32(0)

    @pl.loop(0, SEGS)
    def _(i):
        distance = owner[i] ^ me[0]
        slot = used[distance]
        used[distance] = slot + 1
        segs[distance * capacity + slot] = i

    def rows_of(ref, seg):
        return ref.at[pl.ds(pl.multiple_of(seg * SEG, SEG), SEG)]

    def fetch(seg):
        return pltpu.make_async_copy(rows_of(queries, seg), rows_of(q_all, seg), sems.at[seg])

    def hand(out, at, seg):
        return pltpu.make_async_copy(rows_of(o_all, seg), rows_of(out, at), out_sems.at[seg])

    def clear(out, at, i):
        return pltpu.make_async_copy(blank, rows_of(out, at), zero_sems.at[i])

    def at_of(distance, slot):
        return (me[0] ^ distance) * capacity + slot

    blank[...] = jnp.zeros_like(blank)
    firsts, found, slots = [], jnp.int32(0), 0
    for out, (distance, first, count, before) in zip(outs, groups):
        firsts.append(slots)

        def look(j, found):
            seg = segs[distance * capacity + first + j]
            at = at_of(distance, first + j) if before is None else before + j

            @pl.when(seg >= 0)
            def _():
                fetch(seg).start()
                todo[found] = seg
                place[found] = slots + j

            @pl.when(seg < 0)
            def _():
                clear(out, at, slots + j).start()

            return jnp.where(seg >= 0, found + 1, found)

        found = lax.fori_loop(0, count, look, found)
        slots += count
    blanks = slots
    for distance, first, count in zeros:
        for j in range(count):
            clear(outs[-1], at_of(distance, first + j), blanks + j).start()
        blanks += count
    for copy in copies:
        copy.wait()

    def attend_rows(seg, count, i):
        first = i * at_once
        low = pl.multiple_of((MAXB - blocks[0]) * BLK, BLK)
        pair = first // group * (2 * HEAD_DIM)

        def column(h):
            return pl.ds(pl.multiple_of((first + h) * HEAD_DIM, HEAD_DIM), HEAD_DIM)

        def cached(offset):
            lanes = pl.ds(pl.multiple_of(pair + offset, HEAD_DIM), HEAD_DIM)
            return cache[pl.ds(low, count * BLK), lanes]

        here = pl.ds(pl.multiple_of(seg * SEG, SEG), SEG)
        q = jnp.concatenate([q_all[here, column(h)] for h in range(at_once)], axis=0)
        s = lax.dot_general(
            q, cached(0), (((1,), (1,)), ((), ())), preferred_element_type=jnp.float32
        )
        parts = [s[:, c : c + HEAD_DIM] for c in range(0, count * BLK, HEAD_DIM)]
        token = lax.broadcasted_iota(jnp.int32, (rows, HEAD_DIM), 0) % SEG + seg * SEG % BLK
        key = lax.broadcasted_iota(jnp.int32, (rows, HEAD_DIM), 1)
        masked = BLK // HEAD_DIM
        for c in range(masked):
            at = len(parts) - masked + c
            parts[at] = jnp.where(key + c * HEAD_DIM <= token, parts[at], LOWEST)
        top = jnp.max(functools.reduce(jnp.maximum, parts), axis=-1, keepdims=True)
        top = jnp.broadcast_to(top, (rows, HEAD_DIM))
        weights = [jnp.exp((part - top) * SCALE) for part in parts]
        total = jnp.sum(functools.reduce(jnp.add, weights), axis=-1, keepdims=True)
        mixed = jnp.dot(
            jnp.concatenate([w.astype(jnp.bfloat16) for w in weights], axis=1),
            cached(HEAD_DIM),
            preferred_element_type=jnp.float32,
        )
        out = (mixed / total).astype(o_all.dtype)
        for h in range(at_once):
            o_all[here, column(h)] = out[h * SEG : (h + 1) * SEG]

    @pl.loop(0, found)
    def _(t):
        seg = todo[t]
        fetch(seg).wait()
        blocks_seen = blocks[0] + seg * SEG // BLK + 1
        for count in range(2, MAXB + suffix_rows // BLK + 1):

            @pl.when(blocks_seen == count)
            def _():
                @pl.loop(0, heads // at_once)
                def _(i):
                    attend_rows(seg, count, i)

        to = place[t]
        for out, first, (distance, slot, count, before) in zip(outs, firsts, groups):
            j = to - first

            @pl.when((j >= 0) & (j < count))
            def _():
                at = at_of(distance, slot + j) if before is None else before + j
                hand(out, at, seg).start()

    @pl.loop(0, found)
    def _(t):
        hand(outs[0], 0, todo[t]).wait()

    first = 0
    for distance, slot, count, _ in groups:

        @pl.loop(0, count)
        def _(j):
            @pl.when(segs[distance * capacity + slot + j] < 0)
            def _():
                clear(outs[0], 0, first + j).wait()

        first += count
    for i in range(slots, blanks):
        clear(outs[0], 0, i).wait()


def attend(groups, own, zeros, old, capacity, me, owner, table, blocks, queries, suffix, pool):
    replicas = lax.axis_size("replica")
    width = queries.shape[1]
    suffix_rows, columns = suffix.shape
    held = [(k, a, b - a, 0) for k, a, b in groups]
    sizes = [(b - a) * SEG for _, a, b in groups]
    if own:
        held.append((0, own[0], own[1] - own[0], None))
        sizes.append(replicas * capacity * SEG)
    zeros = [(k, a, b - a) for k, a, b in zeros]
    slots = sum(g[2] for g in held) + sum(z[2] for z in zeros)
    inputs = [queries, suffix, pool] + ([] if old is None else [old])
    return pl.pallas_call(
        functools.partial(attend_kernel, held, zeros, capacity, len(inputs) - 3),
        out_shape=[jax.ShapeDtypeStruct((size, width), queries.dtype) for size in sizes],
        grid_spec=pltpu.PrefetchScalarGridSpec(
            num_scalar_prefetch=4,
            grid=(),
            in_specs=[pl.BlockSpec(memory_space=pl.ANY)] * len(inputs),
            out_specs=[pl.BlockSpec(memory_space=pl.ANY)] * len(sizes),
            scratch_shapes=[
                pltpu.VMEM((suffix_rows + MAXB * BLK, columns), suffix.dtype),
                pltpu.VMEM(queries.shape, queries.dtype),
                pltpu.VMEM(queries.shape, queries.dtype),
                pltpu.VMEM((SEG, width), queries.dtype),
                pltpu.SMEM((replicas * capacity,), jnp.int32),
                pltpu.SMEM((replicas,), jnp.int32),
                pltpu.SMEM((SEGS,), jnp.int32),
                pltpu.SMEM((SEGS,), jnp.int32),
                pltpu.SemaphoreType.DMA((SEGS + MAXB + 1,)),
                pltpu.SemaphoreType.DMA((SEGS,)),
                pltpu.SemaphoreType.DMA((slots,)),
            ],
        ),
        input_output_aliases={} if old is None else {7: len(sizes) - 1},
        compiler_params=pltpu.CompilerParams(vmem_limit_bytes=56 * 2**20),
        cost_estimate=pl.CostEstimate(flops=2**36, bytes_accessed=SEG * width, transcendentals=0),
    )(me[None], owner, table, blocks, *inputs)


def put_kernel(spans, *refs):
    count = len(spans)
    starts, pieces, out, stages = refs[0], refs[1 : 1 + count], refs[2 + count], refs[3 + count :]
    stages, sems = stages[:-1], stages[-1]
    loads = [
        pltpu.make_async_copy(piece, stage, sems.at[0, i])
        for i, (piece, stage) in enumerate(zip(pieces, stages))
    ]
    stores = []
    for i, (span, stage) in enumerate(zip(spans, stages)):
        at = pl.multiple_of(starts[i] * SEG, SEG)
        stores.append(pltpu.make_async_copy(stage, out.at[pl.ds(at, span)], sems.at[1, i]))
    for load in loads:
        load.start()
    for load, store in zip(loads, stores):
        load.wait()
        store.start()
    for store in stores:
        store.wait()


def put(out, pieces):
    rows = [piece for piece, _ in pieces]
    starts = jnp.stack([start for _, start in pieces])
    count = len(rows)
    return pl.pallas_call(
        functools.partial(put_kernel, [r.shape[0] for r in rows]),
        out_shape=jax.ShapeDtypeStruct(out.shape, out.dtype),
        grid_spec=pltpu.PrefetchScalarGridSpec(
            num_scalar_prefetch=1,
            grid=(),
            in_specs=[pl.BlockSpec(memory_space=pl.ANY)] * (count + 1),
            out_specs=pl.BlockSpec(memory_space=pl.ANY),
            scratch_shapes=[pltpu.VMEM(r.shape, r.dtype) for r in rows]
            + [pltpu.SemaphoreType.DMA((2, count))],
        ),
        input_output_aliases={count + 1: 0},
        compiler_params=pltpu.CompilerParams(vmem_limit_bytes=8 * 2**20),
        cost_estimate=pl.CostEstimate(flops=3 * 2**27, bytes_accessed=SEG, transcendentals=0),
    )(starts, *rows, out)


def swap(rows, distance):
    size = lax.axis_size("replica")
    return lax.ppermute(rows, "replica", [(i, i ^ distance) for i in range(size)])


def swap_some(out, rows, distance, start, segments, work):
    most = rows.shape[0] // SEG
    sizes = [0] + [2**i for i in range(most.bit_length()) if 2**i < most] + [most]

    def branch(count):
        def run(out, rows):
            if count == 0:
                return work(out)
            got = swap(rows[: count * SEG], distance)
            return put(work(out), [(got, start)])

        return run

    chosen = sum((segments > size).astype(jnp.int32) for size in sizes[:-1])
    return lax.switch(chosen, [branch(count) for count in sizes], out, rows)


def body(queries, suffix_cache, cache_pool, block_table, prefix_blocks, segment_owner):
    replicas = lax.axis_size("replica")
    me = lax.axis_index("replica").astype(jnp.int32)
    capacity = max(2, 2 * SEGS // replicas)
    base = SEGS // replicas
    owner = segment_owner[:, 0]
    far = list(range(replicas - 1, 0, -1))
    if replicas == 4:
        calls = [[(3, 0, 2)], [(2, 0, 3), (1, 0, 1)], [(2, 3, 4), (3, 2, 4), (1, 1, 4)]]
        parts = [(0, 3), (3, 6), (6, 8)]
    else:
        calls = [[(k, 0, base) for k in far]]
        parts = []

    def run(groups, own=None, zeros=(), old=None):
        return attend(
            groups,
            own,
            zeros,
            old,
            capacity,
            me,
            owner,
            block_table[0],
            prefix_blocks,
            queries,
            suffix_cache,
            cache_pool,
        )

    def row_of(k, slot):
        return (me ^ k) * capacity + slot

    over = [(k, base, capacity) for k in far]
    sent = []
    for i, call in enumerate(calls):
        if i >= 2:
            owner, sent[i - 2] = lax.optimization_barrier((owner, sent[i - 2]))
        if i < len(calls) - 1:
            made = run(call)
        else:
            *made, out = run(call + over, (0, 0) if parts else (0, capacity), over)
        owner, made = lax.optimization_barrier((owner, made))
        sent.append([(swap(rows, k), row_of(k, a)) for (k, a, _), rows in zip(call, made)])
    rest = made[len(calls[-1]) :]
    theirs = [swap(owner[:, None], k) for k in range(1, replicas)]
    distances = jnp.arange(1, replicas, dtype=jnp.int32)
    mine = jnp.sum((owner[None, :] == (me ^ distances)[:, None]).astype(jnp.int32), axis=1)
    given = jnp.sum((jnp.concatenate(theirs, axis=1) == me).astype(jnp.int32), axis=0)
    extra = jnp.clip(jnp.maximum(mine, given) - base, 0, capacity - base)
    early = [piece for part in sent[:-1] for piece in part]
    if early:
        out = put(out, early)
    parts = parts + [None] * (len(far) - len(parts))
    for k, rows, part in zip(far, rest, parts):
        work = lambda out: run([], part, (), out)[0] if part else out
        out = swap_some(out, rows, k, row_of(k, base), extra[k - 1], work)
    return put(out, sent[-1])


def solution(mesh):
    in_specs = (
        P(("groups", "replica"), "tensor"),
        P(("groups", "replica"), "tensor"),
        P(("groups", "replica"), "tensor"),
        P(("groups", "replica"), None),
        P(("groups", "replica")),
        P(("groups", "replica"), None),
    )
    out_specs = P(("groups", "replica"), "tensor")
    return jax.shard_map(body, mesh=mesh, in_specs=in_specs, out_specs=out_specs, check_vma=False)
```

```python
import functools

import jax
import jax.numpy as jnp
from jax import lax
from jax.experimental import pallas as pl
from jax.experimental.pallas import tpu as pltpu
from jax.sharding import PartitionSpec as P

HEAD_DIM = 128
BLK = 256
MAXB = 4
SEGS = 16
SEG = 64
SCALE = HEAD_DIM ** (-0.5)
LOWEST = -1e38
HEADS_AT_ONCE = 4


def attend_kernel(
    groups, zeros, capacity, me, owner, table, blocks, queries, suffix, pool, *refs
):
    outs, (cache, q_all, o_all, blank, segs, used, todo, place, sems, out_sems, zero_sems) = (
        refs[:-11],
        refs[-11:],
    )
    suffix_rows = suffix.shape[0]
    heads = queries.shape[1] // HEAD_DIM
    group = heads // (suffix.shape[1] // (2 * HEAD_DIM))
    at_once = min(HEADS_AT_ONCE, group)
    rows = at_once * SEG
    prefix = MAXB * BLK

    copies = [pltpu.make_async_copy(suffix, cache.at[pl.ds(prefix, suffix_rows)], sems.at[SEGS])]
    for b in range(MAXB):
        start = pl.multiple_of(table[b] * BLK, BLK)
        to = pl.multiple_of((b + MAXB - blocks[0]) % MAXB * BLK, BLK)
        copies.append(
            pltpu.make_async_copy(
                pool.at[pl.ds(start, BLK)], cache.at[pl.ds(to, BLK)], sems.at[SEGS + 1 + b]
            )
        )
    for copy in copies:
        copy.start()

    @pl.loop(0, segs.shape[0])
    def _(i):
        segs[i] = jnp.int32(-1)

    @pl.loop(0, used.shape[0])
    def _(i):
        used[i] = jnp.int32(0)

    @pl.loop(0, SEGS)
    def _(i):
        distance = owner[i] ^ me[0]
        slot = used[distance]
        used[distance] = slot + 1
        segs[distance * capacity + slot] = i

    def rows_of(ref, seg):
        return ref.at[pl.ds(pl.multiple_of(seg * SEG, SEG), SEG)]

    def fetch(seg):
        return pltpu.make_async_copy(rows_of(queries, seg), rows_of(q_all, seg), sems.at[seg])

    def hand(out, at, seg):
        return pltpu.make_async_copy(rows_of(o_all, seg), rows_of(out, at), out_sems.at[seg])

    def clear(out, at, i):
        return pltpu.make_async_copy(blank, rows_of(out, at), zero_sems.at[i])

    def at_of(distance, slot):
        return (me[0] ^ distance) * capacity + slot

    blank[...] = jnp.zeros_like(blank)
    firsts, found, slots = [], jnp.int32(0), 0
    for out, (distance, first, count, before) in zip(outs, groups):
        firsts.append(slots)

        def look(j, found):
            seg = segs[distance * capacity + first + j]
            at = at_of(distance, first + j) if before is None else before + j

            @pl.when(seg >= 0)
            def _():
                fetch(seg).start()
                todo[found] = seg
                place[found] = slots + j

            @pl.when(seg < 0)
            def _():
                clear(out, at, slots + j).start()

            return jnp.where(seg >= 0, found + 1, found)

        found = lax.fori_loop(0, count, look, found)
        slots += count
    blanks = slots
    for distance, first, count in zeros:
        for j in range(count):
            clear(outs[-1], at_of(distance, first + j), blanks + j).start()
        blanks += count
    for copy in copies:
        copy.wait()

    def attend_rows(seg, count, i):
        first = i * at_once
        low = pl.multiple_of((MAXB - blocks[0]) * BLK, BLK)
        pair = first // group * (2 * HEAD_DIM)

        def column(h):
            return pl.ds(pl.multiple_of((first + h) * HEAD_DIM, HEAD_DIM), HEAD_DIM)

        def cached(offset):
            lanes = pl.ds(pl.multiple_of(pair + offset, HEAD_DIM), HEAD_DIM)
            return cache[pl.ds(low, count * BLK), lanes]

        here = pl.ds(pl.multiple_of(seg * SEG, SEG), SEG)
        q = jnp.concatenate([q_all[here, column(h)] for h in range(at_once)], axis=0)
        s = lax.dot_general(
            q, cached(0), (((1,), (1,)), ((), ())), preferred_element_type=jnp.float32
        )
        parts = [s[:, c : c + HEAD_DIM] for c in range(0, count * BLK, HEAD_DIM)]
        token = lax.broadcasted_iota(jnp.int32, (rows, HEAD_DIM), 0) % SEG + seg * SEG % BLK
        key = lax.broadcasted_iota(jnp.int32, (rows, HEAD_DIM), 1)
        masked = BLK // HEAD_DIM
        for c in range(masked):
            at = len(parts) - masked + c
            parts[at] = jnp.where(key + c * HEAD_DIM <= token, parts[at], LOWEST)
        top = jnp.max(functools.reduce(jnp.maximum, parts), axis=-1, keepdims=True)
        top = jnp.broadcast_to(top, (rows, HEAD_DIM))
        weights = [jnp.exp((part - top) * SCALE) for part in parts]
        total = jnp.sum(functools.reduce(jnp.add, weights), axis=-1, keepdims=True)
        mixed = jnp.dot(
            jnp.concatenate([w.astype(jnp.bfloat16) for w in weights], axis=1),
            cached(HEAD_DIM),
            preferred_element_type=jnp.float32,
        )
        out = (mixed / total).astype(o_all.dtype)
        for h in range(at_once):
            o_all[here, column(h)] = out[h * SEG : (h + 1) * SEG]

    @pl.loop(0, found)
    def _(t):
        seg = todo[t]
        fetch(seg).wait()
        blocks_seen = blocks[0] + seg * SEG // BLK + 1
        for count in range(2, MAXB + suffix_rows // BLK + 1):

            @pl.when(blocks_seen == count)
            def _():
                @pl.loop(0, heads // at_once)
                def _(i):
                    attend_rows(seg, count, i)

        to = place[t]
        for out, first, (distance, slot, count, before) in zip(outs, firsts, groups):
            j = to - first

            @pl.when((j >= 0) & (j < count))
            def _():
                at = at_of(distance, slot + j) if before is None else before + j
                hand(out, at, seg).start()

    @pl.loop(0, found)
    def _(t):
        hand(outs[0], 0, todo[t]).wait()

    first = 0
    for distance, slot, count, _ in groups:

        @pl.loop(0, count)
        def _(j):
            @pl.when(segs[distance * capacity + slot + j] < 0)
            def _():
                clear(outs[0], 0, first + j).wait()

        first += count
    for i in range(slots, blanks):
        clear(outs[0], 0, i).wait()


def attend(groups, whole, capacity, me, owner, table, blocks, queries, suffix, pool):
    replicas = lax.axis_size("replica")
    width = queries.shape[1]
    suffix_rows, columns = suffix.shape
    held = [(k, a, b - a, 0) for k, a, b in groups]
    sizes = [(b - a) * SEG for _, a, b in groups]
    zeros = []
    if whole:
        held.append((0, 0, capacity, None))
        sizes.append(replicas * capacity * SEG)
        zeros = [(k, a, b - a) for k, a, b in whole]
    slots = sum(g[2] for g in held) + sum(z[2] for z in zeros)
    return pl.pallas_call(
        functools.partial(attend_kernel, held, zeros, capacity),
        out_shape=[jax.ShapeDtypeStruct((size, width), queries.dtype) for size in sizes],
        grid_spec=pltpu.PrefetchScalarGridSpec(
            num_scalar_prefetch=4,
            grid=(),
            in_specs=[pl.BlockSpec(memory_space=pl.ANY)] * 3,
            out_specs=[pl.BlockSpec(memory_space=pl.ANY)] * len(sizes),
            scratch_shapes=[
                pltpu.VMEM((suffix_rows + MAXB * BLK, columns), suffix.dtype),
                pltpu.VMEM(queries.shape, queries.dtype),
                pltpu.VMEM(queries.shape, queries.dtype),
                pltpu.VMEM((SEG, width), queries.dtype),
                pltpu.SMEM((replicas * capacity,), jnp.int32),
                pltpu.SMEM((replicas,), jnp.int32),
                pltpu.SMEM((SEGS,), jnp.int32),
                pltpu.SMEM((SEGS,), jnp.int32),
                pltpu.SemaphoreType.DMA((SEGS + MAXB + 1,)),
                pltpu.SemaphoreType.DMA((SEGS,)),
                pltpu.SemaphoreType.DMA((slots,)),
            ],
        ),
        compiler_params=pltpu.CompilerParams(vmem_limit_bytes=56 * 2**20),
        cost_estimate=pl.CostEstimate(flops=2**36, bytes_accessed=SEG * width, transcendentals=0),
    )(me[None], owner, table, blocks, queries, suffix, pool)


def put_kernel(spans, *refs):
    count = len(spans)
    starts, pieces, out, stages = refs[0], refs[1 : 1 + count], refs[2 + count], refs[3 + count :]
    stages, sems = stages[:-1], stages[-1]
    loads = [
        pltpu.make_async_copy(piece, stage, sems.at[0, i])
        for i, (piece, stage) in enumerate(zip(pieces, stages))
    ]
    stores = []
    for i, (span, stage) in enumerate(zip(spans, stages)):
        at = pl.multiple_of(starts[i] * SEG, SEG)
        stores.append(pltpu.make_async_copy(stage, out.at[pl.ds(at, span)], sems.at[1, i]))
    for load in loads:
        load.start()
    for load, store in zip(loads, stores):
        load.wait()
        store.start()
    for store in stores:
        store.wait()


def put(out, pieces):
    rows = [piece for piece, _ in pieces]
    starts = jnp.stack([start for _, start in pieces])
    count = len(rows)
    return pl.pallas_call(
        functools.partial(put_kernel, [r.shape[0] for r in rows]),
        out_shape=jax.ShapeDtypeStruct(out.shape, out.dtype),
        grid_spec=pltpu.PrefetchScalarGridSpec(
            num_scalar_prefetch=1,
            grid=(),
            in_specs=[pl.BlockSpec(memory_space=pl.ANY)] * (count + 1),
            out_specs=pl.BlockSpec(memory_space=pl.ANY),
            scratch_shapes=[pltpu.VMEM(r.shape, r.dtype) for r in rows]
            + [pltpu.SemaphoreType.DMA((2, count))],
        ),
        input_output_aliases={count + 1: 0},
        compiler_params=pltpu.CompilerParams(vmem_limit_bytes=8 * 2**20),
        cost_estimate=pl.CostEstimate(flops=3 * 2**27, bytes_accessed=SEG, transcendentals=0),
    )(starts, *rows, out)


def swap(rows, distance):
    size = lax.axis_size("replica")
    return lax.ppermute(rows, "replica", [(i, i ^ distance) for i in range(size)])


def swap_some(out, rows, distance, start, segments):
    def branch(count):
        def run(out, rows):
            if count == 0:
                return out
            return put(out, [(swap(rows[: count * SEG], distance), start)])

        return run

    return lax.switch(segments, [branch(c) for c in range(rows.shape[0] // SEG + 1)], out, rows)


def body(queries, suffix_cache, cache_pool, block_table, prefix_blocks, segment_owner):
    replicas = lax.axis_size("replica")
    me = lax.axis_index("replica").astype(jnp.int32)
    capacity = max(2, 2 * SEGS // replicas)
    base = SEGS // replicas
    owner = segment_owner[:, 0]
    far = list(range(replicas - 1, 0, -1))
    if replicas == 4:
        calls = [[(3, 0, 2)], [(2, 0, 3), (1, 0, 1)], [(2, 3, 4), (3, 2, 4), (1, 1, 4)]]
    else:
        calls = [[(k, 0, base) for k in far]]

    def run(groups, whole=()):
        return attend(
            groups,
            whole,
            capacity,
            me,
            owner,
            block_table[0],
            prefix_blocks,
            queries,
            suffix_cache,
            cache_pool,
        )

    def row_of(k, slot):
        return (me ^ k) * capacity + slot

    theirs = [swap(segment_owner, k) for k in range(1, replicas)]
    sent = []
    for i, call in enumerate(calls):
        if i >= 2:
            owner, sent[i - 2] = lax.optimization_barrier((owner, sent[i - 2]))
        made = run(call)
        owner, made, theirs = lax.optimization_barrier((owner, made, theirs))
        sent.append([(swap(rows, k), row_of(k, a)) for (k, a, _), rows in zip(call, made)])
    for i in range(max(0, len(calls) - 2), len(calls) - 1):
        owner, sent[i] = lax.optimization_barrier((owner, sent[i]))
    over = [(k, base, capacity) for k in far]
    *rest, out = run(over, over)
    distances = jnp.arange(1, replicas, dtype=jnp.int32)
    mine = jnp.sum((owner[None, :] == (me ^ distances)[:, None]).astype(jnp.int32), axis=1)
    given = jnp.sum((jnp.concatenate(theirs, axis=1) == me).astype(jnp.int32), axis=0)
    extra = jnp.clip(jnp.maximum(mine, given) - base, 0, capacity - base)
    early = [piece for part in sent[:-1] for piece in part]
    if early:
        out = put(out, early)
    out = put(out, sent[-1])
    for k, rows in reversed(list(zip(far, rest))):
        out = swap_some(out, rows, k, row_of(k, base), extra[k - 1])
    return out


def solution(mesh):
    in_specs = (
        P(("groups", "replica"), "tensor"),
        P(("groups", "replica"), "tensor"),
        P(("groups", "replica"), "tensor"),
        P(("groups", "replica"), None),
        P(("groups", "replica")),
        P(("groups", "replica"), None),
    )
    out_specs = P(("groups", "replica"), "tensor")
    return jax.shard_map(body, mesh=mesh, in_specs=in_specs, out_specs=out_specs, check_vma=False)
```

```python
import functools

import jax
import jax.numpy as jnp
from jax import lax
from jax.experimental import pallas as pl
from jax.experimental.pallas import tpu as pltpu
from jax.sharding import PartitionSpec as P

HEAD_DIM = 128
BLK = 256
MAXB = 4
SEGS = 16
SEG = 64
SCALE = HEAD_DIM ** (-0.5)
LOWEST = -1e38
HEADS_AT_ONCE = 4


def attend_kernel(
    groups, zeros, capacity, me, owner, table, blocks, queries, suffix, pool, *refs
):
    outs, (cache, q_all, o_all, blank, segs, used, todo, place, sems, out_sems, zero_sems) = (
        refs[:-11],
        refs[-11:],
    )
    suffix_rows = suffix.shape[0]
    heads = queries.shape[1] // HEAD_DIM
    group = heads // (suffix.shape[1] // (2 * HEAD_DIM))
    at_once = min(HEADS_AT_ONCE, group)
    rows = at_once * SEG
    prefix = MAXB * BLK

    copies = [pltpu.make_async_copy(suffix, cache.at[pl.ds(prefix, suffix_rows)], sems.at[SEGS])]
    for b in range(MAXB):
        start = pl.multiple_of(table[b] * BLK, BLK)
        to = pl.multiple_of((b + MAXB - blocks[0]) % MAXB * BLK, BLK)
        copies.append(
            pltpu.make_async_copy(
                pool.at[pl.ds(start, BLK)], cache.at[pl.ds(to, BLK)], sems.at[SEGS + 1 + b]
            )
        )
    for copy in copies:
        copy.start()

    @pl.loop(0, segs.shape[0])
    def _(i):
        segs[i] = jnp.int32(-1)

    @pl.loop(0, used.shape[0])
    def _(i):
        used[i] = jnp.int32(0)

    @pl.loop(0, SEGS)
    def _(i):
        distance = owner[i] ^ me[0]
        slot = used[distance]
        used[distance] = slot + 1
        segs[distance * capacity + slot] = i

    def rows_of(ref, seg):
        return ref.at[pl.ds(pl.multiple_of(seg * SEG, SEG), SEG)]

    def fetch(seg):
        return pltpu.make_async_copy(rows_of(queries, seg), rows_of(q_all, seg), sems.at[seg])

    def hand(out, at, seg):
        return pltpu.make_async_copy(rows_of(o_all, seg), rows_of(out, at), out_sems.at[seg])

    def clear(out, at, i):
        return pltpu.make_async_copy(blank, rows_of(out, at), zero_sems.at[i])

    def at_of(distance, slot):
        return (me[0] ^ distance) * capacity + slot

    blank[...] = jnp.zeros_like(blank)
    firsts, found, slots = [], jnp.int32(0), 0
    for out, (distance, first, count, before) in zip(outs, groups):
        firsts.append(slots)

        def look(j, found):
            seg = segs[distance * capacity + first + j]
            at = at_of(distance, first + j) if before is None else before + j

            @pl.when(seg >= 0)
            def _():
                fetch(seg).start()
                todo[found] = seg
                place[found] = slots + j

            @pl.when(seg < 0)
            def _():
                clear(out, at, slots + j).start()

            return jnp.where(seg >= 0, found + 1, found)

        found = lax.fori_loop(0, count, look, found)
        slots += count
    blanks = slots
    for distance, first, count in zeros:
        for j in range(count):
            clear(outs[-1], at_of(distance, first + j), blanks + j).start()
        blanks += count
    for copy in copies:
        copy.wait()

    def attend_rows(seg, count, i):
        first = i * at_once
        low = pl.multiple_of((MAXB - blocks[0]) * BLK, BLK)
        pair = first // group * (2 * HEAD_DIM)

        def column(h):
            return pl.ds(pl.multiple_of((first + h) * HEAD_DIM, HEAD_DIM), HEAD_DIM)

        def cached(offset):
            lanes = pl.ds(pl.multiple_of(pair + offset, HEAD_DIM), HEAD_DIM)
            return cache[pl.ds(low, count * BLK), lanes]

        here = pl.ds(pl.multiple_of(seg * SEG, SEG), SEG)
        q = jnp.concatenate([q_all[here, column(h)] for h in range(at_once)], axis=0)
        s = lax.dot_general(
            q, cached(0), (((1,), (1,)), ((), ())), preferred_element_type=jnp.float32
        )
        parts = [s[:, c : c + HEAD_DIM] for c in range(0, count * BLK, HEAD_DIM)]
        token = lax.broadcasted_iota(jnp.int32, (rows, HEAD_DIM), 0) % SEG + seg * SEG % BLK
        key = lax.broadcasted_iota(jnp.int32, (rows, HEAD_DIM), 1)
        masked = BLK // HEAD_DIM
        for c in range(masked):
            at = len(parts) - masked + c
            parts[at] = jnp.where(key + c * HEAD_DIM <= token, parts[at], LOWEST)
        top = jnp.max(functools.reduce(jnp.maximum, parts), axis=-1, keepdims=True)
        top = jnp.broadcast_to(top, (rows, HEAD_DIM))
        weights = [jnp.exp((part - top) * SCALE) for part in parts]
        total = jnp.sum(functools.reduce(jnp.add, weights), axis=-1, keepdims=True)
        mixed = jnp.dot(
            jnp.concatenate([w.astype(jnp.bfloat16) for w in weights], axis=1),
            cached(HEAD_DIM),
            preferred_element_type=jnp.float32,
        )
        out = (mixed / total).astype(o_all.dtype)
        for h in range(at_once):
            o_all[here, column(h)] = out[h * SEG : (h + 1) * SEG]

    @pl.loop(0, found)
    def _(t):
        seg = todo[t]
        fetch(seg).wait()
        blocks_seen = blocks[0] + seg * SEG // BLK + 1
        for count in range(2, MAXB + suffix_rows // BLK + 1):

            @pl.when(blocks_seen == count)
            def _():
                @pl.loop(0, heads // at_once)
                def _(i):
                    attend_rows(seg, count, i)

        to = place[t]
        for out, first, (distance, slot, count, before) in zip(outs, firsts, groups):
            j = to - first

            @pl.when((j >= 0) & (j < count))
            def _():
                at = at_of(distance, slot + j) if before is None else before + j
                hand(out, at, seg).start()

    @pl.loop(0, found)
    def _(t):
        hand(outs[0], 0, todo[t]).wait()

    first = 0
    for distance, slot, count, _ in groups:

        @pl.loop(0, count)
        def _(j):
            @pl.when(segs[distance * capacity + slot + j] < 0)
            def _():
                clear(outs[0], 0, first + j).wait()

        first += count
    for i in range(slots, blanks):
        clear(outs[0], 0, i).wait()


def attend(groups, whole, capacity, me, owner, table, blocks, queries, suffix, pool):
    replicas = lax.axis_size("replica")
    width = queries.shape[1]
    suffix_rows, columns = suffix.shape
    held = [(k, a, b - a, 0) for k, a, b in groups]
    sizes = [(b - a) * SEG for _, a, b in groups]
    zeros = []
    if whole:
        held.append((0, 0, capacity, None))
        sizes.append(replicas * capacity * SEG)
        zeros = [(k, a, b - a) for k, a, b in whole]
    slots = sum(g[2] for g in held) + sum(z[2] for z in zeros)
    return pl.pallas_call(
        functools.partial(attend_kernel, held, zeros, capacity),
        out_shape=[jax.ShapeDtypeStruct((size, width), queries.dtype) for size in sizes],
        grid_spec=pltpu.PrefetchScalarGridSpec(
            num_scalar_prefetch=4,
            grid=(),
            in_specs=[pl.BlockSpec(memory_space=pl.ANY)] * 3,
            out_specs=[pl.BlockSpec(memory_space=pl.ANY)] * len(sizes),
            scratch_shapes=[
                pltpu.VMEM((suffix_rows + MAXB * BLK, columns), suffix.dtype),
                pltpu.VMEM(queries.shape, queries.dtype),
                pltpu.VMEM(queries.shape, queries.dtype),
                pltpu.VMEM((SEG, width), queries.dtype),
                pltpu.SMEM((replicas * capacity,), jnp.int32),
                pltpu.SMEM((replicas,), jnp.int32),
                pltpu.SMEM((SEGS,), jnp.int32),
                pltpu.SMEM((SEGS,), jnp.int32),
                pltpu.SemaphoreType.DMA((SEGS + MAXB + 1,)),
                pltpu.SemaphoreType.DMA((SEGS,)),
                pltpu.SemaphoreType.DMA((slots,)),
            ],
        ),
        compiler_params=pltpu.CompilerParams(vmem_limit_bytes=56 * 2**20),
        cost_estimate=pl.CostEstimate(flops=2**36, bytes_accessed=SEG * width, transcendentals=0),
    )(me[None], owner, table, blocks, queries, suffix, pool)


def put_kernel(spans, *refs):
    count = len(spans)
    starts, pieces, out, stages = refs[0], refs[1 : 1 + count], refs[2 + count], refs[3 + count :]
    stages, sems = stages[:-1], stages[-1]
    loads = [
        pltpu.make_async_copy(piece, stage, sems.at[0, i])
        for i, (piece, stage) in enumerate(zip(pieces, stages))
    ]
    stores = []
    for i, (span, stage) in enumerate(zip(spans, stages)):
        at = pl.multiple_of(starts[i] * SEG, SEG)
        stores.append(pltpu.make_async_copy(stage, out.at[pl.ds(at, span)], sems.at[1, i]))
    for load in loads:
        load.start()
    for load, store in zip(loads, stores):
        load.wait()
        store.start()
    for store in stores:
        store.wait()


def put(out, pieces):
    rows = [piece for piece, _ in pieces]
    starts = jnp.stack([start for _, start in pieces])
    count = len(rows)
    return pl.pallas_call(
        functools.partial(put_kernel, [r.shape[0] for r in rows]),
        out_shape=jax.ShapeDtypeStruct(out.shape, out.dtype),
        grid_spec=pltpu.PrefetchScalarGridSpec(
            num_scalar_prefetch=1,
            grid=(),
            in_specs=[pl.BlockSpec(memory_space=pl.ANY)] * (count + 1),
            out_specs=pl.BlockSpec(memory_space=pl.ANY),
            scratch_shapes=[pltpu.VMEM(r.shape, r.dtype) for r in rows]
            + [pltpu.SemaphoreType.DMA((2, count))],
        ),
        input_output_aliases={count + 1: 0},
        compiler_params=pltpu.CompilerParams(vmem_limit_bytes=8 * 2**20),
        cost_estimate=pl.CostEstimate(flops=2**27, bytes_accessed=SEG, transcendentals=0),
    )(starts, *rows, out)


def swap(rows, distance):
    size = lax.axis_size("replica")
    return lax.ppermute(rows, "replica", [(i, i ^ distance) for i in range(size)])


def swap_some(out, rows, distance, start, segments):
    def branch(count):
        def run(out, rows):
            if count == 0:
                return out
            return put(out, [(swap(rows[: count * SEG], distance), start)])

        return run

    return lax.switch(segments, [branch(c) for c in range(rows.shape[0] // SEG + 1)], out, rows)


def body(queries, suffix_cache, cache_pool, block_table, prefix_blocks, segment_owner):
    replicas = lax.axis_size("replica")
    me = lax.axis_index("replica").astype(jnp.int32)
    capacity = max(2, 2 * SEGS // replicas)
    base = SEGS // replicas
    owner = segment_owner[:, 0]
    far = list(range(replicas - 1, 0, -1))
    if replicas == 4:
        calls = [[(3, 0, 2)], [(2, 0, 3), (1, 0, 1)], [(2, 3, 4), (3, 2, 4), (1, 1, 4)]]
    else:
        calls = [[(k, 0, base) for k in far]]

    def run(groups, whole=()):
        return attend(
            groups,
            whole,
            capacity,
            me,
            owner,
            block_table[0],
            prefix_blocks,
            queries,
            suffix_cache,
            cache_pool,
        )

    def row_of(k, slot):
        return (me ^ k) * capacity + slot

    theirs = [swap(segment_owner, k) for k in range(1, replicas)]
    sent = []
    for i, call in enumerate(calls):
        made = run(call)
        if sent:
            made, sent[-1] = lax.optimization_barrier((made, sent[-1]))
        owner, made, theirs = lax.optimization_barrier((owner, made, theirs))
        sent.append([(swap(rows, k), row_of(k, a)) for (k, a, _), rows in zip(call, made)])
    over = [(k, base, capacity) for k in far]
    *rest, out = run(over, over)
    distances = jnp.arange(1, replicas, dtype=jnp.int32)
    mine = jnp.sum((owner[None, :] == (me ^ distances)[:, None]).astype(jnp.int32), axis=1)
    given = jnp.sum((jnp.concatenate(theirs, axis=1) == me).astype(jnp.int32), axis=0)
    extra = jnp.clip(jnp.maximum(mine, given) - base, 0, capacity - base)
    early = [piece for part in sent[:-1] for piece in part]
    if early:
        out = put(out, early)
    out = put(out, sent[-1])
    for k, rows in reversed(list(zip(far, rest))):
        out = swap_some(out, rows, k, row_of(k, base), extra[k - 1])
    return out


def solution(mesh):
    in_specs = (
        P(("groups", "replica"), "tensor"),
        P(("groups", "replica"), "tensor"),
        P(("groups", "replica"), "tensor"),
        P(("groups", "replica"), None),
        P(("groups", "replica")),
        P(("groups", "replica"), None),
    )
    out_specs = P(("groups", "replica"), "tensor")
    return jax.shard_map(body, mesh=mesh, in_specs=in_specs, out_specs=out_specs, check_vma=False)
```

```python
import functools

import jax
import jax.numpy as jnp
from jax import lax
from jax.experimental import pallas as pl
from jax.experimental.pallas import tpu as pltpu
from jax.sharding import PartitionSpec as P

HEAD_DIM = 128
BLK = 256
MAXB = 4
SEGS = 16
SEG = 64
SCALE = HEAD_DIM ** (-0.5)
LOWEST = -1e38
HEADS_AT_ONCE = 4


def attend_kernel(
    groups, zeros, fill, capacity, skip, me, owner, table, blocks, queries, suffix, pool, *refs
):
    outs, (cache, q_all, o_all, blank, segs, used, todo, place, sems, out_sems, zero_sems) = (
        refs[skip:-11],
        refs[-11:],
    )
    suffix_rows = suffix.shape[0]
    heads = queries.shape[1] // HEAD_DIM
    group = heads // (suffix.shape[1] // (2 * HEAD_DIM))
    at_once = min(HEADS_AT_ONCE, group)
    rows = at_once * SEG
    prefix = MAXB * BLK

    copies = [pltpu.make_async_copy(suffix, cache.at[pl.ds(prefix, suffix_rows)], sems.at[SEGS])]
    for b in range(MAXB):
        start = pl.multiple_of(table[b] * BLK, BLK)
        to = pl.multiple_of((b + MAXB - blocks[0]) % MAXB * BLK, BLK)
        copies.append(
            pltpu.make_async_copy(
                pool.at[pl.ds(start, BLK)], cache.at[pl.ds(to, BLK)], sems.at[SEGS + 1 + b]
            )
        )
    for copy in copies:
        copy.start()

    @pl.loop(0, segs.shape[0])
    def _(i):
        segs[i] = jnp.int32(-1)

    @pl.loop(0, used.shape[0])
    def _(i):
        used[i] = jnp.int32(0)

    @pl.loop(0, SEGS)
    def _(i):
        distance = owner[i] ^ me[0]
        slot = used[distance]
        used[distance] = slot + 1
        segs[distance * capacity + slot] = i

    def rows_of(ref, seg):
        return ref.at[pl.ds(pl.multiple_of(seg * SEG, SEG), SEG)]

    def fetch(seg):
        return pltpu.make_async_copy(rows_of(queries, seg), rows_of(q_all, seg), sems.at[seg])

    def hand(out, at, seg):
        return pltpu.make_async_copy(rows_of(o_all, seg), rows_of(out, at), out_sems.at[seg])

    def clear(out, at, i):
        return pltpu.make_async_copy(blank, rows_of(out, at), zero_sems.at[i])

    def at_of(distance, slot):
        return (me[0] ^ distance) * capacity + slot

    blank[...] = jnp.zeros_like(blank)
    firsts, found, slots = [], jnp.int32(0), 0
    for out, (distance, first, count, before) in zip(outs, groups):
        firsts.append(slots)

        def look(j, found):
            seg = segs[distance * capacity + first + j]
            at = at_of(distance, first + j) if before is None else before + j

            @pl.when(seg >= 0)
            def _():
                fetch(seg).start()
                todo[found] = seg
                place[found] = slots + j

            @pl.when(seg < 0)
            def _():
                clear(out, at, slots + j).start()

            return jnp.where(seg >= 0, found + 1, found)

        if before is None:
            earlier, sends, quota = fill

            def room(parts, limit, taken):
                busy = sum((jnp.clip(used[k] - a, 0, b - a) for k, a, b in parts), jnp.int32(0))
                return taken + jnp.clip(limit - busy, 0, used[0] - taken)

            low = jnp.int32(0)
            for parts, limit in earlier:
                low = room(parts, limit, low)
            high = used[0] if quota is None else room(sends, quota, low)
            found = lax.fori_loop(low, high, look, found)
            if quota is None:
                found = lax.fori_loop(used[0], capacity, look, found)
        else:
            found = lax.fori_loop(0, count, look, found)
        slots += count
    blanks = slots
    for distance, first, count in zeros:
        for j in range(count):
            clear(outs[-1], at_of(distance, first + j), blanks + j).start()
        blanks += count
    for copy in copies:
        copy.wait()

    def attend_rows(seg, count, i):
        first = i * at_once
        low = pl.multiple_of((MAXB - blocks[0]) * BLK, BLK)
        pair = first // group * (2 * HEAD_DIM)

        def column(h):
            return pl.ds(pl.multiple_of((first + h) * HEAD_DIM, HEAD_DIM), HEAD_DIM)

        def cached(offset):
            lanes = pl.ds(pl.multiple_of(pair + offset, HEAD_DIM), HEAD_DIM)
            return cache[pl.ds(low, count * BLK), lanes]

        here = pl.ds(pl.multiple_of(seg * SEG, SEG), SEG)
        q = jnp.concatenate([q_all[here, column(h)] for h in range(at_once)], axis=0)
        s = lax.dot_general(
            q, cached(0), (((1,), (1,)), ((), ())), preferred_element_type=jnp.float32
        )
        parts = [s[:, c : c + HEAD_DIM] for c in range(0, count * BLK, HEAD_DIM)]
        token = lax.broadcasted_iota(jnp.int32, (rows, HEAD_DIM), 0) % SEG + seg * SEG % BLK
        key = lax.broadcasted_iota(jnp.int32, (rows, HEAD_DIM), 1)
        masked = BLK // HEAD_DIM
        for c in range(masked):
            at = len(parts) - masked + c
            parts[at] = jnp.where(key + c * HEAD_DIM <= token, parts[at], LOWEST)
        top = jnp.max(functools.reduce(jnp.maximum, parts), axis=-1, keepdims=True)
        top = jnp.broadcast_to(top, (rows, HEAD_DIM))
        weights = [jnp.exp((part - top) * SCALE) for part in parts]
        total = jnp.sum(functools.reduce(jnp.add, weights), axis=-1, keepdims=True)
        mixed = jnp.dot(
            jnp.concatenate([w.astype(jnp.bfloat16) for w in weights], axis=1),
            cached(HEAD_DIM),
            preferred_element_type=jnp.float32,
        )
        out = (mixed / total).astype(o_all.dtype)
        for h in range(at_once):
            o_all[here, column(h)] = out[h * SEG : (h + 1) * SEG]

    @pl.loop(0, found)
    def _(t):
        seg = todo[t]
        fetch(seg).wait()
        blocks_seen = blocks[0] + seg * SEG // BLK + 1
        for count in range(2, MAXB + suffix_rows // BLK + 1):

            @pl.when(blocks_seen == count)
            def _():
                @pl.loop(0, heads // at_once)
                def _(i):
                    attend_rows(seg, count, i)

        to = place[t]
        for out, first, (distance, slot, count, before) in zip(outs, firsts, groups):
            j = to - first

            @pl.when((j >= 0) & (j < count))
            def _():
                at = at_of(distance, slot + j) if before is None else before + j
                hand(out, at, seg).start()

    @pl.loop(0, found)
    def _(t):
        hand(outs[0], 0, todo[t]).wait()

    first = 0
    for distance, slot, count, before in groups:
        whole = before is None and fill[2] is not None

        @pl.loop(0, 0 if whole else count)
        def _(j):
            @pl.when(segs[distance * capacity + slot + j] < 0)
            def _():
                clear(outs[0], 0, first + j).wait()

        first += count
    for i in range(slots, blanks):
        clear(outs[0], 0, i).wait()


def attend(groups, fill, zeros, old, capacity, me, owner, table, blocks, queries, suffix, pool):
    replicas = lax.axis_size("replica")
    width = queries.shape[1]
    suffix_rows, columns = suffix.shape
    held = [(k, a, b - a, 0) for k, a, b in groups]
    sizes = [(b - a) * SEG for _, a, b in groups]
    if fill:
        held.append((0, 0, capacity, None))
        sizes.append(replicas * capacity * SEG)
    zeros = [(k, a, b - a) for k, a, b in zeros]
    slots = sum(g[2] for g in held) + sum(z[2] for z in zeros)
    inputs = [queries, suffix, pool] + ([] if old is None else [old])
    return pl.pallas_call(
        functools.partial(attend_kernel, held, zeros, fill, capacity, len(inputs) - 3),
        out_shape=[jax.ShapeDtypeStruct((size, width), queries.dtype) for size in sizes],
        grid_spec=pltpu.PrefetchScalarGridSpec(
            num_scalar_prefetch=4,
            grid=(),
            in_specs=[pl.BlockSpec(memory_space=pl.ANY)] * len(inputs),
            out_specs=[pl.BlockSpec(memory_space=pl.ANY)] * len(sizes),
            scratch_shapes=[
                pltpu.VMEM((suffix_rows + MAXB * BLK, columns), suffix.dtype),
                pltpu.VMEM(queries.shape, queries.dtype),
                pltpu.VMEM(queries.shape, queries.dtype),
                pltpu.VMEM((SEG, width), queries.dtype),
                pltpu.SMEM((replicas * capacity,), jnp.int32),
                pltpu.SMEM((replicas,), jnp.int32),
                pltpu.SMEM((SEGS,), jnp.int32),
                pltpu.SMEM((SEGS,), jnp.int32),
                pltpu.SemaphoreType.DMA((SEGS + MAXB + 1,)),
                pltpu.SemaphoreType.DMA((SEGS,)),
                pltpu.SemaphoreType.DMA((slots,)),
            ],
        ),
        input_output_aliases={} if old is None else {7: len(sizes) - 1},
        compiler_params=pltpu.CompilerParams(vmem_limit_bytes=56 * 2**20),
        cost_estimate=pl.CostEstimate(flops=2**36, bytes_accessed=SEG * width, transcendentals=0),
    )(me[None], owner, table, blocks, *inputs)


def put_kernel(spans, *refs):
    count = len(spans)
    starts, pieces, out, stages = refs[0], refs[1 : 1 + count], refs[2 + count], refs[3 + count :]
    stages, sems = stages[:-1], stages[-1]
    loads = [
        pltpu.make_async_copy(piece, stage, sems.at[0, i])
        for i, (piece, stage) in enumerate(zip(pieces, stages))
    ]
    stores = []
    for i, (span, stage) in enumerate(zip(spans, stages)):
        at = pl.multiple_of(starts[i] * SEG, SEG)
        stores.append(pltpu.make_async_copy(stage, out.at[pl.ds(at, span)], sems.at[1, i]))
    for load in loads:
        load.start()
    for load, store in zip(loads, stores):
        load.wait()
        store.start()
    for store in stores:
        store.wait()


def put(out, pieces):
    rows = [piece for piece, _ in pieces]
    starts = jnp.stack([start for _, start in pieces])
    count = len(rows)
    return pl.pallas_call(
        functools.partial(put_kernel, [r.shape[0] for r in rows]),
        out_shape=jax.ShapeDtypeStruct(out.shape, out.dtype),
        grid_spec=pltpu.PrefetchScalarGridSpec(
            num_scalar_prefetch=1,
            grid=(),
            in_specs=[pl.BlockSpec(memory_space=pl.ANY)] * (count + 1),
            out_specs=pl.BlockSpec(memory_space=pl.ANY),
            scratch_shapes=[pltpu.VMEM(r.shape, r.dtype) for r in rows]
            + [pltpu.SemaphoreType.DMA((2, count))],
        ),
        input_output_aliases={count + 1: 0},
        compiler_params=pltpu.CompilerParams(vmem_limit_bytes=8 * 2**20),
        cost_estimate=pl.CostEstimate(flops=2**27, bytes_accessed=SEG, transcendentals=0),
    )(starts, *rows, out)


def swap(rows, distance):
    size = lax.axis_size("replica")
    return lax.ppermute(rows, "replica", [(i, i ^ distance) for i in range(size)])


def swap_some(out, rows, distance, start, segments):
    def branch(count):
        def run(out, rows):
            if count == 0:
                return out
            return put(out, [(swap(rows[: count * SEG], distance), start)])

        return run

    return lax.switch(segments, [branch(c) for c in range(rows.shape[0] // SEG + 1)], out, rows)


def body(queries, suffix_cache, cache_pool, block_table, prefix_blocks, segment_owner):
    replicas = lax.axis_size("replica")
    me = lax.axis_index("replica").astype(jnp.int32)
    capacity = max(2, 2 * SEGS // replicas)
    base = SEGS // replicas
    owner = segment_owner[:, 0]
    far = list(range(replicas - 1, 0, -1))
    if replicas == 4:
        calls = [[(3, 0, 2)], [(2, 0, 3), (1, 0, 1)], [(2, 3, 4), (3, 2, 4), (1, 1, 4)]]
    else:
        calls = [[(k, 0, base) for k in far]]

    over = [(k, base, capacity) for k in far]

    def run(groups, fill=None, zeros=(), old=None):
        return attend(
            groups,
            fill,
            zeros,
            old,
            capacity,
            me,
            owner,
            block_table[0],
            prefix_blocks,
            queries,
            suffix_cache,
            cache_pool,
        )

    def row_of(k, slot):
        return (me ^ k) * capacity + slot

    theirs = [swap(segment_owner, k) for k in range(1, replicas)]
    sent, out, quotas = [], None, []
    for i, call in enumerate(calls):
        if i == 0:
            made = run(call)
        else:
            quota = sum(b - a for _, a, b in call)
            zeros = over if out is None else ()
            *made, out = run(call, (list(quotas), call, quota), zeros, out)
            quotas.append((call, quota))
        if sent:
            made, sent[-1] = lax.optimization_barrier((made, sent[-1]))
        owner, made, theirs = lax.optimization_barrier((owner, made, theirs))
        sent.append([(swap(rows, k), row_of(k, a)) for (k, a, _), rows in zip(call, made)])
    *rest, out = run(over, (quotas, over, None), over if out is None else (), out)
    distances = jnp.arange(1, replicas, dtype=jnp.int32)
    mine = jnp.sum((owner[None, :] == (me ^ distances)[:, None]).astype(jnp.int32), axis=1)
    given = jnp.sum((jnp.concatenate(theirs, axis=1) == me).astype(jnp.int32), axis=0)
    extra = jnp.clip(jnp.maximum(mine, given) - base, 0, capacity - base)
    early = [piece for part in sent[:-1] for piece in part]
    if early:
        out = put(out, early)
    out = put(out, sent[-1])
    for k, rows in reversed(list(zip(far, rest))):
        out = swap_some(out, rows, k, row_of(k, base), extra[k - 1])
    return out


def solution(mesh):
    in_specs = (
        P(("groups", "replica"), "tensor"),
        P(("groups", "replica"), "tensor"),
        P(("groups", "replica"), "tensor"),
        P(("groups", "replica"), None),
        P(("groups", "replica")),
        P(("groups", "replica"), None),
    )
    out_specs = P(("groups", "replica"), "tensor")
    return jax.shard_map(body, mesh=mesh, in_specs=in_specs, out_specs=out_specs, check_vma=False)
```
